32 devices in a mesh: grp: 2 (over y), row: 4 (over z), col: 2 (over x), sub: 2 (over core).
Axes of the slice: x: 2, y: 2, z: 4, core: 2. Of those that a mesh axis runs over, the one named last changes fastest.
Arguments:
- samples: bfloat16 [512, 2, 16, 512], P(('grp', 'row', 'col', 'sub')), parts along dimension 0, may hold values from -6 to 6
- analysis_taps: float32 [16, 16], replicated, may hold values from -1 to 1
- synthesis_taps: float32 [16, 16], replicated, may hold values from -1 to 1
- antenna_station: int32 [512], P('grp'), parts along dimension 0, may hold values from 0 to 31, as said below
- station_group: int32 [64, 1], P('grp'), parts along dimension 0, may hold values from 0 to 7
- beam_group: int32 [2048], P('grp'), parts along dimension 0, may hold values from 0 to 7
- beam_weights: bfloat16 [32, 2, 1024, 32], P(('grp', 'row'), None, ('col', 'sub')), parts along dimension 0, may hold values from -6 to 6
Outputs:
- visibilities: float32 [16, 2, 64, 32], P('row', None, ('grp', 'col', 'sub')), parts along dimension 2
- beam_series: float32 [2048, 2, 16, 512], P(('grp', 'col', 'sub', 'row')), parts along dimension 0
The draws below stay inside these ranges and needn't reach their ends.
There are 2 independent parts, one for each index of `grp`. The reference program is written for one: setup_inputs(seed, part) draws one part's arguments, and reference() takes and returns one part's arrays. A program takes and returns all parts, laid end to end along the dimension named above; an argument that names none is the same for every part. Nothing has to cross between parts.
Inputs may be any that keep to these rules, and one draw needn't show every extreme that they name: `antenna_station`: every station is named by exactly 8 antennas.
All inputs are finite; a program needn't handle non-finite values.
Results may differ from the reference program's by a relative error of at most 0.005.
Values may be sent and summed in bfloat16 or wider, within the bound.
No kernel may reach another device: no remote copies, remote signals or barrier semaphores. Data moves between devices by JAX's collectives and lax.ppermute only.
A program may use at most 64 MiB of HBM per device.

```python
import math
import jax
import jax.numpy as jnp
from jax import lax

ANTENNAS = 256
ANTENNAS_PER_STN = 8
STATIONS = 32
CHAN = 16
TAPS = 16
SPEC = 512
BEAMS = 1024
GROUPS = 8


def draw_antenna_station(key, part):
    sort_order = jax.random.permutation(key, ANTENNAS)
    return (sort_order // ANTENNAS_PER_STN).astype(jnp.int32)


def plant(values, stream_key, low, largest):
    extent = values.shape
    spot = [jax.random.randint(jax.random.fold_in(stream_key, axis), (), 0, extent[axis]) for axis in range(len(extent))]
    values = values.at[tuple(spot)].set(low)
    longest = extent.index(max(extent))
    spot[longest] = (spot[longest] + 1) % extent[longest]
    return values.at[tuple(spot)].set(largest)


def levels(stream_key, shape, cuts, low, top_value):
    level, own = 1.0, jax.random.fold_in(stream_key, 6)
    for position, blocks in cuts:
        draws = jnp.exp(jax.random.uniform(jax.random.fold_in(own, position), (blocks,), jnp.float32, low / len(cuts), top_value / len(cuts)))
        level = level * jnp.repeat(draws, shape[position] // blocks).reshape([-1 if axis == position else 1 for axis in range(len(shape))])
    return level


def choose_distinct(key, rows, count, top, lift):
    sequence = jax.random.permutation(jax.random.fold_in(key, 1), count)
    favour = sequence
    for power in range(3):
        favour = favour * favour // count
    favour = favour * lift // count
    lots = jax.random.randint(jax.random.fold_in(key, 2), (rows, count), 0, 4096) + favour
    fixed_rows = jax.random.permutation(jax.random.fold_in(key, 3), rows)[jnp.arange(count) % rows]
    lots = jnp.where(jnp.arange(rows)[:, None] == fixed_rows[None, :], 1 << 14, lots)
    priority = lots * count + jnp.arange(count)
    return lax.top_k(priority.astype(jnp.int32), top)[1].astype(jnp.int32)


def normal_values(own_key, dims, width, limit, pieces=(), dtype=jnp.bfloat16):
    array = jax.random.normal(own_key, dims, jnp.float32) * width
    if len(pieces) > 0:
        array = levels(own_key, dims, pieces, -0.22, 0.18) * array
    return jnp.clip(array, min=-limit, max=limit).astype(dtype)


def setup_inputs(seed: int = 0, part: int = 0) -> dict:
    splits = jax.random.split(jax.random.key(seed), 8)
    part_splits = jax.random.split(jax.random.fold_in(splits[7], part), 8)
    return {
        "samples": normal_values(part_splits[0], (ANTENNAS, 2, CHAN, SPEC), 1.0, 6.0, ((0, 16),)),
        "analysis_taps": normal_values(splits[1], (TAPS, CHAN), 0.25, 1.0, (), jnp.float32),
        "synthesis_taps": normal_values(splits[2], (TAPS, CHAN), 0.25, 1.0, (), jnp.float32),
        "antenna_station": draw_antenna_station(jax.random.fold_in(jax.random.fold_in(splits[7], part), 71), part),
        "station_group": choose_distinct(part_splits[4], STATIONS, GROUPS, 1, 2048),
        "beam_group": plant(jax.random.randint(part_splits[5], (BEAMS,), 0, GROUPS), jax.random.fold_in(part_splits[5], 1), 0, GROUPS - 1).astype(jnp.int32),
        "beam_weights": normal_values(part_splits[6], (CHAN, 2, BEAMS, STATIONS), 1.0, 6.0, ((0, 4), (2, 4))),
    }


def polyphase(signal, coefficients):
    length = signal.shape[-1]
    output = coefficients[0][:, None] * signal
    for tap_index in range(1, coefficients.shape[0]):
        shifted = jnp.pad(signal[..., :length - tap_index], [(0, 0)] * (signal.ndim - 1) + [(tap_index, 0)])
        output = output + coefficients[tap_index][:, None] * shifted
    return output

def fourier_table(length, direction):
    indices = jnp.arange(length)
    angles = 2.0 * math.pi / length * (indices[:, None] * indices[None, :] % length).astype(jnp.float32)
    cosine_part = jnp.cos(angles)
    sine_part = jnp.sin(angles)
    table = jnp.stack([jnp.stack([cosine_part, direction * sine_part]), jnp.stack([-direction * sine_part, cosine_part])])
    return table.transpose(0, 2, 1, 3) * (1.0 / math.sqrt(length))

def reference(samples, analysis_taps, synthesis_taps, antenna_station, station_group, beam_group, beam_weights):
    filtered = polyphase(samples.astype(jnp.float32), analysis_taps)
    spectra = jnp.einsum('aqcf,qcpk->apkf', filtered, fourier_table(CHAN, -1.0), precision=lax.Precision.HIGHEST).astype(jnp.bfloat16)
    summed_values = jax.ops.segment_sum(spectra.astype(jnp.float32), antenna_station, num_segments=STATIONS)
    station_list = (summed_values * (1.0 / math.sqrt(ANTENNAS_PER_STN))).astype(jnp.bfloat16)
    real_part = station_list[:, 0].astype(jnp.float32)
    imag_part = station_list[:, 1].astype(jnp.float32)
    high = lax.Precision.HIGHEST
    vis_real = (jnp.einsum('icf,jcf->cij', real_part, real_part, precision=high) + jnp.einsum('icf,jcf->cij', imag_part, imag_part, precision=high)) * (1.0 / SPEC)
    vis_imag = (jnp.einsum('icf,jcf->cij', imag_part, real_part, precision=high) - jnp.einsum('icf,jcf->cij', real_part, imag_part, precision=high)) * (1.0 / SPEC)
    visibilities = jnp.stack([vis_real, vis_imag], axis=1)
    members = station_group[:, 0][None, :] == beam_group[:, None]
    scaling = 1.0 / jnp.sqrt(lax.optimization_barrier(jnp.sum(members.astype(jnp.float32), axis=1)))
    weights = jnp.where(members[None, None], beam_weights, jnp.zeros((), jnp.bfloat16)).astype(jnp.float32)
    weight_real = weights[:, 0]
    imaginary_weight = weights[:, 1]
    beam_real = jnp.einsum('cbs,scf->bcf', weight_real, real_part, precision=high) - jnp.einsum('cbs,scf->bcf', imaginary_weight, imag_part, precision=high)
    beam_imag = jnp.einsum('cbs,scf->bcf', weight_real, imag_part, precision=high) + jnp.einsum('cbs,scf->bcf', imaginary_weight, real_part, precision=high)
    beams = (jnp.stack([beam_real, beam_imag], axis=1) * scaling[:, None, None, None]).astype(jnp.bfloat16)
    inverse = jnp.einsum('bqkf,qkpc->bpcf', beams.astype(jnp.float32), fourier_table(CHAN, 1.0), precision=high)
    beam_series = polyphase(inverse, synthesis_taps)
    return (visibilities, beam_series)
```

```python
import functools
import math

import jax
import jax.numpy as jnp
from jax import lax
from jax.experimental import pallas as pl
from jax.experimental.pallas import tpu as pltpu
from jax.sharding import PartitionSpec as P

ANTENNAS_PER_STN = 8
SPEC = 512
VMEM_LIMIT = 48 * 1024 * 1024
HALO = 128


def fourier(parts, sign):
    count = len(parts)
    if count == 1:
        return parts
    even, odd = fourier(parts[0::2], sign), fourier(parts[1::2], sign)
    low, top = [], []
    for k in range(count // 2):
        er, ei = even[k]
        re, im = odd[k]
        if k == 0:
            tr, ti = re, im
        elif 4 * k == count:
            tr, ti = (-sign * im, sign * re)
        else:
            c, s = math.cos(2 * math.pi * k / count), sign * math.sin(2 * math.pi * k / count)
            tr, ti = re * c - im * s, re * s + im * c
        low.append((er + tr, ei + ti))
        top.append((er - tr, ei - ti))
    return low + top


def station_kernel(lane_axes, names_ref, taps_ref, x_ref, out_ref):
    lane = lax.axis_index(lane_axes)
    stations, antennas = out_ref.shape[0] // 2, names_ref.shape[1]
    wanted = lax.broadcasted_iota(jnp.int32, (stations, antennas), 0)
    chosen = jnp.where(names_ref[...] == wanted, 1.0, 0.0).astype(jnp.bfloat16)
    frames = x_ref.shape[-1]
    place = lax.broadcasted_iota(jnp.int32, (stations, frames), 1)
    for part in range(2):
        rows = x_ref[:, part].reshape(antennas, frames)
        total = jnp.dot(chosen, rows, preferred_element_type=jnp.float32)
        result = total * taps_ref[0, lane]
        for tap in range(1, taps_ref.shape[0]):
            moved = jnp.where(place >= tap, pltpu.roll(total, tap, 1), 0.0)
            result = result + moved * taps_ref[tap, lane]
        out_ref[part * stations : (part + 1) * stations] = result.astype(out_ref.dtype)


def weight_kernel(groups_ref, beam_ref, w_ref, m_ref):
    chan, _, beams, stations = w_ref.shape
    members = groups_ref[...] == beam_ref[...]
    count = jnp.sum(members.astype(jnp.float32), axis=1, keepdims=True)
    scale = (1.0 / (chan * math.sqrt(ANTENNAS_PER_STN))) / jnp.sqrt(count)
    zero = jnp.zeros((), jnp.float32)
    parts = [
        tuple(jnp.where(members, w_ref[k, q].astype(jnp.float32), zero) for q in range(2))
        for k in range(chan)
    ]
    parts = fourier(parts, -1.0)
    real = [p[0] * scale for p in parts]
    imag = [p[1] * scale for p in parts]
    upper = jnp.concatenate([v for k in range(chan) for v in (real[k], -imag[k])], axis=1)
    lower = jnp.concatenate([v for k in range(chan) for v in (imag[k], real[k])], axis=1)
    whole = jnp.concatenate([upper, lower], axis=0).astype(m_ref.dtype)
    width = whole.shape[1] // 4
    for u in range(4):
        for j in range(4):
            t = (u + j) % 4
            m_ref[u, :, t * width : (t + 1) * width] = whole[:, j * width : (j + 1) * width]


def toeplitz_kernel(taps_ref, t_ref):
    taps, chan = taps_ref.shape
    rows, cols = t_ref.shape[1] // 2, t_ref.shape[2]
    wide = 2 * cols
    lanes = lax.broadcasted_iota(jnp.int32, (8, wide), 1)
    for c in range(chan):
        base = jnp.zeros((8, wide), jnp.float32)
        for tap in range(taps):
            base = jnp.where(lanes == (tap - HALO) % wide, taps_ref[tap, c], base)
        whole = jnp.broadcast_to(base[0:1], (rows, wide))
        whole = pltpu.roll(whole, 0, 1, stride=1, stride_axis=0)[:, :cols]
        high = whole.astype(jnp.bfloat16)
        t_ref[c, :rows] = high
        t_ref[c, rows:] = (whole - high.astype(jnp.float32)).astype(jnp.bfloat16)


def beam_kernel(
    axes,
    x_refs,
    m_hbm,
    t_hbm,
    series_ref,
    vis_ref,
    lanes_ref,
    cross_ref,
    m_ref,
    t_ref,
    tail_ref,
    out_ref,
    load_sems,
    store_sems,
):
    row, col, sub = (lax.axis_index(a) for a in axes)
    loads = [
        pltpu.make_async_copy(m_hbm, m_ref, load_sems.at[0]),
        pltpu.make_async_copy(t_hbm, t_ref, load_sems.at[1]),
    ]
    for copy in loads:
        copy.start()
    rows = x_refs[0].shape[1]
    stations = rows // 2
    chan = 4 * 4
    frames = lanes_ref.shape[1]

    for place, ref in enumerate(x_refs):
        for m in range(4):
            lane = (row ^ m) * 4 + (col ^ (place & 1)) * 2 + (sub ^ (place >> 1))
            lanes_ref[pl.ds(pl.multiple_of(lane * rows, rows), rows)] = ref[m]
    wrap = 3 * rows
    lanes_ref[chan * rows : chan * rows + wrap] = lanes_ref[0:wrap]
    inner = []
    for b in range(4):
        parts = []
        for a in range(4):
            start = (4 * a + b) * rows
            parts.append(
                tuple(
                    lanes_ref[start + q * stations : start + (q + 1) * stations].astype(
                        jnp.float32
                    )
                    for q in range(2)
                )
            )
        inner.append(fourier(parts, -1.0))
    scale = 1.0 / math.sqrt(chan * ANTENNAS_PER_STN)
    block = (col * 2 + sub) * vis_ref.shape[2]
    own = vis_ref.shape[2]
    for j in range(4):
        re, im = inner[0][j]
        for b in range(1, 4):
            cosine = jnp.float32(0.0)
            sine = jnp.float32(0.0)
            for r in range(4):
                angle = -2.0 * math.pi * b * (4 * r + j) / chan
                cosine = jnp.where(row == r, math.cos(angle), cosine)
                sine = jnp.where(row == r, math.sin(angle), sine)
            yr, yi = inner[b][j]
            re = re + (yr * cosine - yi * sine)
            im = im + (yr * sine + yi * cosine)
        both = (jnp.concatenate([re, im], axis=0) * scale).astype(jnp.bfloat16)
        cross_ref[...] = lax.dot_general(
            both, both, (((1,), (1,)), ((), ())), preferred_element_type=jnp.float32
        )
        own_real = cross_ref[pl.ds(pl.multiple_of(block, own), own)]
        own_imag = cross_ref[pl.ds(pl.multiple_of(stations + block, own), own)]
        vis_ref[j, 0] = (own_real[:, :stations] + own_imag[:, stations:]) * (1.0 / SPEC)
        vis_ref[j, 1] = (own_imag[:, :stations] - own_real[:, stations:]) * (1.0 / SPEC)
    for copy in loads:
        copy.wait()
    beams = m_ref.shape[1] // 2
    tile = t_ref.shape[2]
    stores = []
    for n in range(frames // tile):
        for half in range(2):
            slots = [(2 * n + half) * 2 + part for part in range(2)]
            for v in range(4):
                window = lanes_ref[v * rows : (v + chan) * rows, n * tile : (n + 1) * tile]
                pair = m_ref[2 * half : 2 * half + 2].reshape(4 * beams, chan * rows)
                found = jnp.dot(pair, window, preferred_element_type=jnp.float32)
                found = found.astype(jnp.bfloat16)
                for w in range(2):
                    c = 4 * w + v
                    lane = 8 * half + c
                    inverse = found[2 * beams * w : 2 * beams * (w + 1)]
                    if n == 0:
                        value = jnp.dot(
                            inverse, t_ref[lane, HALO : HALO + tile], preferred_element_type=jnp.float32
                        ) + jnp.dot(
                            inverse, t_ref[lane, 2 * HALO + tile :], preferred_element_type=jnp.float32
                        )
                    else:
                        taken = jnp.concatenate([tail_ref[lane], inverse] * 2, axis=1)
                        value = jnp.dot(taken, t_ref[lane], preferred_element_type=jnp.float32)
                    if n + 1 < frames // tile:
                        tail_ref[lane] = inverse[:, tile - HALO :]
                    for part in range(2):
                        for q in range(2):
                            out_ref.at[slots[part]][pl.ds(q * 8 + c, beams, stride=16), :] = value[
                                q * beams : (q + 1) * beams, part * 128 : (part + 1) * 128
                            ]
            for part in range(2):
                first = n * tile + part * 128
                stores.append(
                    pltpu.make_async_copy(
                        out_ref.at[slots[part]].reshape(2 * beams, 8, 128),
                        series_ref.at[:, half, :, first : first + 128],
                        store_sems.at[slots[part]],
                    )
                )
                stores[-1].start()
    for copy in stores:
        copy.wait()


def swap(x, axis, mask):
    size = lax.axis_size(axis)
    return lax.ppermute(x, axis, [(i, i ^ mask) for i in range(size)])


def fast_body(
    samples, analysis_taps, synthesis_taps, antenna_station, station_group, beam_group, beam_weights
):
    axes = ("row", "col", "sub")
    params = pltpu.CompilerParams(vmem_limit_bytes=VMEM_LIMIT)
    vmem = pl.BlockSpec(memory_space=pltpu.VMEM)
    smem = pl.BlockSpec(memory_space=pltpu.SMEM)
    local, _, chan, frames = samples.shape
    stations = station_group.shape[0]
    antennas = antenna_station.shape[0]

    given = lax.all_to_all(beam_weights, "row", split_axis=2, concat_axis=0, tiled=True)
    beams = given.shape[2]
    own = (lax.axis_index(("col", "sub", "row"))) * beams
    own_groups = lax.dynamic_slice_in_dim(beam_group, own, beams, 0).reshape(beams, 1)

    turned = samples.transpose(2, 1, 0, 3)
    lane = lax.all_to_all(turned, axes, split_axis=0, concat_axis=0, tiled=True)
    filtered = pl.pallas_call(
        functools.partial(station_kernel, axes),
        out_shape=jax.ShapeDtypeStruct((2 * stations, frames), jnp.bfloat16),
        in_specs=[vmem, smem, vmem],
        out_specs=vmem,
        compiler_params=params,
        name="station_sums",
    )(antenna_station.reshape(1, antennas), analysis_taps, lane)

    matrix = pl.pallas_call(
        weight_kernel,
        out_shape=jax.ShapeDtypeStruct((4, 2 * beams, 2 * chan * stations), jnp.bfloat16),
        in_specs=[vmem, vmem, vmem],
        out_specs=vmem,
        compiler_params=params,
        name="weight_matrix",
    )(station_group.reshape(1, stations), own_groups, given)
    tile = 256
    bands = pl.pallas_call(
        toeplitz_kernel,
        out_shape=jax.ShapeDtypeStruct((chan, 2 * (tile + HALO), tile), jnp.bfloat16),
        in_specs=[smem],
        out_specs=vmem,
        compiler_params=params,
        name="synthesis_bands",
    )(synthesis_taps)

    held = jnp.stack([filtered] + [swap(filtered, "row", m) for m in (1, 2, 3)])
    other = swap(held, "col", 1)
    pieces = [held, other, swap(held, "sub", 1), swap(other, "sub", 1)]

    anywhere = pl.BlockSpec(memory_space=pl.ANY)
    slots = frames // 128 * 2
    series, visibilities = pl.pallas_call(
        lambda a, b, c, d, *rest: beam_kernel(axes, (a, b, c, d), *rest),
        out_shape=(
            jax.ShapeDtypeStruct((2 * beams, 2, 8, frames), jnp.float32),
            jax.ShapeDtypeStruct((4, 2, stations // 4, stations), jnp.float32),
        ),
        in_specs=[vmem, vmem, vmem, vmem, anywhere, anywhere],
        out_specs=(anywhere, vmem),
        scratch_shapes=[
            pltpu.VMEM(((chan + 3) * 2 * stations, frames), jnp.bfloat16),
            pltpu.VMEM((2 * stations, 2 * stations), jnp.float32),
            pltpu.VMEM(matrix.shape, matrix.dtype),
            pltpu.VMEM(bands.shape, bands.dtype),
            pltpu.VMEM((chan, 2 * beams, HALO), jnp.bfloat16),
            pltpu.VMEM((slots, 2 * beams * 8, 128), jnp.float32),
            pltpu.SemaphoreType.DMA((2,)),
            pltpu.SemaphoreType.DMA((slots,)),
        ],
        compiler_params=params,
        name="beams_and_series",
    )(*pieces, matrix, bands)
    return visibilities, series.reshape(beams, 2, chan, frames)


def polyphase(signal, coefficients):
    length = signal.shape[-1]
    output = coefficients[0][:, None] * signal
    for tap_index in range(1, coefficients.shape[0]):
        shifted = jnp.pad(
            signal[..., : length - tap_index], [(0, 0)] * (signal.ndim - 1) + [(tap_index, 0)]
        )
        output = output + coefficients[tap_index][:, None] * shifted
    return output


def fourier_table(length, direction):
    indices = jnp.arange(length)
    angles = (
        2.0 * math.pi / length * (indices[:, None] * indices[None, :] % length).astype(jnp.float32)
    )
    cosine_part = jnp.cos(angles)
    sine_part = jnp.sin(angles)
    table = jnp.stack(
        [
            jnp.stack([cosine_part, direction * sine_part]),
            jnp.stack([-direction * sine_part, cosine_part]),
        ]
    )
    return table.transpose(0, 2, 1, 3) * (1.0 / math.sqrt(length))


def general_body(
    samples, analysis_taps, synthesis_taps, antenna_station, station_group, beam_group, beam_weights
):
    high = lax.Precision.HIGHEST
    block_count = lax.axis_size(("col", "sub"))
    block_index = lax.axis_index(("col", "sub"))
    filtered = polyphase(samples.astype(jnp.float32), analysis_taps)
    spectra = jnp.einsum(
        "aqcf,qcpk->apkf", filtered, fourier_table(samples.shape[2], -1.0), precision=high
    ).astype(jnp.bfloat16)
    turned = lax.all_to_all(spectra, "row", split_axis=2, concat_axis=0, tiled=True)
    local_count = spectra.shape[0]
    held_rows = turned.shape[0]
    chan_rows = turned.shape[2]
    spec_len = turned.shape[3]
    station_count = station_group.shape[0]
    flat_width = 2 * chan_rows * spec_len
    tile_rows = station_count // block_count
    shard_rows = lax.all_gather(turned, ("col", "sub"), axis=0, tiled=True)
    row_total = shard_rows.shape[0]
    positions = jnp.arange(row_total, dtype=jnp.int32)
    source_block = positions // held_rows
    offset_rows = positions % held_rows
    source_row = offset_rows // local_count
    antenna = offset_rows % local_count
    global_index = (source_row * block_count + source_block) * local_count + antenna
    targets = antenna_station[global_index]
    wanted = jnp.arange(station_count, dtype=jnp.int32)
    one_hot = (targets[None, :] == wanted[:, None]).astype(jnp.bfloat16)
    summed_values = jnp.dot(
        one_hot, shard_rows.reshape(row_total, flat_width), preferred_element_type=jnp.float32
    )
    flat_stations = (summed_values * (1.0 / math.sqrt(ANTENNAS_PER_STN))).astype(jnp.bfloat16)
    station_list = flat_stations.reshape(station_count, 2, chan_rows, spec_len)
    real_part = station_list[:, 0]
    imag_part = station_list[:, 1]
    own_rows = lax.dynamic_slice_in_dim(station_list, block_index * tile_rows, tile_rows, 0)
    own_real = own_rows[:, 0]
    own_imag = own_rows[:, 1]
    vis_real = (
        jnp.einsum("icf,jcf->cij", own_real, real_part, preferred_element_type=jnp.float32)
        + jnp.einsum("icf,jcf->cij", own_imag, imag_part, preferred_element_type=jnp.float32)
    ) * (1.0 / SPEC)
    vis_imag = (
        jnp.einsum("icf,jcf->cij", own_imag, real_part, preferred_element_type=jnp.float32)
        - jnp.einsum("icf,jcf->cij", own_real, imag_part, preferred_element_type=jnp.float32)
    ) * (1.0 / SPEC)
    visibilities = jnp.stack([vis_real, vis_imag], axis=1)
    beam_block = beam_weights.shape[2]
    own_groups = lax.dynamic_slice_in_dim(beam_group, block_index * beam_block, beam_block, 0)
    members = station_group[:, 0][None, :] == own_groups[:, None]
    scaling = 1.0 / jnp.sqrt(jnp.sum(members.astype(jnp.float32), axis=1))
    weights = jnp.where(members[None, None], beam_weights, jnp.zeros((), jnp.bfloat16))
    weight_real = weights[:, 0]
    imaginary_weight = weights[:, 1]
    beam_real = jnp.einsum(
        "cbs,scf->bcf", weight_real, real_part, preferred_element_type=jnp.float32
    ) - jnp.einsum("cbs,scf->bcf", imaginary_weight, imag_part, preferred_element_type=jnp.float32)
    beam_imag = jnp.einsum(
        "cbs,scf->bcf", weight_real, imag_part, preferred_element_type=jnp.float32
    ) + jnp.einsum("cbs,scf->bcf", imaginary_weight, real_part, preferred_element_type=jnp.float32)
    beams = (jnp.stack([beam_real, beam_imag], axis=1) * scaling[:, None, None, None]).astype(
        jnp.bfloat16
    )
    returned = lax.all_to_all(beams, "row", split_axis=0, concat_axis=2, tiled=True)
    inverse = jnp.einsum(
        "bqkf,qkpc->bpcf",
        returned.astype(jnp.float32),
        fourier_table(returned.shape[2], 1.0),
        precision=high,
    )
    beam_series = polyphase(inverse, synthesis_taps)
    return (visibilities, beam_series)


def solution(mesh):
    sizes = dict(mesh.shape)

    def body(samples, *others):
        chan = samples.shape[2]
        fits = (sizes["row"], sizes["col"], sizes["sub"], chan) == (4, 2, 2, 16)
        return (fast_body if fits else general_body)(samples, *others)

    return jax.shard_map(
        body,
        mesh=mesh,
        in_specs=(
            P(("grp", "row", "col", "sub"), None, None, None),
            P(),
            P(),
            P("grp"),
            P("grp", None),
            P("grp"),
            P(("grp", "row"), None, ("col", "sub"), None),
        ),
        out_specs=(
            P("row", None, ("grp", "col", "sub"), None),
            P(("grp", "col", "sub", "row"), None, None, None),
        ),
        check_vma=False,
    )
```

```python
import functools
import math

import jax
import jax.numpy as jnp
from jax import lax
from jax.experimental import pallas as pl
from jax.experimental.pallas import tpu as pltpu
from jax.sharding import PartitionSpec as P

ANTENNAS_PER_STN = 8
SPEC = 512
VMEM_LIMIT = 32 * 1024 * 1024
HALO = 128


def fourier(parts, sign):
    count = len(parts)
    if count == 1:
        return parts
    even, odd = fourier(parts[0::2], sign), fourier(parts[1::2], sign)
    low, top = [], []
    for k in range(count // 2):
        er, ei = even[k]
        re, im = odd[k]
        if k == 0:
            tr, ti = re, im
        elif 4 * k == count:
            tr, ti = (-sign * im, sign * re)
        else:
            c, s = math.cos(2 * math.pi * k / count), sign * math.sin(2 * math.pi * k / count)
            tr, ti = re * c - im * s, re * s + im * c
        low.append((er + tr, ei + ti))
        top.append((er - tr, ei - ti))
    return low + top


def lane_of(row, col, sub):
    return sub * 8 + col * 4 + row


def spread_kernel(axes, x_ref, *out_refs):
    row, col, sub = (lax.axis_index(a) for a in axes)
    antennas, parts, chan, frames = x_ref.shape
    count = antennas * parts * chan
    shape = (count, count)
    place = lax.broadcasted_iota(jnp.int32, (count, 1), 0)
    antenna = place % antennas
    part = place // antennas % parts
    piece = place // (antennas * parts)
    lane = lane_of(row ^ (piece % 4), col ^ (piece // 4 % 2), sub ^ (piece // 8))
    source = (antenna * parts + part) * chan + lane
    order = jnp.where(lax.broadcasted_iota(jnp.int32, shape, 1) == source, 1.0, 0.0)
    moved = jnp.dot(
        order.astype(jnp.bfloat16),
        x_ref[...].reshape(count, frames),
        preferred_element_type=jnp.float32,
    ).astype(jnp.bfloat16)
    size = count // len(out_refs)
    for k, ref in enumerate(out_refs):
        ref[...] = moved[k * size : (k + 1) * size].reshape(ref.shape)


def sum_kernel(members_ref, *refs):
    x_refs, out_refs = refs[:4], refs[4:]
    for m, ref in enumerate(out_refs):
        rows = jnp.concatenate([x[m] for x in x_refs], axis=0)
        ref[...] = jnp.dot(
            members_ref[...], rows, preferred_element_type=jnp.float32
        ).astype(ref.dtype)


def filter_kernel(taps_ref, *refs):
    x_refs, out_ref = refs[:-1], refs[-1]
    total = x_refs[0][...].astype(jnp.float32)
    for ref in x_refs[1:]:
        total = total + ref[...].astype(jnp.float32)
    place = lax.broadcasted_iota(jnp.int32, total.shape, 1)
    result = total * taps_ref[0:1]
    for tap in range(1, taps_ref.shape[0]):
        moved = jnp.where(place >= tap, pltpu.roll(total, tap, 1), 0.0)
        result = result + moved * taps_ref[tap : tap + 1]
    out_ref[...] = result.astype(out_ref.dtype)


def pack_kernel(axes, w_ref, names_ref, taps_ref, members_ref, own_taps_ref, *out_refs):
    row, col, sub = (lax.axis_index(a) for a in axes)
    names = []
    for k in range(4):
        owner = (row * 2 + (col ^ (k // 2))) * 2 + (sub ^ (k % 2))
        names += [names_ref[pl.ds(owner, 1)]] * 2
    names = jnp.concatenate(names, axis=1)
    local = names_ref.shape[1]
    place = lax.broadcasted_iota(jnp.int32, members_ref.shape, 0)
    column = lax.broadcasted_iota(jnp.int32, members_ref.shape, 1)
    wanted = members_ref.shape[0] // 2
    same = (place % wanted == names) & (place // wanted == column // local % 2)
    members_ref[...] = jnp.where(same, 1.0, 0.0).astype(members_ref.dtype)
    taps = taps_ref[...]
    mine = lax.broadcasted_iota(jnp.int32, taps.shape, 1) == lane_of(row, col, sub)
    own = jnp.sum(jnp.where(mine, taps, 0.0), axis=1, keepdims=True)
    own_taps_ref[...] = jnp.broadcast_to(own, own_taps_ref.shape)
    chan, _, _, stations = w_ref.shape
    beams = out_refs[0].shape[0]
    for mask, ref in enumerate(out_refs):
        first = pl.multiple_of((row ^ mask) * beams, beams)
        for k in range(chan):
            for q in range(2):
                place = (2 * k + q) * stations
                ref[:, place : place + stations] = w_ref[k, q, pl.ds(first, beams)]


def weight_kernel(axes, groups_ref, beam_ref, *refs):
    row = lax.axis_index(axes[0])
    w_refs, m_ref, all_ref = refs[:4], refs[4], refs[5]
    stations = groups_ref.shape[1]
    held = w_refs[0].shape[1] // (2 * stations)
    chan = 4 * held
    for mask, ref in enumerate(w_refs):
        all_ref[row ^ mask] = ref[...]
    members = groups_ref[...] == beam_ref[...]
    count = jnp.sum(members.astype(jnp.float32), axis=1, keepdims=True)
    scale = (1.0 / (chan * math.sqrt(ANTENNAS_PER_STN))) / jnp.sqrt(count)
    zero = jnp.zeros((), jnp.float32)
    parts = []
    for k in range(chan):
        whole = all_ref[k // held].astype(jnp.float32)
        places = [(2 * (k % held) + q) * stations for q in range(2)]
        parts.append(
            tuple(jnp.where(members, whole[:, p : p + stations], zero) for p in places)
        )
    parts = fourier(parts, -1.0)
    real = [p[0] * scale for p in parts]
    imag = [p[1] * scale for p in parts]
    upper = jnp.concatenate([v for k in range(chan) for v in (real[k], -imag[k])], axis=1)
    lower = jnp.concatenate([v for k in range(chan) for v in (imag[k], real[k])], axis=1)
    whole = jnp.concatenate([upper, lower], axis=0).astype(m_ref.dtype)
    width = whole.shape[1] // 4
    for u in range(4):
        for j in range(4):
            t = (u + j) % 4
            m_ref[u, :, t * width : (t + 1) * width] = whole[:, j * width : (j + 1) * width]


def bands(taps_ref, lane, rows, cols):
    wide = 2 * cols
    places = lax.broadcasted_iota(jnp.int32, (8, wide), 1)
    base = jnp.zeros((8, wide), jnp.float32)
    for tap in range(taps_ref.shape[0]):
        base = jnp.where(places == (tap - HALO) % wide, taps_ref[tap, lane], base)
    whole = jnp.broadcast_to(base[0:1], (rows, wide))
    whole = pltpu.roll(whole, 0, 1, stride=1, stride_axis=0)[:, :cols]
    high = whole.astype(jnp.bfloat16)
    low = (whole - high.astype(jnp.float32)).astype(jnp.bfloat16)
    return jnp.concatenate([high[:HALO], low[:HALO], high[HALO:], low[HALO:]], axis=0)


def beam_kernel(
    axes,
    x_refs,
    m_ref,
    taps_ref,
    series_ref,
    vis_ref,
    lanes_ref,
    cross_ref,
    t_ref,
    inverse_ref,
    out_ref,
    store_sems,
):
    row, col, sub = (lax.axis_index(a) for a in axes)
    rows = x_refs[0].shape[1]
    stations = rows // 2
    chan = 4 * 4
    frames = lanes_ref.shape[1]

    for place, ref in enumerate(x_refs):
        for m in range(4):
            lane = lane_of(row ^ m, col ^ (place & 1), sub ^ (place >> 1))
            lanes_ref[pl.ds(pl.multiple_of(lane * rows, rows), rows)] = ref[m]
    wrap = 3 * rows
    lanes_ref[chan * rows : chan * rows + wrap] = lanes_ref[0:wrap]
    beams = m_ref.shape[1] // 2
    tile = t_ref.shape[2]
    stores = []
    for half in range(2):
        for c in range(8):
            t_ref[8 * half + c] = bands(taps_ref, 8 * half + c, HALO + tile, tile)
        some = m_ref[2 * half : 2 * half + 2].reshape(4 * beams, chan * rows)
        for v in range(4):
            window = lanes_ref[v * rows : (v + chan) * rows]
            found = jnp.dot(some, window, preferred_element_type=jnp.float32)
            found = found.astype(jnp.bfloat16)
            for u in range(2):
                inverse_ref[8 * half + 4 * u + v] = found[2 * beams * u : 2 * beams * (u + 1)]
        for n in range(frames // tile):
            for c in range(8):
                lane = 8 * half + c
                taken = [inverse_ref[lane, :, n * tile : (n + 1) * tile]] * 2
                first = 2 * HALO
                if n > 0:
                    taken = [inverse_ref[lane, :, n * tile - HALO : n * tile]] * 2 + taken
                    first = 0
                value = jnp.dot(
                    jnp.concatenate(taken, axis=1),
                    t_ref[lane, first:],
                    preferred_element_type=jnp.float32,
                )
                for part in range(2):
                    slot = (2 * n + half) * 2 + part
                    for q in range(2):
                        out_ref.at[slot][pl.ds(q * 8 + c, beams, stride=16), :] = value[
                            q * beams : (q + 1) * beams, part * 128 : (part + 1) * 128
                        ]
            for part in range(2):
                first = n * tile + part * 128
                slot = (2 * n + half) * 2 + part
                stores.append(
                    pltpu.make_async_copy(
                        out_ref.at[slot].reshape(2 * beams, 8, 128),
                        series_ref.at[:, half, :, first : first + 128],
                        store_sems.at[slot],
                    )
                )
                stores[-1].start()
    inner = []
    for b in range(4):
        parts = []
        for a in range(4):
            start = (4 * a + b) * rows
            parts.append(
                tuple(
                    lanes_ref[start + q * stations : start + (q + 1) * stations].astype(
                        jnp.float32
                    )
                    for q in range(2)
                )
            )
        inner.append(fourier(parts, -1.0))
    scale = 1.0 / math.sqrt(chan * ANTENNAS_PER_STN)
    block = (col * 2 + sub) * vis_ref.shape[2]
    own = vis_ref.shape[2]
    for j in range(4):
        re, im = inner[0][j]
        for b in range(1, 4):
            cosine = jnp.float32(0.0)
            sine = jnp.float32(0.0)
            for r in range(4):
                angle = -2.0 * math.pi * b * (4 * r + j) / chan
                cosine = jnp.where(row == r, math.cos(angle), cosine)
                sine = jnp.where(row == r, math.sin(angle), sine)
            yr, yi = inner[b][j]
            re = re + (yr * cosine - yi * sine)
            im = im + (yr * sine + yi * cosine)
        both = (jnp.concatenate([re, im], axis=0) * scale).astype(jnp.bfloat16)
        cross_ref[...] = lax.dot_general(
            both, both, (((1,), (1,)), ((), ())), preferred_element_type=jnp.float32
        )
        own_real = cross_ref[pl.ds(pl.multiple_of(block, own), own)]
        own_imag = cross_ref[pl.ds(pl.multiple_of(stations + block, own), own)]
        vis_ref[j, 0] = (own_real[:, :stations] + own_imag[:, stations:]) * (1.0 / SPEC)
        vis_ref[j, 1] = (own_imag[:, :stations] - own_real[:, stations:]) * (1.0 / SPEC)
    for copy in stores:
        copy.wait()


def call_beams(axes, pieces, matrix, taps):
    params = pltpu.CompilerParams(vmem_limit_bytes=VMEM_LIMIT)
    vmem = pl.BlockSpec(memory_space=pltpu.VMEM)
    smem = pl.BlockSpec(memory_space=pltpu.SMEM)
    chan, frames, tile = taps.shape[1], pieces[0].shape[2], 256
    stations, beams = pieces[0].shape[1] // 2, matrix.shape[1] // 2
    anywhere = pl.BlockSpec(memory_space=pl.ANY)
    slots = frames // 128 * 2
    series, visibilities = pl.pallas_call(
        lambda a, b, c, d, *rest: beam_kernel(axes, (a, b, c, d), *rest),
        out_shape=(
            jax.ShapeDtypeStruct((2 * beams, 2, 8, frames), jnp.float32),
            jax.ShapeDtypeStruct((4, 2, stations // 4, stations), jnp.float32),
        ),
        in_specs=[vmem] * 5 + [smem],
        out_specs=(anywhere, vmem),
        scratch_shapes=[
            pltpu.VMEM(((chan + 3) * 2 * stations, frames), jnp.bfloat16),
            pltpu.VMEM((2 * stations, 2 * stations), jnp.float32),
            pltpu.VMEM((chan, 2 * (tile + HALO), tile), jnp.bfloat16),
            pltpu.VMEM((chan, 2 * beams, frames), jnp.bfloat16),
            pltpu.VMEM((slots, 2 * beams * 8, 128), jnp.float32),
            pltpu.SemaphoreType.DMA((slots,)),
        ],
        compiler_params=params,
        name="beams_and_series",
    )(*pieces, matrix, taps)
    return visibilities, series


def swap(x, axis, mask):
    size = lax.axis_size(axis)
    return lax.ppermute(x, axis, [(i, i ^ mask) for i in range(size)])


def fast_body(
    samples, analysis_taps, synthesis_taps, antenna_station, station_group, beam_group, beam_weights
):
    axes = ("row", "col", "sub")
    params = pltpu.CompilerParams(vmem_limit_bytes=VMEM_LIMIT)
    vmem = pl.BlockSpec(memory_space=pltpu.VMEM)
    smem = pl.BlockSpec(memory_space=pltpu.SMEM)
    local, _, chan, frames = samples.shape
    stations = station_group.shape[0]
    antennas = antenna_station.shape[0]

    held_chan = beam_weights.shape[0]
    beams = beam_weights.shape[2] // 4
    block = jax.ShapeDtypeStruct((4, 2 * local, frames), jnp.bfloat16)
    kept, crossing, paired, far = pl.pallas_call(
        functools.partial(spread_kernel, axes),
        out_shape=[block] * 4,
        in_specs=[vmem],
        out_specs=[vmem] * 4,
        compiler_params=params,
        name="lane_spread",
    )(samples)
    far = swap(far, "sub", 1)
    crossed = swap(crossing, "col", 1)
    paired = swap(paired, "sub", 1)
    far = swap(far, "col", 1)

    packed = jax.ShapeDtypeStruct((beams, held_chan * 2 * stations), jnp.bfloat16)
    members, own_taps, *shares = pl.pallas_call(
        functools.partial(pack_kernel, axes),
        out_shape=[
            jax.ShapeDtypeStruct((2 * stations, 8 * local), jnp.bfloat16),
            jax.ShapeDtypeStruct((analysis_taps.shape[0], frames), jnp.float32),
        ]
        + [packed] * 4,
        in_specs=[vmem] * 3,
        out_specs=[vmem] * 6,
        compiler_params=params,
        cost_estimate=pl.CostEstimate(flops=0, bytes_accessed=4 << 20, transcendentals=0),
        name="weight_shares",
    )(beam_weights, antenna_station.reshape(antennas // local, local), analysis_taps)
    given = [shares[0]] + [swap(shares[m], "row", m) for m in (1, 2, 3)]
    own = (lax.axis_index(("col", "sub", "row"))) * beams
    own_groups = lax.dynamic_slice_in_dim(beam_group, own, beams, 0).reshape(beams, 1)

    lane = jax.ShapeDtypeStruct((2 * stations, frames), jnp.bfloat16)
    sums = pl.pallas_call(
        sum_kernel,
        out_shape=[lane] * 4,
        in_specs=[vmem] * 5,
        out_specs=[vmem] * 4,
        compiler_params=params,
        name="plane_sums",
    )(members, kept, paired, crossed, far)
    moved = [swap(sums[m], "row", m) for m in (1, 2, 3)]
    first, *given = lax.optimization_barrier((sums[0], *given))
    matrix = pl.pallas_call(
        functools.partial(weight_kernel, axes),
        out_shape=jax.ShapeDtypeStruct((4, 2 * beams, 2 * chan * stations), jnp.bfloat16),
        in_specs=[vmem] * 6,
        out_specs=vmem,
        scratch_shapes=[pltpu.VMEM((4,) + packed.shape, jnp.bfloat16)],
        compiler_params=params,
        cost_estimate=pl.CostEstimate(flops=1_000_000_000, bytes_accessed=2 << 20, transcendentals=0),
        name="weight_matrix",
    )(station_group.reshape(1, stations), own_groups, *given)
    filtered = pl.pallas_call(
        filter_kernel,
        out_shape=lane,
        in_specs=[vmem] * 5,
        out_specs=vmem,
        compiler_params=params,
        name="station_filter",
    )(own_taps, first, *moved)

    held = jnp.stack([filtered] + [swap(filtered, "row", m) for m in (1, 2, 3)])
    other = swap(held, "col", 1)
    pieces = [held, other, swap(held, "sub", 1), swap(other, "sub", 1)]

    visibilities, series = call_beams(axes, pieces, matrix, synthesis_taps)
    return visibilities, series.reshape(beams, 2, chan, frames)


def polyphase(signal, coefficients):
    length = signal.shape[-1]
    output = coefficients[0][:, None] * signal
    for tap_index in range(1, coefficients.shape[0]):
        shifted = jnp.pad(
            signal[..., : length - tap_index], [(0, 0)] * (signal.ndim - 1) + [(tap_index, 0)]
        )
        output = output + coefficients[tap_index][:, None] * shifted
    return output


def fourier_table(length, direction):
    indices = jnp.arange(length)
    angles = (
        2.0 * math.pi / length * (indices[:, None] * indices[None, :] % length).astype(jnp.float32)
    )
    cosine_part = jnp.cos(angles)
    sine_part = jnp.sin(angles)
    table = jnp.stack(
        [
            jnp.stack([cosine_part, direction * sine_part]),
            jnp.stack([-direction * sine_part, cosine_part]),
        ]
    )
    return table.transpose(0, 2, 1, 3) * (1.0 / math.sqrt(length))


def general_body(
    samples, analysis_taps, synthesis_taps, antenna_station, station_group, beam_group, beam_weights
):
    high = lax.Precision.HIGHEST
    block_count = lax.axis_size(("col", "sub"))
    block_index = lax.axis_index(("col", "sub"))
    filtered = polyphase(samples.astype(jnp.float32), analysis_taps)
    spectra = jnp.einsum(
        "aqcf,qcpk->apkf", filtered, fourier_table(samples.shape[2], -1.0), precision=high
    ).astype(jnp.bfloat16)
    turned = lax.all_to_all(spectra, "row", split_axis=2, concat_axis=0, tiled=True)
    local_count = spectra.shape[0]
    held_rows = turned.shape[0]
    chan_rows = turned.shape[2]
    spec_len = turned.shape[3]
    station_count = station_group.shape[0]
    flat_width = 2 * chan_rows * spec_len
    tile_rows = station_count // block_count
    shard_rows = lax.all_gather(turned, ("col", "sub"), axis=0, tiled=True)
    row_total = shard_rows.shape[0]
    positions = jnp.arange(row_total, dtype=jnp.int32)
    source_block = positions // held_rows
    offset_rows = positions % held_rows
    source_row = offset_rows // local_count
    antenna = offset_rows % local_count
    global_index = (source_row * block_count + source_block) * local_count + antenna
    targets = antenna_station[global_index]
    wanted = jnp.arange(station_count, dtype=jnp.int32)
    one_hot = (targets[None, :] == wanted[:, None]).astype(jnp.bfloat16)
    summed_values = jnp.dot(
        one_hot, shard_rows.reshape(row_total, flat_width), preferred_element_type=jnp.float32
    )
    flat_stations = (summed_values * (1.0 / math.sqrt(ANTENNAS_PER_STN))).astype(jnp.bfloat16)
    station_list = flat_stations.reshape(station_count, 2, chan_rows, spec_len)
    real_part = station_list[:, 0]
    imag_part = station_list[:, 1]
    own_rows = lax.dynamic_slice_in_dim(station_list, block_index * tile_rows, tile_rows, 0)
    own_real = own_rows[:, 0]
    own_imag = own_rows[:, 1]
    vis_real = (
        jnp.einsum("icf,jcf->cij", own_real, real_part, preferred_element_type=jnp.float32)
        + jnp.einsum("icf,jcf->cij", own_imag, imag_part, preferred_element_type=jnp.float32)
    ) * (1.0 / SPEC)
    vis_imag = (
        jnp.einsum("icf,jcf->cij", own_imag, real_part, preferred_element_type=jnp.float32)
        - jnp.einsum("icf,jcf->cij", own_real, imag_part, preferred_element_type=jnp.float32)
    ) * (1.0 / SPEC)
    visibilities = jnp.stack([vis_real, vis_imag], axis=1)
    beam_block = beam_weights.shape[2]
    own_groups = lax.dynamic_slice_in_dim(beam_group, block_index * beam_block, beam_block, 0)
    members = station_group[:, 0][None, :] == own_groups[:, None]
    scaling = 1.0 / jnp.sqrt(jnp.sum(members.astype(jnp.float32), axis=1))
    weights = jnp.where(members[None, None], beam_weights, jnp.zeros((), jnp.bfloat16))
    weight_real = weights[:, 0]
    imaginary_weight = weights[:, 1]
    beam_real = jnp.einsum(
        "cbs,scf->bcf", weight_real, real_part, preferred_element_type=jnp.float32
    ) - jnp.einsum("cbs,scf->bcf", imaginary_weight, imag_part, preferred_element_type=jnp.float32)
    beam_imag = jnp.einsum(
        "cbs,scf->bcf", weight_real, imag_part, preferred_element_type=jnp.float32
    ) + jnp.einsum("cbs,scf->bcf", imaginary_weight, real_part, preferred_element_type=jnp.float32)
    beams = (jnp.stack([beam_real, beam_imag], axis=1) * scaling[:, None, None, None]).astype(
        jnp.bfloat16
    )
    returned = lax.all_to_all(beams, "row", split_axis=0, concat_axis=2, tiled=True)
    inverse = jnp.einsum(
        "bqkf,qkpc->bpcf",
        returned.astype(jnp.float32),
        fourier_table(returned.shape[2], 1.0),
        precision=high,
    )
    beam_series = polyphase(inverse, synthesis_taps)
    return (visibilities, beam_series)


def solution(mesh):
    sizes = dict(mesh.shape)

    def body(samples, *others):
        chan = samples.shape[2]
        fits = (sizes["row"], sizes["col"], sizes["sub"], chan) == (4, 2, 2, 16)
        return (fast_body if fits else general_body)(samples, *others)

    return jax.shard_map(
        body,
        mesh=mesh,
        in_specs=(
            P(("grp", "row", "col", "sub"), None, None, None),
            P(),
            P(),
            P("grp"),
            P("grp", None),
            P("grp"),
            P(("grp", "row"), None, ("col", "sub"), None),
        ),
        out_specs=(
            P("row", None, ("grp", "col", "sub"), None),
            P(("grp", "col", "sub", "row"), None, None, None),
        ),
        check_vma=False,
    )
```

```python
import functools
import math

import jax
import jax.numpy as jnp
from jax import lax
from jax.experimental import pallas as pl
from jax.experimental.pallas import tpu as pltpu
from jax.sharding import PartitionSpec as P

ANTENNAS_PER_STN = 8
SPEC = 512
VMEM_LIMIT = 24 * 1024 * 1024
HALO = 128


def fourier(parts, sign):
    count = len(parts)
    if count == 1:
        return parts
    even, odd = fourier(parts[0::2], sign), fourier(parts[1::2], sign)
    low, top = [], []
    for k in range(count // 2):
        er, ei = even[k]
        re, im = odd[k]
        if k == 0:
            tr, ti = re, im
        elif 4 * k == count:
            tr, ti = (-sign * im, sign * re)
        else:
            c, s = math.cos(2 * math.pi * k / count), sign * math.sin(2 * math.pi * k / count)
            tr, ti = re * c - im * s, re * s + im * c
        low.append((er + tr, ei + ti))
        top.append((er - tr, ei - ti))
    return low + top


def lane_of(row, col, sub):
    return sub * 8 + col * 4 + row


def spread_kernel(axes, x_hbm, *refs):
    out_refs, (x_ref, sem) = refs[:-2], refs[-2:]
    load = pltpu.make_async_copy(x_hbm, x_ref, sem)
    load.start()
    row, col, sub = (lax.axis_index(a) for a in axes)
    antennas, parts, chan, frames = x_ref.shape
    count = antennas * parts * chan
    shape = (count, count)
    place = lax.broadcasted_iota(jnp.int32, (count, 1), 0)
    antenna = place % antennas
    part = place // antennas % parts
    piece = place // (antennas * parts)
    lane = lane_of(row ^ (piece % 4) ^ 2, col ^ (piece // 4 % 2), sub ^ (piece // 8))
    source = (antenna * parts + part) * chan + lane
    order = jnp.where(lax.broadcasted_iota(jnp.int32, shape, 1) == source, 1.0, 0.0)
    order = order.astype(jnp.bfloat16)
    load.wait()
    moved = jnp.dot(
        order,
        x_ref[...].reshape(count, frames),
        preferred_element_type=jnp.float32,
    ).astype(jnp.bfloat16)
    start = 0
    for ref in out_refs:
        size = ref.shape[0] * ref.shape[1]
        ref[...] = moved[start : start + size].reshape(ref.shape)
        start += size


def member_matrix(axes, names_ref, stations, local):
    row, col, sub = (lax.axis_index(a) for a in axes)
    antennas = 16 * local
    every = jnp.broadcast_to(names_ref[:, :antennas], (8, antennas))
    names = []
    for k in range(4):
        owner = (row * 2 + (col ^ (k // 2))) * 2 + (sub ^ (k % 2))
        names += [pltpu.roll(every, lax.rem(antennas - owner * local, antennas), 1)[:1, :local]] * 2
    names = jnp.concatenate(names, axis=1)
    shape = (2 * stations, 8 * local)
    place = lax.broadcasted_iota(jnp.int32, shape, 0)
    column = lax.broadcasted_iota(jnp.int32, shape, 1)
    same = ((place % stations).astype(jnp.float32) == names) & (place // stations == column // local % 2)
    return jnp.where(same, 1.0, 0.0).astype(jnp.bfloat16)


def own_taps(axes, taps, count, chan):
    lane = lane_of(*(lax.axis_index(a) for a in axes))
    shape = (count, count * chan)
    column = lax.broadcasted_iota(jnp.int32, shape, 1)
    mine = column == lax.broadcasted_iota(jnp.int32, shape, 0) * chan + lane
    taps = jnp.where(mine, jnp.broadcast_to(taps, shape), 0.0)
    return jnp.sum(taps, axis=1, keepdims=True)


def sum_kernel(axes, first, names_ref, *refs):
    x_refs, out_refs = refs[:4], refs[4:6]
    for taps_ref in refs[6:]:
        count = taps_ref.shape[0]
        taps = names_ref[:, names_ref.shape[1] - count * count :]
        taps_ref[...] = jnp.broadcast_to(own_taps(axes, taps, count, count), taps_ref.shape)
    stations, local = out_refs[0].shape[0] // 2, x_refs[0].shape[1] // 2
    members = member_matrix(axes, names_ref, stations, local)
    for k, ref in enumerate(out_refs):
        rows = jnp.concatenate([x[first + k if x.shape[0] == 4 else k] for x in x_refs], axis=0)
        ref[...] = jnp.dot(members, rows, preferred_element_type=jnp.float32).astype(ref.dtype)


def filter_kernel(taps_ref, *refs):
    x_refs, share_refs, out_refs = refs[:4], refs[4:7], refs[7:]
    rows = out_refs[0].shape[0]
    total = x_refs[0][...]
    for ref in x_refs[1:]:
        total = total + ref[...].astype(jnp.float32)
    place = lax.broadcasted_iota(jnp.int32, total.shape, 1)
    result = total * taps_ref[0:1]
    for tap in range(1, taps_ref.shape[0]):
        moved = jnp.where(place >= tap, pltpu.roll(total, tap, 1), 0.0)
        result = result + moved * taps_ref[tap : tap + 1]
    result = result.astype(out_refs[0].dtype)
    out_refs[0][...] = result
    for ref, share in zip(out_refs[1:], share_refs):
        ref[:rows] = result
        ref[rows:] = share[...]


def pack_kernel(axes, w_ref, *out_refs):
    row = lax.axis_index(axes[0])
    chan, _, _, width = w_ref.shape
    beams = width // 4
    for k in range(chan):
        for q in range(2):
            place = (2 * k + q) * beams
            parts = [w_ref[k, q, :, j * beams : (j + 1) * beams] for j in range(4)]
            for mask, ref in enumerate(out_refs):
                taken = parts[0]
                for j in range(1, 4):
                    taken = jnp.where((row ^ mask) == j, parts[j], taken)
                ref[:, place : place + beams] = taken


def bands(taps_ref, lane, rows, cols):
    wide = 2 * cols
    places = lax.broadcasted_iota(jnp.int32, (8, wide), 1)
    base = jnp.zeros((8, wide), jnp.float32)
    for tap in range(taps_ref.shape[0]):
        base = jnp.where(places == (tap - HALO) % wide, taps_ref[tap, lane], base)
    whole = jnp.broadcast_to(base[0:1], (rows, wide))
    whole = pltpu.roll(whole, 0, 1, stride=1, stride_axis=0)[:, :cols]
    high = whole.astype(jnp.bfloat16)
    low = (whole - high.astype(jnp.float32)).astype(jnp.bfloat16)
    return jnp.concatenate([high[:HALO], low[:HALO], high[HALO:], low[HALO:]], axis=0)


def weight_kernel(axes, groups_ref, beam_ref, taps_ref, *refs):
    row, col, sub = (lax.axis_index(a) for a in axes)
    w_refs, (m_ref, t_ref, all_ref) = refs[:4], refs[4:]
    stations, beams = groups_ref.shape[1], m_ref.shape[1] // 2
    held = all_ref.shape[2] // (2 * beams)
    chan = 4 * held
    for mask, ref in enumerate(w_refs):
        all_ref[row ^ mask] = ref[ref.shape[0] - stations :]
    square = (stations, stations)
    diagonal = lax.broadcasted_iota(jnp.int32, square, 0) == lax.broadcasted_iota(
        jnp.int32, square, 1
    )
    groups = jnp.broadcast_to(groups_ref[...], square).astype(jnp.float32)
    groups = jnp.sum(jnp.where(diagonal, groups, 0.0), axis=1, keepdims=True)
    total = beam_ref.shape[1]
    first = ((col * 2 + sub) * 4 + row) * beams
    every = jnp.broadcast_to(beam_ref[...], (8, total))
    wanted = pltpu.roll(every, lax.rem(total - first, total), 1)[:1, :beams]
    members = groups == wanted.astype(jnp.float32)
    scale = (1.0 / (chan * math.sqrt(ANTENNAS_PER_STN))) / jnp.sqrt(
        jnp.sum(members.astype(jnp.float32), axis=0, keepdims=True)
    )
    zero = jnp.zeros((), jnp.float32)
    parts = []
    for k in range(chan):
        whole = all_ref[k // held].astype(jnp.float32)
        places = [(2 * (k % held) + q) * beams for q in range(2)]
        parts.append(tuple(jnp.where(members, whole[:, p : p + beams], zero) for p in places))
    parts = fourier(parts, -1.0)
    real = [p[0] * scale for p in parts]
    imag = [p[1] * scale for p in parts]
    upper = jnp.concatenate([v for k in range(chan) for v in (real[k], -imag[k])], axis=0)
    lower = jnp.concatenate([v for k in range(chan) for v in (imag[k], real[k])], axis=0)
    whole = jnp.concatenate([upper, lower], axis=1).T.astype(m_ref.dtype)
    width = whole.shape[1] // 4
    for u in range(4):
        for j in range(4):
            t = (u + j) % 4
            m_ref[u, :, t * width : (t + 1) * width] = whole[:, j * width : (j + 1) * width]
    for c in range(chan):
        t_ref[c] = bands(taps_ref, c, t_ref.shape[1] // 2, t_ref.shape[2])


def beam_kernel(
    axes,
    x_refs,
    m_ref,
    t_ref,
    series_ref,
    vis_ref,
    lanes_ref,
    cross_ref,
    inverse_ref,
    out_ref,
    store_sems,
):
    row, col, sub = (lax.axis_index(a) for a in axes)
    rows = x_refs[0].shape[1]
    stations = rows // 2
    chan = 4 * 4
    frames = lanes_ref.shape[1]

    for place, ref in enumerate(x_refs):
        for m in range(4):
            lane = lane_of(row ^ m, col ^ (place % 2), sub ^ (place // 2))
            lanes_ref[pl.ds(pl.multiple_of(lane * rows, rows), rows)] = ref[m]
    wrap = 3 * rows
    lanes_ref[chan * rows : chan * rows + wrap] = lanes_ref[0:wrap]
    beams = m_ref.shape[1] // 2
    tile = t_ref.shape[2]
    stores = []
    for half in range(2):
        some = m_ref[2 * half : 2 * half + 2].reshape(4 * beams, chan * rows)
        for v in range(4):
            window = lanes_ref[v * rows : (v + chan) * rows]
            found = jnp.dot(some, window, preferred_element_type=jnp.float32)
            found = found.astype(jnp.bfloat16)
            for u in range(2):
                inverse_ref[8 * half + 4 * u + v] = found[2 * beams * u : 2 * beams * (u + 1)]
        for n in range(frames // tile):
            for c in range(8):
                lane = 8 * half + c
                taken = [inverse_ref[lane, :, n * tile : (n + 1) * tile]] * 2
                first = 2 * HALO
                if n > 0:
                    taken = [inverse_ref[lane, :, n * tile - HALO : n * tile]] * 2 + taken
                    first = 0
                value = jnp.dot(
                    jnp.concatenate(taken, axis=1),
                    t_ref[lane, first:],
                    preferred_element_type=jnp.float32,
                )
                for part in range(2):
                    slot = (2 * n + half) * 2 + part
                    for q in range(2):
                        out_ref.at[slot][pl.ds(q * 8 + c, beams, stride=16), :] = value[
                            q * beams : (q + 1) * beams, part * 128 : (part + 1) * 128
                        ]
            for part in range(2):
                first = n * tile + part * 128
                slot = (2 * n + half) * 2 + part
                stores.append(
                    pltpu.make_async_copy(
                        out_ref.at[slot].reshape(2 * beams, 8, 128),
                        series_ref.at[:, half, :, first : first + 128],
                        store_sems.at[slot],
                    )
                )
                stores[-1].start()
    inner = []
    for b in range(4):
        parts = []
        for a in range(4):
            start = (4 * a + b) * rows
            parts.append(
                tuple(
                    lanes_ref[start + q * stations : start + (q + 1) * stations].astype(
                        jnp.float32
                    )
                    for q in range(2)
                )
            )
        inner.append(fourier(parts, -1.0))
    scale = 1.0 / math.sqrt(chan * ANTENNAS_PER_STN)
    block = (col * 2 + sub) * vis_ref.shape[2]
    own = vis_ref.shape[2]
    for j in range(4):
        re, im = inner[0][j]
        for b in range(1, 4):
            cosine = jnp.float32(0.0)
            sine = jnp.float32(0.0)
            for r in range(4):
                angle = -2.0 * math.pi * b * (4 * r + j) / chan
                cosine = jnp.where(row == r, math.cos(angle), cosine)
                sine = jnp.where(row == r, math.sin(angle), sine)
            yr, yi = inner[b][j]
            re = re + (yr * cosine - yi * sine)
            im = im + (yr * sine + yi * cosine)
        both = (jnp.concatenate([re, im], axis=0) * scale).astype(jnp.bfloat16)
        cross_ref[...] = lax.dot_general(
            both, both, (((1,), (1,)), ((), ())), preferred_element_type=jnp.float32
        )
        own_real = cross_ref[pl.ds(pl.multiple_of(block, own), own)]
        own_imag = cross_ref[pl.ds(pl.multiple_of(stations + block, own), own)]
        vis_ref[j, 0] = (own_real[:, :stations] + own_imag[:, stations:]) * (1.0 / SPEC)
        vis_ref[j, 1] = (own_imag[:, :stations] - own_real[:, stations:]) * (1.0 / SPEC)
    for copy in stores:
        copy.wait()


def call_beams(axes, pieces, matrix, bands):
    params = pltpu.CompilerParams(vmem_limit_bytes=VMEM_LIMIT)
    vmem = pl.BlockSpec(memory_space=pltpu.VMEM)
    chan, frames = bands.shape[0], pieces[0].shape[2]
    stations, beams = pieces[0].shape[1] // 2, matrix.shape[1] // 2
    anywhere = pl.BlockSpec(memory_space=pl.ANY)
    slots = frames // 128 * 2
    series, visibilities = pl.pallas_call(
        lambda *refs: beam_kernel(axes, refs[: len(pieces)], *refs[len(pieces) :]),
        out_shape=(
            jax.ShapeDtypeStruct((2 * beams, 2, 8, frames), jnp.float32),
            jax.ShapeDtypeStruct((4, 2, stations // 4, stations), jnp.float32),
        ),
        in_specs=[vmem] * (len(pieces) + 2),
        out_specs=(anywhere, vmem),
        scratch_shapes=[
            pltpu.VMEM(((chan + 3) * 2 * stations, frames), jnp.bfloat16),
            pltpu.VMEM((2 * stations, 2 * stations), jnp.float32),
            pltpu.VMEM((chan, 2 * beams, frames), jnp.bfloat16),
            pltpu.VMEM((slots, 2 * beams * 8, 128), jnp.float32),
            pltpu.SemaphoreType.DMA((slots,)),
        ],
        compiler_params=params,
        name="beams_and_series",
    )(*pieces, matrix, bands)
    return visibilities, series


def swap(x, axis, mask):
    size = lax.axis_size(axis)
    return lax.ppermute(x, axis, [(i, i ^ mask) for i in range(size)])


def fast_body(
    samples, analysis_taps, synthesis_taps, antenna_station, station_group, beam_group, beam_weights
):
    axes = ("row", "col", "sub")
    params = pltpu.CompilerParams(vmem_limit_bytes=VMEM_LIMIT)
    vmem = pl.BlockSpec(memory_space=pltpu.VMEM)
    smem = pl.BlockSpec(memory_space=pltpu.SMEM)
    hbm = pl.BlockSpec(memory_space=pltpu.HBM)
    local, _, chan, frames = samples.shape
    stations = station_group.shape[0]
    antennas = antenna_station.shape[0]

    held_chan = beam_weights.shape[0]
    beams = beam_weights.shape[2] // 4
    block = jax.ShapeDtypeStruct((4, 2 * local, frames), jnp.bfloat16)
    half = jax.ShapeDtypeStruct((2, 2 * local, frames), jnp.bfloat16)
    kept, crossing_a, crossing_b, paired, far_a, far_b = pl.pallas_call(
        functools.partial(spread_kernel, axes),
        out_shape=[block, half, half, block, half, half],
        in_specs=[hbm],
        out_specs=[vmem] * 6,
        scratch_shapes=[pltpu.VMEM(samples.shape, samples.dtype), pltpu.SemaphoreType.DMA],
        compiler_params=params,
        name="lane_spread",
    )(samples)
    far_a = swap(far_a, "sub", 1)
    crossing_a = swap(crossing_a, "col", 1)
    far_a = swap(far_a, "col", 1)
    far_b = swap(far_b, "sub", 1)
    paired = swap(paired, "sub", 1)
    crossing_b = swap(crossing_b, "col", 1)
    far_b = swap(far_b, "col", 1)

    lane = jax.ShapeDtypeStruct((2 * stations, frames), jnp.bfloat16)
    names = jnp.concatenate([antenna_station.astype(jnp.float32), analysis_taps.reshape(-1)])
    names = names.reshape(1, -1)
    sums2, sums3, taps = pl.pallas_call(
        functools.partial(sum_kernel, axes, 0),
        out_shape=[lane] * 2
        + [jax.ShapeDtypeStruct((analysis_taps.shape[0], frames), jnp.float32)],
        in_specs=[vmem] * 5,
        out_specs=[vmem] * 3,
        compiler_params=params,
        name="plane_sums_far",
    )(names, kept, paired, crossing_a, far_a)
    sums3, sums2 = swap(sums3, "row", 3), swap(sums2, "row", 2)
    sums0, sums1 = pl.pallas_call(
        functools.partial(sum_kernel, axes, 2),
        out_shape=[jax.ShapeDtypeStruct(lane.shape, jnp.float32), lane],
        in_specs=[vmem] * 5,
        out_specs=[vmem] * 2,
        compiler_params=params,
        name="plane_sums_near",
    )(names, kept, paired, crossing_b, far_b)

    share = jax.ShapeDtypeStruct((stations, 2 * held_chan * beams), jnp.bfloat16)
    shares = pl.pallas_call(
        functools.partial(pack_kernel, axes),
        out_shape=[share] * 4,
        in_specs=[vmem],
        out_specs=[vmem] * 4,
        compiler_params=params,
        cost_estimate=pl.CostEstimate(flops=0, bytes_accessed=8 << 20, transcendentals=0),
        name="weight_shares",
    )(beam_weights.transpose(0, 1, 3, 2))

    lane_share = jax.ShapeDtypeStruct((3 * stations, frames), jnp.bfloat16)
    filtered, *sent = pl.pallas_call(
        filter_kernel,
        out_shape=[lane] + [lane_share] * 3,
        in_specs=[vmem] * 8,
        out_specs=[vmem] * 4,
        compiler_params=params,
        name="station_filter",
    )(taps, sums0, swap(sums1, "row", 1), sums2, sums3, *shares[1:])
    moved = [swap(x, "row", m) for x, m in zip(sent, (1, 2, 3))]

    tile = 256
    matrix, bands = pl.pallas_call(
        functools.partial(weight_kernel, axes),
        out_shape=[
            jax.ShapeDtypeStruct((4, 2 * beams, 2 * chan * stations), jnp.bfloat16),
            jax.ShapeDtypeStruct((chan, 2 * (tile + HALO), tile), jnp.bfloat16),
        ],
        in_specs=[vmem, vmem, smem] + [vmem] * 4,
        out_specs=[vmem] * 2,
        scratch_shapes=[pltpu.VMEM((4,) + share.shape, jnp.bfloat16)],
        compiler_params=params,
        cost_estimate=pl.CostEstimate(flops=2_000_000_000, bytes_accessed=2 << 20, transcendentals=0),
        name="weight_matrix",
    )(
        station_group.reshape(1, stations),
        beam_group.reshape(1, beam_group.shape[0]),
        synthesis_taps,
        shares[0],
        *moved,
    )

    held = jnp.stack([filtered] + [x[: 2 * stations] for x in moved])
    other = swap(held, "col", 1)
    other, matrix, bands = lax.optimization_barrier((other, matrix, bands))
    pieces = [held, other]
    pieces += [swap(x, "sub", 1) for x in pieces]

    visibilities, series = call_beams(axes, pieces, matrix, bands)
    return visibilities, series.reshape(beams, 2, chan, frames)


def polyphase(signal, coefficients):
    length = signal.shape[-1]
    output = coefficients[0][:, None] * signal
    for tap_index in range(1, coefficients.shape[0]):
        shifted = jnp.pad(
            signal[..., : length - tap_index], [(0, 0)] * (signal.ndim - 1) + [(tap_index, 0)]
        )
        output = output + coefficients[tap_index][:, None] * shifted
    return output


def fourier_table(length, direction):
    indices = jnp.arange(length)
    angles = (
        2.0 * math.pi / length * (indices[:, None] * indices[None, :] % length).astype(jnp.float32)
    )
    cosine_part = jnp.cos(angles)
    sine_part = jnp.sin(angles)
    table = jnp.stack(
        [
            jnp.stack([cosine_part, direction * sine_part]),
            jnp.stack([-direction * sine_part, cosine_part]),
        ]
    )
    return table.transpose(0, 2, 1, 3) * (1.0 / math.sqrt(length))


def general_body(
    samples, analysis_taps, synthesis_taps, antenna_station, station_group, beam_group, beam_weights
):
    high = lax.Precision.HIGHEST
    block_count = lax.axis_size(("col", "sub"))
    block_index = lax.axis_index(("col", "sub"))
    filtered = polyphase(samples.astype(jnp.float32), analysis_taps)
    spectra = jnp.einsum(
        "aqcf,qcpk->apkf", filtered, fourier_table(samples.shape[2], -1.0), precision=high
    ).astype(jnp.bfloat16)
    turned = lax.all_to_all(spectra, "row", split_axis=2, concat_axis=0, tiled=True)
    local_count = spectra.shape[0]
    held_rows = turned.shape[0]
    chan_rows = turned.shape[2]
    spec_len = turned.shape[3]
    station_count = station_group.shape[0]
    flat_width = 2 * chan_rows * spec_len
    tile_rows = station_count // block_count
    shard_rows = lax.all_gather(turned, ("col", "sub"), axis=0, tiled=True)
    row_total = shard_rows.shape[0]
    positions = jnp.arange(row_total, dtype=jnp.int32)
    source_block = positions // held_rows
    offset_rows = positions % held_rows
    source_row = offset_rows // local_count
    antenna = offset_rows % local_count
    global_index = (source_row * block_count + source_block) * local_count + antenna
    targets = antenna_station[global_index]
    wanted = jnp.arange(station_count, dtype=jnp.int32)
    one_hot = (targets[None, :] == wanted[:, None]).astype(jnp.bfloat16)
    summed_values = jnp.dot(
        one_hot, shard_rows.reshape(row_total, flat_width), preferred_element_type=jnp.float32
    )
    flat_stations = (summed_values * (1.0 / math.sqrt(ANTENNAS_PER_STN))).astype(jnp.bfloat16)
    station_list = flat_stations.reshape(station_count, 2, chan_rows, spec_len)
    real_part = station_list[:, 0]
    imag_part = station_list[:, 1]
    own_rows = lax.dynamic_slice_in_dim(station_list, block_index * tile_rows, tile_rows, 0)
    own_real = own_rows[:, 0]
    own_imag = own_rows[:, 1]
    vis_real = (
        jnp.einsum("icf,jcf->cij", own_real, real_part, preferred_element_type=jnp.float32)
        + jnp.einsum("icf,jcf->cij", own_imag, imag_part, preferred_element_type=jnp.float32)
    ) * (1.0 / SPEC)
    vis_imag = (
        jnp.einsum("icf,jcf->cij", own_imag, real_part, preferred_element_type=jnp.float32)
        - jnp.einsum("icf,jcf->cij", own_real, imag_part, preferred_element_type=jnp.float32)
    ) * (1.0 / SPEC)
    visibilities = jnp.stack([vis_real, vis_imag], axis=1)
    beam_block = beam_weights.shape[2]
    own_groups = lax.dynamic_slice_in_dim(beam_group, block_index * beam_block, beam_block, 0)
    members = station_group[:, 0][None, :] == own_groups[:, None]
    scaling = 1.0 / jnp.sqrt(jnp.sum(members.astype(jnp.float32), axis=1))
    weights = jnp.where(members[None, None], beam_weights, jnp.zeros((), jnp.bfloat16))
    weight_real = weights[:, 0]
    imaginary_weight = weights[:, 1]
    beam_real = jnp.einsum(
        "cbs,scf->bcf", weight_real, real_part, preferred_element_type=jnp.float32
    ) - jnp.einsum("cbs,scf->bcf", imaginary_weight, imag_part, preferred_element_type=jnp.float32)
    beam_imag = jnp.einsum(
        "cbs,scf->bcf", weight_real, imag_part, preferred_element_type=jnp.float32
    ) + jnp.einsum("cbs,scf->bcf", imaginary_weight, real_part, preferred_element_type=jnp.float32)
    beams = (jnp.stack([beam_real, beam_imag], axis=1) * scaling[:, None, None, None]).astype(
        jnp.bfloat16
    )
    returned = lax.all_to_all(beams, "row", split_axis=0, concat_axis=2, tiled=True)
    inverse = jnp.einsum(
        "bqkf,qkpc->bpcf",
        returned.astype(jnp.float32),
        fourier_table(returned.shape[2], 1.0),
        precision=high,
    )
    beam_series = polyphase(inverse, synthesis_taps)
    return (visibilities, beam_series)


def solution(mesh):
    sizes = dict(mesh.shape)

    def body(samples, *others):
        chan = samples.shape[2]
        fits = (sizes["row"], sizes["col"], sizes["sub"], chan) == (4, 2, 2, 16)
        return (fast_body if fits else general_body)(samples, *others)

    return jax.shard_map(
        body,
        mesh=mesh,
        in_specs=(
            P(("grp", "row", "col", "sub"), None, None, None),
            P(),
            P(),
            P("grp"),
            P("grp", None),
            P("grp"),
            P(("grp", "row"), None, ("col", "sub"), None),
        ),
        out_specs=(
            P("row", None, ("grp", "col", "sub"), None),
            P(("grp", "col", "sub", "row"), None, None, None),
        ),
        check_vma=False,
    )
```

```python
import functools
import math

import jax
import jax.numpy as jnp
from jax import lax
from jax.experimental import pallas as pl
from jax.experimental.pallas import tpu as pltpu
from jax.sharding import PartitionSpec as P

ANTENNAS_PER_STN = 8
SPEC = 512
VMEM_LIMIT = 24 * 1024 * 1024
HALO = 128
FLIPS = ((0, 0), (0, 1), (1, 0), (1, 1))


def fourier(parts, sign):
    count = len(parts)
    if count == 1:
        return parts
    even, odd = fourier(parts[0::2], sign), fourier(parts[1::2], sign)
    low, top = [], []
    for k in range(count // 2):
        er, ei = even[k]
        re, im = odd[k]
        if k == 0:
            tr, ti = re, im
        elif 4 * k == count:
            tr, ti = (-sign * im, sign * re)
        else:
            c, s = math.cos(2 * math.pi * k / count), sign * math.sin(2 * math.pi * k / count)
            tr, ti = re * c - im * s, re * s + im * c
        low.append((er + tr, ei + ti))
        top.append((er - tr, ei - ti))
    return low + top


def lane_of(row, col, sub):
    return sub * 8 + col * 4 + row


def spread_kernel(axes, x_ref, *out_refs):
    row, col, sub = (lax.axis_index(a) for a in axes)
    antennas, parts, chan, frames = x_ref.shape
    count = antennas * parts * chan
    shape = (count, count)
    place = lax.broadcasted_iota(jnp.int32, (count, 1), 0)
    antenna = place % antennas
    part = place // antennas % parts
    piece = place // (antennas * parts)
    lane = lane_of(row ^ (piece % 4) ^ 2, col ^ (piece // 4 % 2), sub ^ (piece // 8))
    source = (antenna * parts + part) * chan + lane
    order = jnp.where(lax.broadcasted_iota(jnp.int32, shape, 1) == source, 1.0, 0.0)
    moved = jnp.dot(
        order.astype(jnp.bfloat16),
        x_ref[...].reshape(count, frames),
        preferred_element_type=jnp.float32,
    ).astype(jnp.bfloat16)
    start = 0
    for ref in out_refs:
        size = ref.shape[0] * ref.shape[1]
        ref[...] = moved[start : start + size].reshape(ref.shape)
        start += size


def member_matrix(axes, names_ref, stations, local):
    row, col, sub = (lax.axis_index(a) for a in axes)
    antennas = names_ref.shape[1]
    every = jnp.broadcast_to(names_ref[...], (8, antennas))
    names = []
    for k in range(4):
        owner = (row * 2 + (col ^ (k // 2))) * 2 + (sub ^ (k % 2))
        names += [pltpu.roll(every, lax.rem(antennas - owner * local, antennas), 1)[:1, :local]] * 2
    names = jnp.concatenate(names, axis=1)
    shape = (2 * stations, 8 * local)
    place = lax.broadcasted_iota(jnp.int32, shape, 0)
    column = lax.broadcasted_iota(jnp.int32, shape, 1)
    same = (place % stations == names) & (place // stations == column // local % 2)
    return jnp.where(same, 1.0, 0.0).astype(jnp.bfloat16)


def table_kernel(axes, names_ref, taps_ref, members_ref, own_taps_ref):
    stations, local = members_ref.shape[0] // 2, members_ref.shape[1] // 8
    members_ref[...] = member_matrix(axes, names_ref, stations, local)
    taps = taps_ref[...]
    lane = lane_of(*(lax.axis_index(a) for a in axes))
    mine = lax.broadcasted_iota(jnp.int32, taps.shape, 1) == lane
    own = jnp.sum(jnp.where(mine, taps, 0.0), axis=1, keepdims=True)
    own_taps_ref[...] = jnp.broadcast_to(own, own_taps_ref.shape)


def sum_kernel(first, members_ref, *refs):
    x_refs, out_refs = refs[:4], refs[4:]
    for k, ref in enumerate(out_refs):
        rows = jnp.concatenate([x[first + k if x.shape[0] == 4 else k] for x in x_refs], axis=0)
        ref[...] = jnp.dot(
            members_ref[...], rows, preferred_element_type=jnp.float32
        ).astype(ref.dtype)


def filter_kernel(taps_ref, *refs):
    x_refs, share_refs, out_refs = refs[:4], refs[4:7], refs[7:]
    rows = out_refs[0].shape[0]
    total = x_refs[0][...]
    for ref in x_refs[1:]:
        total = total + ref[...].astype(jnp.float32)
    place = lax.broadcasted_iota(jnp.int32, total.shape, 1)
    result = total * taps_ref[0:1]
    for tap in range(1, taps_ref.shape[0]):
        moved = jnp.where(place >= tap, pltpu.roll(total, tap, 1), 0.0)
        result = result + moved * taps_ref[tap : tap + 1]
    result = result.astype(out_refs[0].dtype)
    out_refs[0][...] = result
    for ref, share in zip(out_refs[1:], share_refs):
        ref[:rows] = result
        ref[rows:] = share[...]


def pack_kernel(axes, w_ref, *out_refs):
    row = lax.axis_index(axes[0])
    chan, _, _, width = w_ref.shape
    beams = width // 4
    for k in range(chan):
        for q in range(2):
            place = (2 * k + q) * beams
            parts = [w_ref[k, q, :, j * beams : (j + 1) * beams] for j in range(4)]
            for mask, ref in enumerate(out_refs):
                taken = parts[0]
                for j in range(1, 4):
                    taken = jnp.where((row ^ mask) == j, parts[j], taken)
                ref[:, place : place + beams] = taken


def bands(taps_ref, lane, rows, cols):
    wide = 2 * cols
    places = lax.broadcasted_iota(jnp.int32, (8, wide), 1)
    base = jnp.zeros((8, wide), jnp.float32)
    for tap in range(taps_ref.shape[0]):
        base = jnp.where(places == (tap - HALO) % wide, taps_ref[tap, lane], base)
    whole = jnp.broadcast_to(base[0:1], (rows, wide))
    whole = pltpu.roll(whole, 0, 1, stride=1, stride_axis=0)[:, :cols]
    high = whole.astype(jnp.bfloat16)
    low = (whole - high.astype(jnp.float32)).astype(jnp.bfloat16)
    return jnp.concatenate([high[:HALO], low[:HALO], high[HALO:], low[HALO:]], axis=0)


def band_kernel(axes, groups_ref, beam_ref, taps_ref, t_ref, chosen_ref, scale_ref):
    row, col, sub = (lax.axis_index(a) for a in axes)
    stations, beams = chosen_ref.shape
    chan = t_ref.shape[0]
    square = (stations, stations)
    diagonal = lax.broadcasted_iota(jnp.int32, square, 0) == lax.broadcasted_iota(
        jnp.int32, square, 1
    )
    groups = jnp.broadcast_to(groups_ref[...], square).astype(jnp.float32)
    groups = jnp.sum(jnp.where(diagonal, groups, 0.0), axis=1, keepdims=True)
    total = beam_ref.shape[1]
    first = ((col * 2 + sub) * 4 + row) * beams
    every = jnp.broadcast_to(beam_ref[...], (8, total))
    wanted = pltpu.roll(every, lax.rem(total - first, total), 1)[:1, :beams]
    chosen = (groups == wanted.astype(jnp.float32)).astype(jnp.float32)
    chosen_ref[...] = chosen
    scale = (1.0 / (chan * math.sqrt(ANTENNAS_PER_STN))) / jnp.sqrt(
        jnp.sum(chosen, axis=0, keepdims=True)
    )
    scale_ref[...] = jnp.broadcast_to(scale, scale_ref.shape)
    for c in range(chan):
        t_ref[c] = bands(taps_ref, c, t_ref.shape[1] // 2, t_ref.shape[2])


def weight_kernel(axes, chosen_ref, scale_ref, *refs):
    row = lax.axis_index(axes[0])
    w_refs, (m_ref, all_ref) = refs[:4], refs[4:]
    stations, beams = chosen_ref.shape
    held = all_ref.shape[2] // (2 * beams)
    chan = 4 * held
    for mask, ref in enumerate(w_refs):
        all_ref[row ^ mask] = ref[ref.shape[0] - stations :]
    members = chosen_ref[...] > 0
    scale = scale_ref[...]
    zero = jnp.zeros((), jnp.float32)
    parts = []
    for k in range(chan):
        whole = all_ref[k // held].astype(jnp.float32)
        places = [(2 * (k % held) + q) * beams for q in range(2)]
        parts.append(tuple(jnp.where(members, whole[:, p : p + beams], zero) for p in places))
    parts = fourier(parts, -1.0)
    real = [p[0] * scale for p in parts]
    imag = [p[1] * scale for p in parts]
    upper = jnp.concatenate([v for k in range(chan) for v in (real[k], -imag[k])], axis=0)
    lower = jnp.concatenate([v for k in range(chan) for v in (imag[k], real[k])], axis=0)
    whole = jnp.concatenate([upper, lower], axis=1).T.astype(m_ref.dtype)
    width = whole.shape[1]
    step = 2 * stations
    odd = jnp.concatenate([whole[:, width - step :], whole[:, : width - step]], axis=1)
    for c in range(chan):
        base = odd if c % 2 else whole
        start = c // 2 * 2 * step
        m_ref[c, :, start:] = base[:, : width - start]
        if start:
            m_ref[c, :, :start] = base[:, width - start :]


def gather_lanes(axes, x_refs, flips, lanes_ref):
    row, col, sub = (lax.axis_index(a) for a in axes)
    rows = x_refs[0].shape[1]
    for (dc, ds), ref in zip(flips, x_refs):
        for m in range(4):
            lane = lane_of(row ^ m, col ^ dc, sub ^ ds)
            lanes_ref[pl.ds(pl.multiple_of(lane * rows, rows), rows)] = ref[m]


def lane_products(axes, flips, m_ref, lanes_ref, first, count):
    col, sub = (lax.axis_index(a) for a in axes[1:])
    width = 4 * lanes_ref.shape[0] // 16
    total = None
    for dc, ds in flips:
        start = pl.multiple_of((2 * (sub ^ ds) + (col ^ dc)) * width, width)
        some = m_ref[first : first + count, :, pl.ds(start, width)]
        some = some.reshape(count * m_ref.shape[1], width)
        found = jnp.dot(some, lanes_ref[pl.ds(start, width)], preferred_element_type=jnp.float32)
        total = found if total is None else total + found
    return total


def part_kernel(axes, flips, m_ref, *refs):
    x_refs, (sum_ref, lanes_ref) = refs[: len(flips)], refs[-2:]
    before = refs[len(flips) : -2]
    gather_lanes(axes, x_refs, flips, lanes_ref)
    for first in range(0, m_ref.shape[0], 4):
        found = lane_products(axes, flips, m_ref, lanes_ref, first, 4)
        found = found.reshape((4,) + sum_ref.shape[1:])
        for ref in before:
            found = found + ref[first : first + 4]
        sum_ref[first : first + 4] = found


def beam_kernel(
    axes,
    x_refs,
    m_ref,
    t_ref,
    sum_ref,
    series_ref,
    vis_ref,
    lanes_ref,
    cross_ref,
    inverse_ref,
    out_ref,
    store_sems,
):
    row, col, sub = (lax.axis_index(a) for a in axes)
    rows = x_refs[0].shape[1]
    stations = rows // 2
    chan = 4 * 4
    frames = lanes_ref.shape[1]

    gather_lanes(axes, x_refs, FLIPS, lanes_ref)
    beams = m_ref.shape[1] // 2
    tile = t_ref.shape[2]
    stores = []
    for half in range(2):
        for first in range(8 * half, 8 * half + 8, 4):
            found = lane_products(axes, FLIPS[3:], m_ref, lanes_ref, first, 4)
            found = found.reshape((4,) + sum_ref.shape[1:]) + sum_ref[first : first + 4]
            inverse_ref[first : first + 4] = found.astype(jnp.bfloat16)
        for n in range(frames // tile):
            for c in range(8):
                lane = 8 * half + c
                taken = [inverse_ref[lane, :, n * tile : (n + 1) * tile]] * 2
                first = 2 * HALO
                if n > 0:
                    taken = [inverse_ref[lane, :, n * tile - HALO : n * tile]] * 2 + taken
                    first = 0
                value = jnp.dot(
                    jnp.concatenate(taken, axis=1),
                    t_ref[lane, first:],
                    preferred_element_type=jnp.float32,
                )
                for part in range(2):
                    slot = (2 * n + half) * 2 + part
                    for q in range(2):
                        out_ref.at[slot][pl.ds(q * 8 + c, beams, stride=16), :] = value[
                            q * beams : (q + 1) * beams, part * 128 : (part + 1) * 128
                        ]
            for part in range(2):
                first = n * tile + part * 128
                slot = (2 * n + half) * 2 + part
                stores.append(
                    pltpu.make_async_copy(
                        out_ref.at[slot].reshape(2 * beams, 8, 128),
                        series_ref.at[:, half, :, first : first + 128],
                        store_sems.at[slot],
                    )
                )
                stores[-1].start()
    inner = []
    for b in range(4):
        parts = []
        for a in range(4):
            start = (4 * a + b) * rows
            parts.append(
                tuple(
                    lanes_ref[start + q * stations : start + (q + 1) * stations].astype(
                        jnp.float32
                    )
                    for q in range(2)
                )
            )
        inner.append(fourier(parts, -1.0))
    scale = 1.0 / math.sqrt(chan * ANTENNAS_PER_STN)
    block = (col * 2 + sub) * vis_ref.shape[2]
    own = vis_ref.shape[2]
    for j in range(4):
        re, im = inner[0][j]
        for b in range(1, 4):
            cosine = jnp.float32(0.0)
            sine = jnp.float32(0.0)
            for r in range(4):
                angle = -2.0 * math.pi * b * (4 * r + j) / chan
                cosine = jnp.where(row == r, math.cos(angle), cosine)
                sine = jnp.where(row == r, math.sin(angle), sine)
            yr, yi = inner[b][j]
            re = re + (yr * cosine - yi * sine)
            im = im + (yr * sine + yi * cosine)
        both = (jnp.concatenate([re, im], axis=0) * scale).astype(jnp.bfloat16)
        cross_ref[...] = lax.dot_general(
            both, both, (((1,), (1,)), ((), ())), preferred_element_type=jnp.float32
        )
        own_real = cross_ref[pl.ds(pl.multiple_of(block, own), own)]
        own_imag = cross_ref[pl.ds(pl.multiple_of(stations + block, own), own)]
        vis_ref[j, 0] = (own_real[:, :stations] + own_imag[:, stations:]) * (1.0 / SPEC)
        vis_ref[j, 1] = (own_imag[:, :stations] - own_real[:, stations:]) * (1.0 / SPEC)
    for copy in stores:
        copy.wait()


def call_beams(axes, pieces, matrix, bands, sums):
    params = pltpu.CompilerParams(vmem_limit_bytes=VMEM_LIMIT)
    vmem = pl.BlockSpec(memory_space=pltpu.VMEM)
    chan, frames = bands.shape[0], pieces[0].shape[2]
    stations, beams = pieces[0].shape[1] // 2, matrix.shape[1] // 2
    anywhere = pl.BlockSpec(memory_space=pl.ANY)
    slots = frames // 128 * 2
    series, visibilities = pl.pallas_call(
        lambda *refs: beam_kernel(axes, refs[: len(pieces)], *refs[len(pieces) :]),
        out_shape=(
            jax.ShapeDtypeStruct((2 * beams, 2, 8, frames), jnp.float32),
            jax.ShapeDtypeStruct((4, 2, stations // 4, stations), jnp.float32),
        ),
        in_specs=[vmem] * (len(pieces) + 3),
        out_specs=(anywhere, vmem),
        scratch_shapes=[
            pltpu.VMEM((chan * 2 * stations, frames), jnp.bfloat16),
            pltpu.VMEM((2 * stations, 2 * stations), jnp.float32),
            pltpu.VMEM((chan, 2 * beams, frames), jnp.bfloat16),
            pltpu.VMEM((slots, 2 * beams * 8, 128), jnp.float32),
            pltpu.SemaphoreType.DMA((slots,)),
        ],
        compiler_params=params,
        name="beams_and_series",
    )(*pieces, matrix, bands, sums)
    return visibilities, series


def swap(x, axis, mask):
    size = lax.axis_size(axis)
    return lax.ppermute(x, axis, [(i, i ^ mask) for i in range(size)])


def fast_body(
    samples, analysis_taps, synthesis_taps, antenna_station, station_group, beam_group, beam_weights
):
    axes = ("row", "col", "sub")
    params = pltpu.CompilerParams(vmem_limit_bytes=VMEM_LIMIT)
    vmem = pl.BlockSpec(memory_space=pltpu.VMEM)
    smem = pl.BlockSpec(memory_space=pltpu.SMEM)
    hbm = pl.BlockSpec(memory_space=pltpu.HBM)
    local, _, chan, frames = samples.shape
    stations = station_group.shape[0]
    antennas = antenna_station.shape[0]

    held_chan = beam_weights.shape[0]
    beams = beam_weights.shape[2] // 4
    block = jax.ShapeDtypeStruct((4, 2 * local, frames), jnp.bfloat16)
    half = jax.ShapeDtypeStruct((2, 2 * local, frames), jnp.bfloat16)
    kept, crossing_a, crossing_b, paired, far_a, far_b = pl.pallas_call(
        functools.partial(spread_kernel, axes),
        out_shape=[block, half, half, block, half, half],
        in_specs=[vmem],
        out_specs=[vmem] * 6,
        compiler_params=params,
        name="lane_spread",
    )(samples)
    members, taps = pl.pallas_call(
        functools.partial(table_kernel, axes),
        out_shape=[
            jax.ShapeDtypeStruct((2 * stations, 8 * local), jnp.bfloat16),
            jax.ShapeDtypeStruct((analysis_taps.shape[0], frames), jnp.float32),
        ],
        in_specs=[vmem] * 2,
        out_specs=[vmem] * 2,
        compiler_params=params,
        cost_estimate=pl.CostEstimate(flops=0, bytes_accessed=16 << 20, transcendentals=0),
        name="station_tables",
    )(antenna_station.reshape(1, antennas), analysis_taps)
    far_a = swap(far_a, "sub", 1)
    crossing_a = swap(crossing_a, "col", 1)
    far_a = swap(far_a, "col", 1)
    far_b = swap(far_b, "sub", 1)
    paired = swap(paired, "sub", 1)
    crossing_b = swap(crossing_b, "col", 1)
    far_b = swap(far_b, "col", 1)

    lane = jax.ShapeDtypeStruct((2 * stations, frames), jnp.bfloat16)
    sums2, sums3 = pl.pallas_call(
        functools.partial(sum_kernel, 0),
        out_shape=[lane] * 2,
        in_specs=[vmem] * 5,
        out_specs=[vmem] * 2,
        compiler_params=params,
        name="plane_sums_far",
    )(members, kept, paired, crossing_a, far_a)
    sums3, sums2 = swap(sums3, "row", 3), swap(sums2, "row", 2)
    sums0, sums1 = pl.pallas_call(
        functools.partial(sum_kernel, 2),
        out_shape=[jax.ShapeDtypeStruct(lane.shape, jnp.float32), lane],
        in_specs=[vmem] * 5,
        out_specs=[vmem] * 2,
        compiler_params=params,
        name="plane_sums_near",
    )(members, kept, paired, crossing_b, far_b)

    share = jax.ShapeDtypeStruct((stations, 2 * held_chan * beams), jnp.bfloat16)
    shares = pl.pallas_call(
        functools.partial(pack_kernel, axes),
        out_shape=[share] * 4,
        in_specs=[vmem],
        out_specs=[vmem] * 4,
        compiler_params=params,
        cost_estimate=pl.CostEstimate(flops=0, bytes_accessed=8 << 20, transcendentals=0),
        name="weight_shares",
    )(beam_weights.transpose(0, 1, 3, 2))

    lane_share = jax.ShapeDtypeStruct((3 * stations, frames), jnp.bfloat16)
    filtered, *sent = pl.pallas_call(
        filter_kernel,
        out_shape=[lane] + [lane_share] * 3,
        in_specs=[vmem] * 8,
        out_specs=[vmem] * 4,
        compiler_params=params,
        name="station_filter",
    )(taps, sums0, swap(sums1, "row", 1), sums2, sums3, *shares[1:])
    moved = [swap(x, "row", m) for x, m in zip(sent, (1, 2, 3))]

    tile = 256
    table = jax.ShapeDtypeStruct((stations, beams), jnp.float32)
    moved[0], *small = lax.optimization_barrier(
        (moved[0], station_group, beam_group, synthesis_taps)
    )
    bands, chosen, scale = pl.pallas_call(
        functools.partial(band_kernel, axes),
        out_shape=[
            jax.ShapeDtypeStruct((chan, 2 * (tile + HALO), tile), jnp.bfloat16),
            table,
            table,
        ],
        in_specs=[vmem, vmem, smem],
        out_specs=[vmem] * 3,
        compiler_params=params,
        cost_estimate=pl.CostEstimate(flops=0, bytes_accessed=16 << 20, transcendentals=0),
        name="synthesis_bands",
    )(
        small[0].reshape(1, stations),
        small[1].reshape(1, beam_group.shape[0]),
        small[2],
    )
    *moved[1:], bands, chosen, scale = lax.optimization_barrier((*moved[1:], bands, chosen, scale))
    matrix = pl.pallas_call(
        functools.partial(weight_kernel, axes),
        out_shape=jax.ShapeDtypeStruct((chan, 2 * beams, 2 * chan * stations), jnp.bfloat16),
        in_specs=[vmem] * 6,
        out_specs=vmem,
        scratch_shapes=[pltpu.VMEM((4,) + share.shape, jnp.bfloat16)],
        compiler_params=params,
        cost_estimate=pl.CostEstimate(flops=0, bytes_accessed=8 << 20, transcendentals=0),
        name="weight_matrix",
    )(chosen, scale, shares[0], *moved)

    def add_part(flips, xs, before, name):
        return pl.pallas_call(
            functools.partial(part_kernel, axes, flips),
            out_shape=jax.ShapeDtypeStruct((chan, 2 * beams, frames), jnp.float32),
            in_specs=[vmem] * (1 + len(xs) + len(before)),
            out_specs=vmem,
            scratch_shapes=[pltpu.VMEM((chan * 2 * stations, frames), jnp.bfloat16)],
            compiler_params=params,
            cost_estimate=pl.CostEstimate(flops=0, bytes_accessed=8 << 20, transcendentals=0),
            name=name,
        )(matrix, *xs, *before)

    held = jnp.stack([filtered] + [x[: 2 * stations] for x in moved])
    other = swap(held, "col", 1)
    paired = swap(held, "sub", 1)
    sums = add_part(FLIPS[:1], [held], [], "own_beams")
    other, sums = lax.optimization_barrier((other, sums))
    last = swap(other, "sub", 1)
    sums = add_part(FLIPS[1:3], [paired, other], [sums], "near_beams")
    pieces = [held, paired, other, last]

    visibilities, series = call_beams(axes, pieces, matrix, bands, sums)
    return visibilities, series.reshape(beams, 2, chan, frames)


def polyphase(signal, coefficients):
    length = signal.shape[-1]
    output = coefficients[0][:, None] * signal
    for tap_index in range(1, coefficients.shape[0]):
        shifted = jnp.pad(
            signal[..., : length - tap_index], [(0, 0)] * (signal.ndim - 1) + [(tap_index, 0)]
        )
        output = output + coefficients[tap_index][:, None] * shifted
    return output


def fourier_table(length, direction):
    indices = jnp.arange(length)
    angles = (
        2.0 * math.pi / length * (indices[:, None] * indices[None, :] % length).astype(jnp.float32)
    )
    cosine_part = jnp.cos(angles)
    sine_part = jnp.sin(angles)
    table = jnp.stack(
        [
            jnp.stack([cosine_part, direction * sine_part]),
            jnp.stack([-direction * sine_part, cosine_part]),
        ]
    )
    return table.transpose(0, 2, 1, 3) * (1.0 / math.sqrt(length))


def general_body(
    samples, analysis_taps, synthesis_taps, antenna_station, station_group, beam_group, beam_weights
):
    high = lax.Precision.HIGHEST
    block_count = lax.axis_size(("col", "sub"))
    block_index = lax.axis_index(("col", "sub"))
    filtered = polyphase(samples.astype(jnp.float32), analysis_taps)
    spectra = jnp.einsum(
        "aqcf,qcpk->apkf", filtered, fourier_table(samples.shape[2], -1.0), precision=high
    ).astype(jnp.bfloat16)
    turned = lax.all_to_all(spectra, "row", split_axis=2, concat_axis=0, tiled=True)
    local_count = spectra.shape[0]
    held_rows = turned.shape[0]
    chan_rows = turned.shape[2]
    spec_len = turned.shape[3]
    station_count = station_group.shape[0]
    flat_width = 2 * chan_rows * spec_len
    tile_rows = station_count // block_count
    shard_rows = lax.all_gather(turned, ("col", "sub"), axis=0, tiled=True)
    row_total = shard_rows.shape[0]
    positions = jnp.arange(row_total, dtype=jnp.int32)
    source_block = positions // held_rows
    offset_rows = positions % held_rows
    source_row = offset_rows // local_count
    antenna = offset_rows % local_count
    global_index = (source_row * block_count + source_block) * local_count + antenna
    targets = antenna_station[global_index]
    wanted = jnp.arange(station_count, dtype=jnp.int32)
    one_hot = (targets[None, :] == wanted[:, None]).astype(jnp.bfloat16)
    summed_values = jnp.dot(
        one_hot, shard_rows.reshape(row_total, flat_width), preferred_element_type=jnp.float32
    )
    flat_stations = (summed_values * (1.0 / math.sqrt(ANTENNAS_PER_STN))).astype(jnp.bfloat16)
    station_list = flat_stations.reshape(station_count, 2, chan_rows, spec_len)
    real_part = station_list[:, 0]
    imag_part = station_list[:, 1]
    own_rows = lax.dynamic_slice_in_dim(station_list, block_index * tile_rows, tile_rows, 0)
    own_real = own_rows[:, 0]
    own_imag = own_rows[:, 1]
    vis_real = (
        jnp.einsum("icf,jcf->cij", own_real, real_part, preferred_element_type=jnp.float32)
        + jnp.einsum("icf,jcf->cij", own_imag, imag_part, preferred_element_type=jnp.float32)
    ) * (1.0 / SPEC)
    vis_imag = (
        jnp.einsum("icf,jcf->cij", own_imag, real_part, preferred_element_type=jnp.float32)
        - jnp.einsum("icf,jcf->cij", own_real, imag_part, preferred_element_type=jnp.float32)
    ) * (1.0 / SPEC)
    visibilities = jnp.stack([vis_real, vis_imag], axis=1)
    beam_block = beam_weights.shape[2]
    own_groups = lax.dynamic_slice_in_dim(beam_group, block_index * beam_block, beam_block, 0)
    members = station_group[:, 0][None, :] == own_groups[:, None]
    scaling = 1.0 / jnp.sqrt(jnp.sum(members.astype(jnp.float32), axis=1))
    weights = jnp.where(members[None, None], beam_weights, jnp.zeros((), jnp.bfloat16))
    weight_real = weights[:, 0]
    imaginary_weight = weights[:, 1]
    beam_real = jnp.einsum(
        "cbs,scf->bcf", weight_real, real_part, preferred_element_type=jnp.float32
    ) - jnp.einsum("cbs,scf->bcf", imaginary_weight, imag_part, preferred_element_type=jnp.float32)
    beam_imag = jnp.einsum(
        "cbs,scf->bcf", weight_real, imag_part, preferred_element_type=jnp.float32
    ) + jnp.einsum("cbs,scf->bcf", imaginary_weight, real_part, preferred_element_type=jnp.float32)
    beams = (jnp.stack([beam_real, beam_imag], axis=1) * scaling[:, None, None, None]).astype(
        jnp.bfloat16
    )
    returned = lax.all_to_all(beams, "row", split_axis=0, concat_axis=2, tiled=True)
    inverse = jnp.einsum(
        "bqkf,qkpc->bpcf",
        returned.astype(jnp.float32),
        fourier_table(returned.shape[2], 1.0),
        precision=high,
    )
    beam_series = polyphase(inverse, synthesis_taps)
    return (visibilities, beam_series)


def solution(mesh):
    sizes = dict(mesh.shape)

    def body(samples, *others):
        chan = samples.shape[2]
        fits = (sizes["row"], sizes["col"], sizes["sub"], chan) == (4, 2, 2, 16)
        return (fast_body if fits else general_body)(samples, *others)

    return jax.shard_map(
        body,
        mesh=mesh,
        in_specs=(
            P(("grp", "row", "col", "sub"), None, None, None),
            P(),
            P(),
            P("grp"),
            P("grp", None),
            P("grp"),
            P(("grp", "row"), None, ("col", "sub"), None),
        ),
        out_specs=(
            P("row", None, ("grp", "col", "sub"), None),
            P(("grp", "col", "sub", "row"), None, None, None),
        ),
        check_vma=False,
    )
```

```python
import functools
import math

import jax
import jax.numpy as jnp
from jax import lax
from jax.experimental import pallas as pl
from jax.experimental.pallas import tpu as pltpu
from jax.sharding import PartitionSpec as P

ANTENNAS_PER_STN = 8
SPEC = 512
VMEM_LIMIT = 24 * 1024 * 1024
HALO = 128
FLIPS = ((0, 0), (0, 1), (1, 0), (1, 1))
NEAR, FAR = (0, 1), (2, 3)
PLACES = (
    (FLIPS[0], NEAR + FAR),
    (FLIPS[1], NEAR + FAR),
    (FLIPS[2], NEAR),
    (FLIPS[2], FAR),
    (FLIPS[3], NEAR),
    (FLIPS[3], FAR),
)


def fourier(parts, sign):
    count = len(parts)
    if count == 1:
        return parts
    even, odd = fourier(parts[0::2], sign), fourier(parts[1::2], sign)
    low, top = [], []
    for k in range(count // 2):
        er, ei = even[k]
        re, im = odd[k]
        if k == 0:
            tr, ti = re, im
        elif 4 * k == count:
            tr, ti = (-sign * im, sign * re)
        else:
            c, s = math.cos(2 * math.pi * k / count), sign * math.sin(2 * math.pi * k / count)
            tr, ti = re * c - im * s, re * s + im * c
        low.append((er + tr, ei + ti))
        top.append((er - tr, ei - ti))
    return low + top


def lane_of(row, col, sub):
    return sub * 8 + col * 4 + row


def spread_kernel(axes, x_ref, *out_refs):
    row, col, sub = (lax.axis_index(a) for a in axes)
    antennas, parts, chan, frames = x_ref.shape
    count = antennas * parts * chan
    shape = (count, count)
    place = lax.broadcasted_iota(jnp.int32, (count, 1), 0)
    antenna = place % antennas
    part = place // antennas % parts
    piece = place // (antennas * parts)
    lane = lane_of(row ^ (piece % 4) ^ 2, col ^ (piece // 4 % 2), sub ^ (piece // 8))
    source = (antenna * parts + part) * chan + lane
    order = jnp.where(lax.broadcasted_iota(jnp.int32, shape, 1) == source, 1.0, 0.0)
    moved = jnp.dot(
        order.astype(jnp.bfloat16),
        x_ref[...].reshape(count, frames),
        preferred_element_type=jnp.float32,
    ).astype(jnp.bfloat16)
    start = 0
    for ref in out_refs:
        size = ref.shape[0] * ref.shape[1]
        ref[...] = moved[start : start + size].reshape(ref.shape)
        start += size


def member_matrix(axes, names_ref, stations, local):
    row, col, sub = (lax.axis_index(a) for a in axes)
    antennas = names_ref.shape[1]
    every = jnp.broadcast_to(names_ref[...], (8, antennas))
    names = []
    for k in range(4):
        owner = (row * 2 + (col ^ (k // 2))) * 2 + (sub ^ (k % 2))
        names += [pltpu.roll(every, lax.rem(antennas - owner * local, antennas), 1)[:1, :local]] * 2
    names = jnp.concatenate(names, axis=1)
    shape = (2 * stations, 8 * local)
    place = lax.broadcasted_iota(jnp.int32, shape, 0)
    column = lax.broadcasted_iota(jnp.int32, shape, 1)
    same = (place % stations == names) & (place // stations == column // local % 2)
    return jnp.where(same, 1.0, 0.0).astype(jnp.bfloat16)


def table_kernel(axes, names_ref, taps_ref, members_ref, own_taps_ref):
    stations, local = members_ref.shape[0] // 2, members_ref.shape[1] // 8
    members_ref[...] = member_matrix(axes, names_ref, stations, local)
    taps = taps_ref[...]
    lane = lane_of(*(lax.axis_index(a) for a in axes))
    mine = lax.broadcasted_iota(jnp.int32, taps.shape, 1) == lane
    own = jnp.sum(jnp.where(mine, taps, 0.0), axis=1, keepdims=True)
    own_taps_ref[...] = jnp.broadcast_to(own, own_taps_ref.shape)


def sum_kernel(first, members_ref, *refs):
    x_refs, out_refs = refs[:4], refs[4:]
    for k, ref in enumerate(out_refs):
        rows = jnp.concatenate([x[first + k if x.shape[0] == 4 else k] for x in x_refs], axis=0)
        ref[...] = jnp.dot(
            members_ref[...], rows, preferred_element_type=jnp.float32
        ).astype(ref.dtype)


def filter_kernel(taps_ref, *refs):
    x_refs, share_refs, out_refs = refs[:4], refs[4:7], refs[7:]
    rows = out_refs[0].shape[0]
    total = x_refs[0][...]
    for ref in x_refs[1:]:
        total = total + ref[...].astype(jnp.float32)
    place = lax.broadcasted_iota(jnp.int32, total.shape, 1)
    result = total * taps_ref[0:1]
    for tap in range(1, taps_ref.shape[0]):
        moved = jnp.where(place >= tap, pltpu.roll(total, tap, 1), 0.0)
        result = result + moved * taps_ref[tap : tap + 1]
    result = result.astype(out_refs[0].dtype)
    out_refs[0][...] = result
    for ref, share in zip(out_refs[1:], share_refs):
        ref[:rows] = result
        ref[rows:] = share[...]


def pack_kernel(axes, w_ref, *out_refs):
    row = lax.axis_index(axes[0])
    chan, _, _, width = w_ref.shape
    beams = width // 4
    for k in range(chan):
        for q in range(2):
            place = (2 * k + q) * beams
            parts = [w_ref[k, q, :, j * beams : (j + 1) * beams] for j in range(4)]
            for mask, ref in enumerate(out_refs):
                taken = parts[0]
                for j in range(1, 4):
                    taken = jnp.where((row ^ mask) == j, parts[j], taken)
                ref[:, place : place + beams] = taken


def bands(taps_ref, lane, rows, cols):
    wide = 2 * cols
    places = lax.broadcasted_iota(jnp.int32, (8, wide), 1)
    base = jnp.zeros((8, wide), jnp.float32)
    for tap in range(taps_ref.shape[0]):
        base = jnp.where(places == (tap - HALO) % wide, taps_ref[tap, lane], base)
    whole = jnp.broadcast_to(base[0:1], (rows, wide))
    whole = pltpu.roll(whole, 0, 1, stride=1, stride_axis=0)[:, :cols]
    high = whole.astype(jnp.bfloat16)
    low = (whole - high.astype(jnp.float32)).astype(jnp.bfloat16)
    return jnp.concatenate([high[:HALO], low[:HALO], high[HALO:], low[HALO:]], axis=0)


def band_kernel(axes, groups_ref, beam_ref, taps_ref, t_ref, chosen_ref, scale_ref):
    row, col, sub = (lax.axis_index(a) for a in axes)
    stations, beams = chosen_ref.shape
    chan = t_ref.shape[0]
    square = (stations, stations)
    diagonal = lax.broadcasted_iota(jnp.int32, square, 0) == lax.broadcasted_iota(
        jnp.int32, square, 1
    )
    groups = jnp.broadcast_to(groups_ref[...], square).astype(jnp.float32)
    groups = jnp.sum(jnp.where(diagonal, groups, 0.0), axis=1, keepdims=True)
    total = beam_ref.shape[1]
    first = ((col * 2 + sub) * 4 + row) * beams
    every = jnp.broadcast_to(beam_ref[...], (8, total))
    wanted = pltpu.roll(every, lax.rem(total - first, total), 1)[:1, :beams]
    chosen = (groups == wanted.astype(jnp.float32)).astype(jnp.float32)
    chosen_ref[...] = chosen
    scale = (1.0 / (chan * math.sqrt(ANTENNAS_PER_STN))) / jnp.sqrt(
        jnp.sum(chosen, axis=0, keepdims=True)
    )
    scale_ref[...] = jnp.broadcast_to(scale, scale_ref.shape)
    for c in range(chan):
        t_ref[c] = bands(taps_ref, c, t_ref.shape[1] // 2, t_ref.shape[2])


def weight_kernel(axes, chosen_ref, scale_ref, *refs):
    row = lax.axis_index(axes[0])
    w_refs, (m_ref, all_ref) = refs[:4], refs[4:]
    stations, beams = chosen_ref.shape
    held = all_ref.shape[2] // (2 * beams)
    chan = 4 * held
    for mask, ref in enumerate(w_refs):
        all_ref[row ^ mask] = ref[ref.shape[0] - stations :]
    members = chosen_ref[...] > 0
    scale = scale_ref[...]
    zero = jnp.zeros((), jnp.float32)
    parts = []
    for k in range(chan):
        whole = all_ref[k // held].astype(jnp.float32)
        places = [(2 * (k % held) + q) * beams for q in range(2)]
        parts.append(tuple(jnp.where(members, whole[:, p : p + beams], zero) for p in places))
    parts = fourier(parts, -1.0)
    real = [p[0] * scale for p in parts]
    imag = [p[1] * scale for p in parts]
    upper = jnp.concatenate([v for k in range(chan) for v in (real[k], -imag[k])], axis=0)
    lower = jnp.concatenate([v for k in range(chan) for v in (imag[k], real[k])], axis=0)
    whole = jnp.concatenate([upper, lower], axis=1).T.astype(m_ref.dtype)
    count = 2 * beams
    place = lax.broadcasted_iota(jnp.int32, (count, 1), 0)
    source = place % 2 * beams + place // 2
    order = jnp.where(lax.broadcasted_iota(jnp.int32, (count, count), 1) == source, 1.0, 0.0)
    whole = jnp.dot(order.astype(m_ref.dtype), whole, preferred_element_type=jnp.float32)
    whole = whole.astype(m_ref.dtype)
    width = whole.shape[1]
    step = 2 * stations
    odd = jnp.concatenate([whole[:, width - step :], whole[:, : width - step]], axis=1)
    for c in range(chan):
        base = odd if c % 2 else whole
        start = c // 2 * 2 * step
        m_ref[c, :, start:] = base[:, : width - start]
        if start:
            m_ref[c, :, :start] = base[:, width - start :]


def gather_lanes(axes, x_refs, places, lanes_ref):
    row, col, sub = (lax.axis_index(a) for a in axes)
    rows = x_refs[0].shape[1]
    for ((dc, ds), masks), ref in zip(places, x_refs):
        for k, m in enumerate(masks):
            lane = lane_of(row ^ m, col ^ dc, sub ^ ds)
            lanes_ref[pl.ds(pl.multiple_of(lane * rows, rows), rows)] = ref[k]


def lane_products(axes, flips, m_ref, lanes_ref, first, count):
    col, sub = (lax.axis_index(a) for a in axes[1:])
    width = 4 * lanes_ref.shape[0] // 16
    total = None
    for dc, ds in flips:
        start = pl.multiple_of((2 * (sub ^ ds) + (col ^ dc)) * width, width)
        some = m_ref[first : first + count, :, pl.ds(start, width)]
        some = some.reshape(count * m_ref.shape[1], width)
        found = jnp.dot(some, lanes_ref[pl.ds(start, width)], preferred_element_type=jnp.float32)
        total = found if total is None else total + found
    return total


def part_kernel(axes, places, m_ref, *refs):
    x_refs, (sum_ref, lanes_ref) = refs[: len(places)], refs[-2:]
    before = refs[len(places) : -2]
    gather_lanes(axes, x_refs, places, lanes_ref)
    flips = sorted({flip for flip, _ in places})
    for first in range(0, m_ref.shape[0], 4):
        found = lane_products(axes, flips, m_ref, lanes_ref, first, 4)
        found = found.reshape((4,) + sum_ref.shape[1:])
        for ref in before:
            found = found + ref[first : first + 4]
        sum_ref[first : first + 4] = found


def beam_kernel(
    axes,
    x_refs,
    m_ref,
    t_ref,
    sum_ref,
    series_ref,
    vis_ref,
    lanes_ref,
    cross_ref,
    inverse_ref,
    out_ref,
    store_sems,
):
    row, col, sub = (lax.axis_index(a) for a in axes)
    rows = x_refs[0].shape[1]
    stations = rows // 2
    chan = 4 * 4
    frames = lanes_ref.shape[1]

    gather_lanes(axes, x_refs[4:], PLACES[4:], lanes_ref)
    beams = m_ref.shape[1] // 2
    tile = t_ref.shape[2]
    stores = []
    for first in range(0, 16, 4):
        found = lane_products(axes, FLIPS[3:], m_ref, lanes_ref, first, 4)
        found = found.reshape((4,) + sum_ref.shape[1:]) + sum_ref[first : first + 4]
        inverse_ref[first : first + 4] = found.astype(jnp.bfloat16)
    for lane in range(chan):
        for n in range(frames // tile):
            taken = [inverse_ref[lane, :, n * tile : (n + 1) * tile]] * 2
            first = 2 * HALO
            if n > 0:
                taken = [inverse_ref[lane, :, n * tile - HALO : n * tile]] * 2 + taken
                first = 0
            value = jnp.dot(
                jnp.concatenate(taken, axis=1), t_ref[lane, first:], preferred_element_type=jnp.float32
            )
            for part in range(tile // 128):
                slot = n * (tile // 128) + part
                out_ref[lane, slot] = value[:, part * 128 : (part + 1) * 128]
                stores.append(
                    pltpu.make_async_copy(
                        out_ref.at[lane, slot],
                        series_ref.at[:, lane // 8, lane % 8, pl.ds(slot * 128, 128)],
                        store_sems.at[lane, slot],
                    )
                )
                stores[-1].start()
    gather_lanes(axes, x_refs[:4], PLACES[:4], lanes_ref)
    inner = []
    for b in range(4):
        parts = []
        for a in range(4):
            start = (4 * a + b) * rows
            parts.append(
                tuple(
                    lanes_ref[start + q * stations : start + (q + 1) * stations].astype(
                        jnp.float32
                    )
                    for q in range(2)
                )
            )
        inner.append(fourier(parts, -1.0))
    scale = 1.0 / math.sqrt(chan * ANTENNAS_PER_STN)
    block = (col * 2 + sub) * vis_ref.shape[2]
    own = vis_ref.shape[2]
    for j in range(4):
        re, im = inner[0][j]
        for b in range(1, 4):
            cosine = jnp.float32(0.0)
            sine = jnp.float32(0.0)
            for r in range(4):
                angle = -2.0 * math.pi * b * (4 * r + j) / chan
                cosine = jnp.where(row == r, math.cos(angle), cosine)
                sine = jnp.where(row == r, math.sin(angle), sine)
            yr, yi = inner[b][j]
            re = re + (yr * cosine - yi * sine)
            im = im + (yr * sine + yi * cosine)
        both = (jnp.concatenate([re, im], axis=0) * scale).astype(jnp.bfloat16)
        cross_ref[...] = lax.dot_general(
            both, both, (((1,), (1,)), ((), ())), preferred_element_type=jnp.float32
        )
        own_real = cross_ref[pl.ds(pl.multiple_of(block, own), own)]
        own_imag = cross_ref[pl.ds(pl.multiple_of(stations + block, own), own)]
        vis_ref[j, 0] = (own_real[:, :stations] + own_imag[:, stations:]) * (1.0 / SPEC)
        vis_ref[j, 1] = (own_imag[:, :stations] - own_real[:, stations:]) * (1.0 / SPEC)
    for copy in stores:
        copy.wait()


def call_beams(axes, pieces, matrix, bands, sums):
    params = pltpu.CompilerParams(vmem_limit_bytes=VMEM_LIMIT)
    vmem = pl.BlockSpec(memory_space=pltpu.VMEM)
    chan, frames = bands.shape[0], pieces[0].shape[2]
    stations, beams = pieces[0].shape[1] // 2, matrix.shape[1] // 2
    anywhere = pl.BlockSpec(memory_space=pl.ANY)
    series, visibilities = pl.pallas_call(
        lambda *refs: beam_kernel(axes, refs[: len(pieces)], *refs[len(pieces) :]),
        out_shape=(
            jax.ShapeDtypeStruct((2 * beams, 2, 8, frames), jnp.float32),
            jax.ShapeDtypeStruct((4, 2, stations // 4, stations), jnp.float32),
        ),
        in_specs=[vmem] * (len(pieces) + 3),
        out_specs=(anywhere, vmem),
        scratch_shapes=[
            pltpu.VMEM((chan * 2 * stations, frames), jnp.bfloat16),
            pltpu.VMEM((2 * stations, 2 * stations), jnp.float32),
            pltpu.VMEM((chan, 2 * beams, frames), jnp.bfloat16),
            pltpu.VMEM((chan, frames // 128, 2 * beams, 128), jnp.float32),
            pltpu.SemaphoreType.DMA((chan, frames // 128)),
        ],
        compiler_params=params,
        name="beams_and_series",
    )(*pieces, matrix, bands, sums)
    return visibilities, series


def swap(x, axis, mask):
    size = lax.axis_size(axis)
    return lax.ppermute(x, axis, [(i, i ^ mask) for i in range(size)])


def fast_body(
    samples, analysis_taps, synthesis_taps, antenna_station, station_group, beam_group, beam_weights
):
    axes = ("row", "col", "sub")
    params = pltpu.CompilerParams(vmem_limit_bytes=VMEM_LIMIT)
    vmem = pl.BlockSpec(memory_space=pltpu.VMEM)
    smem = pl.BlockSpec(memory_space=pltpu.SMEM)
    hbm = pl.BlockSpec(memory_space=pltpu.HBM)
    local, _, chan, frames = samples.shape
    stations = station_group.shape[0]
    antennas = antenna_station.shape[0]

    held_chan = beam_weights.shape[0]
    beams = beam_weights.shape[2] // 4
    block = jax.ShapeDtypeStruct((4, 2 * local, frames), jnp.bfloat16)
    half = jax.ShapeDtypeStruct((2, 2 * local, frames), jnp.bfloat16)
    kept, crossing_a, crossing_b, paired, far_a, far_b = pl.pallas_call(
        functools.partial(spread_kernel, axes),
        out_shape=[block, half, half, block, half, half],
        in_specs=[vmem],
        out_specs=[vmem] * 6,
        compiler_params=params,
        name="lane_spread",
    )(samples)
    members, taps = pl.pallas_call(
        functools.partial(table_kernel, axes),
        out_shape=[
            jax.ShapeDtypeStruct((2 * stations, 8 * local), jnp.bfloat16),
            jax.ShapeDtypeStruct((analysis_taps.shape[0], frames), jnp.float32),
        ],
        in_specs=[vmem] * 2,
        out_specs=[vmem] * 2,
        compiler_params=params,
        cost_estimate=pl.CostEstimate(flops=0, bytes_accessed=16 << 20, transcendentals=0),
        name="station_tables",
    )(antenna_station.reshape(1, antennas), analysis_taps)
    far_a = swap(far_a, "sub", 1)
    crossing_a = swap(crossing_a, "col", 1)
    far_a = swap(far_a, "col", 1)
    far_b = swap(far_b, "sub", 1)
    paired = swap(paired, "sub", 1)
    crossing_b = swap(crossing_b, "col", 1)
    far_b = swap(far_b, "col", 1)

    lane = jax.ShapeDtypeStruct((2 * stations, frames), jnp.bfloat16)
    sums2, sums3 = pl.pallas_call(
        functools.partial(sum_kernel, 0),
        out_shape=[lane] * 2,
        in_specs=[vmem] * 5,
        out_specs=[vmem] * 2,
        compiler_params=params,
        name="plane_sums_far",
    )(members, kept, paired, crossing_a, far_a)
    sums3, sums2 = swap(sums3, "row", 3), swap(sums2, "row", 2)
    sums0, sums1 = pl.pallas_call(
        functools.partial(sum_kernel, 2),
        out_shape=[jax.ShapeDtypeStruct(lane.shape, jnp.float32), lane],
        in_specs=[vmem] * 5,
        out_specs=[vmem] * 2,
        compiler_params=params,
        name="plane_sums_near",
    )(members, kept, paired, crossing_b, far_b)

    share = jax.ShapeDtypeStruct((stations, 2 * held_chan * beams), jnp.bfloat16)
    shares = pl.pallas_call(
        functools.partial(pack_kernel, axes),
        out_shape=[share] * 4,
        in_specs=[vmem],
        out_specs=[vmem] * 4,
        compiler_params=params,
        cost_estimate=pl.CostEstimate(flops=0, bytes_accessed=8 << 20, transcendentals=0),
        name="weight_shares",
    )(beam_weights.transpose(0, 1, 3, 2))

    lane_share = jax.ShapeDtypeStruct((3 * stations, frames), jnp.bfloat16)
    filtered, *sent = pl.pallas_call(
        filter_kernel,
        out_shape=[lane] + [lane_share] * 3,
        in_specs=[vmem] * 8,
        out_specs=[vmem] * 4,
        compiler_params=params,
        name="station_filter",
    )(taps, sums0, swap(sums1, "row", 1), sums2, sums3, *shares[1:])
    moved = [swap(x, "row", m) for x, m in zip(sent, (1, 2, 3))]

    tile = 256
    table = jax.ShapeDtypeStruct((stations, beams), jnp.float32)
    other = [swap(filtered, "col", 1)]
    moved[0], *small = lax.optimization_barrier(
        (moved[0], station_group, beam_group, synthesis_taps)
    )
    other.append(swap(moved[0][: 2 * stations], "col", 1))
    bands, chosen, scale = pl.pallas_call(
        functools.partial(band_kernel, axes),
        out_shape=[
            jax.ShapeDtypeStruct((chan, 2 * (tile + HALO), tile), jnp.bfloat16),
            table,
            table,
        ],
        in_specs=[vmem, vmem, smem],
        out_specs=[vmem] * 3,
        compiler_params=params,
        cost_estimate=pl.CostEstimate(flops=0, bytes_accessed=16 << 20, transcendentals=0),
        name="synthesis_bands",
    )(
        small[0].reshape(1, stations),
        small[1].reshape(1, beam_group.shape[0]),
        small[2],
    )
    moved[1], moved[2], other[0], other[1], bands, chosen, scale = lax.optimization_barrier(
        (*moved[1:], *other, bands, chosen, scale)
    )
    matrix = pl.pallas_call(
        functools.partial(weight_kernel, axes),
        out_shape=jax.ShapeDtypeStruct((chan, 2 * beams, 2 * chan * stations), jnp.bfloat16),
        in_specs=[vmem] * 6,
        out_specs=vmem,
        scratch_shapes=[pltpu.VMEM((4,) + share.shape, jnp.bfloat16)],
        compiler_params=params,
        cost_estimate=pl.CostEstimate(flops=0, bytes_accessed=8 << 20, transcendentals=0),
        name="weight_matrix",
    )(chosen, scale, shares[0], *moved)

    def add_part(places, xs, before, name):
        return pl.pallas_call(
            functools.partial(part_kernel, axes, places),
            out_shape=jax.ShapeDtypeStruct((chan, 2 * beams, frames), jnp.float32),
            in_specs=[vmem] * (1 + len(xs) + len(before)),
            out_specs=vmem,
            scratch_shapes=[pltpu.VMEM((chan * 2 * stations, frames), jnp.bfloat16)],
            compiler_params=params,
            cost_estimate=pl.CostEstimate(flops=0, bytes_accessed=8 << 20, transcendentals=0),
            name=name,
        )(matrix, *xs, *before)

    distant = [x[: 2 * stations] for x in moved[1:]]
    held = jnp.stack([filtered, moved[0][: 2 * stations], *distant])
    near = jnp.stack(other)
    far = swap(jnp.stack(distant), "col", 1)
    paired, last_near = swap(held, "sub", 1), swap(near, "sub", 1)
    sums = add_part(PLACES[:1], [held], [], "own_beams")
    far, sums = lax.optimization_barrier((far, sums))
    last_far = swap(far, "sub", 1)
    sums = add_part(PLACES[1:4], [paired, near, far], [sums], "near_beams")
    pieces = [held, paired, near, far, last_near, last_far]

    visibilities, series = call_beams(axes, pieces, matrix, bands, sums)
    return visibilities, series.reshape(beams, 2, chan, frames)


def polyphase(signal, coefficients):
    length = signal.shape[-1]
    output = coefficients[0][:, None] * signal
    for tap_index in range(1, coefficients.shape[0]):
        shifted = jnp.pad(
            signal[..., : length - tap_index], [(0, 0)] * (signal.ndim - 1) + [(tap_index, 0)]
        )
        output = output + coefficients[tap_index][:, None] * shifted
    return output


def fourier_table(length, direction):
    indices = jnp.arange(length)
    angles = (
        2.0 * math.pi / length * (indices[:, None] * indices[None, :] % length).astype(jnp.float32)
    )
    cosine_part = jnp.cos(angles)
    sine_part = jnp.sin(angles)
    table = jnp.stack(
        [
            jnp.stack([cosine_part, direction * sine_part]),
            jnp.stack([-direction * sine_part, cosine_part]),
        ]
    )
    return table.transpose(0, 2, 1, 3) * (1.0 / math.sqrt(length))


def general_body(
    samples, analysis_taps, synthesis_taps, antenna_station, station_group, beam_group, beam_weights
):
    high = lax.Precision.HIGHEST
    block_count = lax.axis_size(("col", "sub"))
    block_index = lax.axis_index(("col", "sub"))
    filtered = polyphase(samples.astype(jnp.float32), analysis_taps)
    spectra = jnp.einsum(
        "aqcf,qcpk->apkf", filtered, fourier_table(samples.shape[2], -1.0), precision=high
    ).astype(jnp.bfloat16)
    turned = lax.all_to_all(spectra, "row", split_axis=2, concat_axis=0, tiled=True)
    local_count = spectra.shape[0]
    held_rows = turned.shape[0]
    chan_rows = turned.shape[2]
    spec_len = turned.shape[3]
    station_count = station_group.shape[0]
    flat_width = 2 * chan_rows * spec_len
    tile_rows = station_count // block_count
    shard_rows = lax.all_gather(turned, ("col", "sub"), axis=0, tiled=True)
    row_total = shard_rows.shape[0]
    positions = jnp.arange(row_total, dtype=jnp.int32)
    source_block = positions // held_rows
    offset_rows = positions % held_rows
    source_row = offset_rows // local_count
    antenna = offset_rows % local_count
    global_index = (source_row * block_count + source_block) * local_count + antenna
    targets = antenna_station[global_index]
    wanted = jnp.arange(station_count, dtype=jnp.int32)
    one_hot = (targets[None, :] == wanted[:, None]).astype(jnp.bfloat16)
    summed_values = jnp.dot(
        one_hot, shard_rows.reshape(row_total, flat_width), preferred_element_type=jnp.float32
    )
    flat_stations = (summed_values * (1.0 / math.sqrt(ANTENNAS_PER_STN))).astype(jnp.bfloat16)
    station_list = flat_stations.reshape(station_count, 2, chan_rows, spec_len)
    real_part = station_list[:, 0]
    imag_part = station_list[:, 1]
    own_rows = lax.dynamic_slice_in_dim(station_list, block_index * tile_rows, tile_rows, 0)
    own_real = own_rows[:, 0]
    own_imag = own_rows[:, 1]
    vis_real = (
        jnp.einsum("icf,jcf->cij", own_real, real_part, preferred_element_type=jnp.float32)
        + jnp.einsum("icf,jcf->cij", own_imag, imag_part, preferred_element_type=jnp.float32)
    ) * (1.0 / SPEC)
    vis_imag = (
        jnp.einsum("icf,jcf->cij", own_imag, real_part, preferred_element_type=jnp.float32)
        - jnp.einsum("icf,jcf->cij", own_real, imag_part, preferred_element_type=jnp.float32)
    ) * (1.0 / SPEC)
    visibilities = jnp.stack([vis_real, vis_imag], axis=1)
    beam_block = beam_weights.shape[2]
    own_groups = lax.dynamic_slice_in_dim(beam_group, block_index * beam_block, beam_block, 0)
    members = station_group[:, 0][None, :] == own_groups[:, None]
    scaling = 1.0 / jnp.sqrt(jnp.sum(members.astype(jnp.float32), axis=1))
    weights = jnp.where(members[None, None], beam_weights, jnp.zeros((), jnp.bfloat16))
    weight_real = weights[:, 0]
    imaginary_weight = weights[:, 1]
    beam_real = jnp.einsum(
        "cbs,scf->bcf", weight_real, real_part, preferred_element_type=jnp.float32
    ) - jnp.einsum("cbs,scf->bcf", imaginary_weight, imag_part, preferred_element_type=jnp.float32)
    beam_imag = jnp.einsum(
        "cbs,scf->bcf", weight_real, imag_part, preferred_element_type=jnp.float32
    ) + jnp.einsum("cbs,scf->bcf", imaginary_weight, real_part, preferred_element_type=jnp.float32)
    beams = (jnp.stack([beam_real, beam_imag], axis=1) * scaling[:, None, None, None]).astype(
        jnp.bfloat16
    )
    returned = lax.all_to_all(beams, "row", split_axis=0, concat_axis=2, tiled=True)
    inverse = jnp.einsum(
        "bqkf,qkpc->bpcf",
        returned.astype(jnp.float32),
        fourier_table(returned.shape[2], 1.0),
        precision=high,
    )
    beam_series = polyphase(inverse, synthesis_taps)
    return (visibilities, beam_series)


def solution(mesh):
    sizes = dict(mesh.shape)

    def body(samples, *others):
        chan = samples.shape[2]
        fits = (sizes["row"], sizes["col"], sizes["sub"], chan) == (4, 2, 2, 16)
        return (fast_body if fits else general_body)(samples, *others)

    return jax.shard_map(
        body,
        mesh=mesh,
        in_specs=(
            P(("grp", "row", "col", "sub"), None, None, None),
            P(),
            P(),
            P("grp"),
            P("grp", None),
            P("grp"),
            P(("grp", "row"), None, ("col", "sub"), None),
        ),
        out_specs=(
            P("row", None, ("grp", "col", "sub"), None),
            P(("grp", "col", "sub", "row"), None, None, None),
        ),
        check_vma=False,
    )
```

```python
import functools
import math

import jax
import jax.numpy as jnp
from jax import lax
from jax.experimental import pallas as pl
from jax.experimental.pallas import tpu as pltpu
from jax.sharding import PartitionSpec as P

ANTENNAS_PER_STN = 8
SPEC = 512
VMEM_LIMIT = 24 * 1024 * 1024
HALO = 128
FLIPS = ((0, 0), (0, 1), (1, 0), (1, 1))
NEAR, FAR = (0, 1), (2, 3)
PLACES = (
    (FLIPS[0], NEAR + FAR),
    (FLIPS[1], NEAR + FAR),
    (FLIPS[2], NEAR),
    (FLIPS[2], FAR),
    (FLIPS[3], NEAR),
    (FLIPS[3], FAR),
)


def fourier(parts, sign):
    count = len(parts)
    if count == 1:
        return parts
    even, odd = fourier(parts[0::2], sign), fourier(parts[1::2], sign)
    low, top = [], []
    for k in range(count // 2):
        er, ei = even[k]
        re, im = odd[k]
        if k == 0:
            tr, ti = re, im
        elif 4 * k == count:
            tr, ti = (-sign * im, sign * re)
        else:
            c, s = math.cos(2 * math.pi * k / count), sign * math.sin(2 * math.pi * k / count)
            tr, ti = re * c - im * s, re * s + im * c
        low.append((er + tr, ei + ti))
        top.append((er - tr, ei - ti))
    return low + top


def lane_of(row, col, sub):
    return sub * 8 + col * 4 + row


def spread_kernel(axes, x_ref, *out_refs):
    row, col, sub = (lax.axis_index(a) for a in axes)
    antennas, parts, chan, frames = x_ref.shape
    count = antennas * parts * chan
    shape = (count, count)
    place = lax.broadcasted_iota(jnp.int32, (count, 1), 0)
    antenna = place % antennas
    part = place // antennas % parts
    piece = place // (antennas * parts)
    lane = lane_of(row ^ (piece % 4) ^ 2, col ^ (piece // 4 % 2), sub ^ (piece // 8))
    source = (antenna * parts + part) * chan + lane
    order = jnp.where(lax.broadcasted_iota(jnp.int32, shape, 1) == source, 1.0, 0.0)
    moved = jnp.dot(
        order.astype(jnp.bfloat16),
        x_ref[...].reshape(count, frames),
        preferred_element_type=jnp.float32,
    ).astype(jnp.bfloat16)
    start = 0
    for ref in out_refs:
        size = ref.shape[0] * ref.shape[1]
        ref[...] = moved[start : start + size].reshape(ref.shape)
        start += size


def member_matrix(axes, names_ref, stations, local):
    row, col, sub = (lax.axis_index(a) for a in axes)
    antennas = names_ref.shape[1]
    every = jnp.broadcast_to(names_ref[...], (8, antennas))
    names = []
    for k in range(4):
        owner = (row * 2 + (col ^ (k // 2))) * 2 + (sub ^ (k % 2))
        names += [pltpu.roll(every, lax.rem(antennas - owner * local, antennas), 1)[:1, :local]] * 2
    names = jnp.concatenate(names, axis=1)
    shape = (2 * stations, 8 * local)
    place = lax.broadcasted_iota(jnp.int32, shape, 0)
    column = lax.broadcasted_iota(jnp.int32, shape, 1)
    same = (place % stations == names) & (place // stations == column // local % 2)
    return jnp.where(same, 1.0, 0.0).astype(jnp.bfloat16)


def table_kernel(axes, names_ref, taps_ref, members_ref, own_taps_ref):
    stations, local = members_ref.shape[0] // 2, members_ref.shape[1] // 8
    members_ref[...] = member_matrix(axes, names_ref, stations, local)
    taps = taps_ref[...]
    lane = lane_of(*(lax.axis_index(a) for a in axes))
    mine = lax.broadcasted_iota(jnp.int32, taps.shape, 1) == lane
    own = jnp.sum(jnp.where(mine, taps, 0.0), axis=1, keepdims=True)
    own_taps_ref[...] = jnp.broadcast_to(own, own_taps_ref.shape)


def sum_kernel(first, members_ref, *refs):
    x_refs, out_refs = refs[:4], refs[4:]
    for k, ref in enumerate(out_refs):
        rows = jnp.concatenate([x[first + k if x.shape[0] == 4 else k] for x in x_refs], axis=0)
        ref[...] = jnp.dot(
            members_ref[...], rows, preferred_element_type=jnp.float32
        ).astype(ref.dtype)


def filter_kernel(taps_ref, *refs):
    x_refs, share_refs, out_refs = refs[:4], refs[4:7], refs[7:]
    rows = out_refs[0].shape[0]
    total = x_refs[0][...]
    for ref in x_refs[1:]:
        total = total + ref[...].astype(jnp.float32)
    place = lax.broadcasted_iota(jnp.int32, total.shape, 1)
    result = total * taps_ref[0:1]
    for tap in range(1, taps_ref.shape[0]):
        moved = jnp.where(place >= tap, pltpu.roll(total, tap, 1), 0.0)
        result = result + moved * taps_ref[tap : tap + 1]
    result = result.astype(out_refs[0].dtype)
    out_refs[0][...] = result
    for ref, share in zip(out_refs[1:], share_refs):
        ref[:rows] = result
        ref[rows:] = share[...]


def pack_kernel(axes, w_ref, *out_refs):
    row = lax.axis_index(axes[0])
    chan, _, _, width = w_ref.shape
    beams = width // 4
    for k in range(chan):
        for q in range(2):
            place = (2 * k + q) * beams
            parts = [w_ref[k, q, :, j * beams : (j + 1) * beams] for j in range(4)]
            for mask, ref in enumerate(out_refs):
                taken = parts[0]
                for j in range(1, 4):
                    taken = jnp.where((row ^ mask) == j, parts[j], taken)
                ref[:, place : place + beams] = taken


def bands(taps_ref, lane, rows, cols):
    wide = 2 * cols
    places = lax.broadcasted_iota(jnp.int32, (8, wide), 1)
    base = jnp.zeros((8, wide), jnp.float32)
    for tap in range(taps_ref.shape[0]):
        base = jnp.where(places == (tap - HALO) % wide, taps_ref[tap, lane], base)
    whole = jnp.broadcast_to(base[0:1], (rows, wide))
    whole = pltpu.roll(whole, 0, 1, stride=1, stride_axis=0)[:, :cols]
    high = whole.astype(jnp.bfloat16)
    low = (whole - high.astype(jnp.float32)).astype(jnp.bfloat16)
    return jnp.concatenate([high[:HALO], low[:HALO], high[HALO:], low[HALO:]], axis=0)


def band_kernel(axes, groups_ref, beam_ref, taps_ref, t_ref, chosen_ref, scale_ref):
    row, col, sub = (lax.axis_index(a) for a in axes)
    stations, beams = chosen_ref.shape
    chan = t_ref.shape[0]
    square = (stations, stations)
    diagonal = lax.broadcasted_iota(jnp.int32, square, 0) == lax.broadcasted_iota(
        jnp.int32, square, 1
    )
    groups = jnp.broadcast_to(groups_ref[...], square).astype(jnp.float32)
    groups = jnp.sum(jnp.where(diagonal, groups, 0.0), axis=1, keepdims=True)
    total = beam_ref.shape[1]
    first = ((col * 2 + sub) * 4 + row) * beams
    every = jnp.broadcast_to(beam_ref[...], (8, total))
    wanted = pltpu.roll(every, lax.rem(total - first, total), 1)[:1, :beams]
    chosen = (groups == wanted.astype(jnp.float32)).astype(jnp.float32)
    chosen_ref[...] = chosen
    scale = (1.0 / (chan * math.sqrt(ANTENNAS_PER_STN))) / jnp.sqrt(
        jnp.sum(chosen, axis=0, keepdims=True)
    )
    scale_ref[...] = jnp.broadcast_to(scale, scale_ref.shape)
    for c in range(chan):
        t_ref[c] = bands(taps_ref, c, t_ref.shape[1] // 2, t_ref.shape[2])


def weight_kernel(axes, chosen_ref, scale_ref, *refs):
    row = lax.axis_index(axes[0])
    w_refs, (m_ref, all_ref) = refs[:4], refs[4:]
    stations, beams = chosen_ref.shape
    held = all_ref.shape[2] // (2 * beams)
    chan = 4 * held
    for mask, ref in enumerate(w_refs):
        all_ref[row ^ mask] = ref[ref.shape[0] - stations :]
    members = chosen_ref[...] > 0
    scale = scale_ref[...]
    zero = jnp.zeros((), jnp.float32)
    parts = []
    for k in range(chan):
        whole = all_ref[k // held].astype(jnp.float32)
        places = [(2 * (k % held) + q) * beams for q in range(2)]
        parts.append(tuple(jnp.where(members, whole[:, p : p + beams], zero) for p in places))
    parts = fourier(parts, -1.0)
    real = [p[0] * scale for p in parts]
    imag = [p[1] * scale for p in parts]
    upper = jnp.concatenate([v for k in range(chan) for v in (real[k], -imag[k])], axis=0)
    lower = jnp.concatenate([v for k in range(chan) for v in (imag[k], real[k])], axis=0)
    whole = jnp.concatenate([upper, lower], axis=1).T.astype(m_ref.dtype)
    count = 2 * beams
    place = lax.broadcasted_iota(jnp.int32, (count, 1), 0)
    source = place % 2 * beams + place // 2
    order = jnp.where(lax.broadcasted_iota(jnp.int32, (count, count), 1) == source, 1.0, 0.0)
    whole = jnp.dot(order.astype(m_ref.dtype), whole, preferred_element_type=jnp.float32)
    whole = whole.astype(m_ref.dtype)
    width = whole.shape[1]
    step = 2 * stations
    odd = jnp.concatenate([whole[:, width - step :], whole[:, : width - step]], axis=1)
    for c in range(chan):
        base = odd if c % 2 else whole
        start = c // 2 * 2 * step
        m_ref[c, :, start:] = base[:, : width - start]
        if start:
            m_ref[c, :, :start] = base[:, width - start :]


def gather_lanes(axes, x_refs, places, lanes_ref):
    row, col, sub = (lax.axis_index(a) for a in axes)
    rows = x_refs[0].shape[1]
    for ((dc, ds), masks), ref in zip(places, x_refs):
        for k, m in enumerate(masks):
            lane = lane_of(row ^ m, col ^ dc, sub ^ ds)
            lanes_ref[pl.ds(pl.multiple_of(lane * rows, rows), rows)] = ref[k]


def lane_products(axes, flips, m_ref, lanes_ref, first, count):
    col, sub = (lax.axis_index(a) for a in axes[1:])
    width = 4 * lanes_ref.shape[0] // 16
    total = None
    for dc, ds in flips:
        start = pl.multiple_of((2 * (sub ^ ds) + (col ^ dc)) * width, width)
        some = m_ref[first : first + count, :, pl.ds(start, width)]
        some = some.reshape(count * m_ref.shape[1], width)
        found = jnp.dot(some, lanes_ref[pl.ds(start, width)], preferred_element_type=jnp.float32)
        total = found if total is None else total + found
    return total


def part_kernel(axes, places, m_ref, *refs):
    x_refs, (sum_ref, lanes_ref) = refs[: len(places)], refs[-2:]
    before = refs[len(places) : -2]
    gather_lanes(axes, x_refs, places, lanes_ref)
    flips = sorted({flip for flip, _ in places})
    for first in range(0, m_ref.shape[0], 4):
        found = lane_products(axes, flips, m_ref, lanes_ref, first, 4)
        found = found.reshape((4,) + sum_ref.shape[1:])
        for ref in before:
            found = found + ref[first : first + 4]
        sum_ref[first : first + 4] = found


def beam_kernel(
    axes,
    x_refs,
    m_ref,
    t_ref,
    sum_ref,
    series_ref,
    vis_ref,
    lanes_ref,
    cross_ref,
    inverse_ref,
    out_ref,
    store_sems,
):
    row, col, sub = (lax.axis_index(a) for a in axes)
    rows = x_refs[0].shape[1]
    stations = rows // 2
    chan = 4 * 4
    frames = lanes_ref.shape[1]

    gather_lanes(axes, x_refs[4:], PLACES[4:], lanes_ref)
    beams = m_ref.shape[1] // 2
    tile = t_ref.shape[2]
    stores = []
    for first in range(0, 16, 4):
        found = lane_products(axes, FLIPS[3:], m_ref, lanes_ref, first, 4)
        found = found.reshape((4,) + sum_ref.shape[1:]) + sum_ref[first : first + 4]
        inverse_ref[first : first + 4] = found.astype(jnp.bfloat16)
    for lane in range(chan):
        for n in range(frames // tile):
            taken = [inverse_ref[lane, :, n * tile : (n + 1) * tile]] * 2
            first = 2 * HALO
            if n > 0:
                taken = [inverse_ref[lane, :, n * tile - HALO : n * tile]] * 2 + taken
                first = 0
            value = jnp.dot(
                jnp.concatenate(taken, axis=1), t_ref[lane, first:], preferred_element_type=jnp.float32
            )
            for part in range(tile // 128):
                slot = n * (tile // 128) + part
                out_ref[lane, slot] = value[:, part * 128 : (part + 1) * 128]
                stores.append(
                    pltpu.make_async_copy(
                        out_ref.at[lane, slot],
                        series_ref.at[:, lane // 8, lane % 8, pl.ds(slot * 128, 128)],
                        store_sems.at[lane, slot],
                    )
                )
                stores[-1].start()
    gather_lanes(axes, x_refs[:4], PLACES[:4], lanes_ref)
    inner = []
    for b in range(4):
        parts = []
        for a in range(4):
            start = (4 * a + b) * rows
            parts.append(
                tuple(
                    lanes_ref[start + q * stations : start + (q + 1) * stations].astype(
                        jnp.float32
                    )
                    for q in range(2)
                )
            )
        inner.append(fourier(parts, -1.0))
    scale = 1.0 / math.sqrt(chan * ANTENNAS_PER_STN)
    block = (col * 2 + sub) * vis_ref.shape[2]
    own = vis_ref.shape[2]
    for j in range(4):
        re, im = inner[0][j]
        for b in range(1, 4):
            cosine = jnp.float32(0.0)
            sine = jnp.float32(0.0)
            for r in range(4):
                angle = -2.0 * math.pi * b * (4 * r + j) / chan
                cosine = jnp.where(row == r, math.cos(angle), cosine)
                sine = jnp.where(row == r, math.sin(angle), sine)
            yr, yi = inner[b][j]
            re = re + (yr * cosine - yi * sine)
            im = im + (yr * sine + yi * cosine)
        both = (jnp.concatenate([re, im], axis=0) * scale).astype(jnp.bfloat16)
        cross_ref[...] = lax.dot_general(
            both, both, (((1,), (1,)), ((), ())), preferred_element_type=jnp.float32
        )
        own_real = cross_ref[pl.ds(pl.multiple_of(block, own), own)]
        own_imag = cross_ref[pl.ds(pl.multiple_of(stations + block, own), own)]
        vis_ref[j, 0] = (own_real[:, :stations] + own_imag[:, stations:]) * (1.0 / SPEC)
        vis_ref[j, 1] = (own_imag[:, :stations] - own_real[:, stations:]) * (1.0 / SPEC)
    for copy in stores:
        copy.wait()


def call_beams(axes, pieces, matrix, bands, sums):
    params = pltpu.CompilerParams(vmem_limit_bytes=VMEM_LIMIT)
    vmem = pl.BlockSpec(memory_space=pltpu.VMEM)
    chan, frames = bands.shape[0], pieces[0].shape[2]
    stations, beams = pieces[0].shape[1] // 2, matrix.shape[1] // 2
    anywhere = pl.BlockSpec(memory_space=pl.ANY)
    series, visibilities = pl.pallas_call(
        lambda *refs: beam_kernel(axes, refs[: len(pieces)], *refs[len(pieces) :]),
        out_shape=(
            jax.ShapeDtypeStruct((2 * beams, 2, 8, frames), jnp.float32),
            jax.ShapeDtypeStruct((4, 2, stations // 4, stations), jnp.float32),
        ),
        in_specs=[vmem] * (len(pieces) + 3),
        out_specs=(anywhere, vmem),
        scratch_shapes=[
            pltpu.VMEM((chan * 2 * stations, frames), jnp.bfloat16),
            pltpu.VMEM((2 * stations, 2 * stations), jnp.float32),
            pltpu.VMEM((chan, 2 * beams, frames), jnp.bfloat16),
            pltpu.VMEM((chan, frames // 128, 2 * beams, 128), jnp.float32),
            pltpu.SemaphoreType.DMA((chan, frames // 128)),
        ],
        compiler_params=params,
        name="beams_and_series",
    )(*pieces, matrix, bands, sums)
    return visibilities, series


def swap(x, axis, mask):
    size = lax.axis_size(axis)
    return lax.ppermute(x, axis, [(i, i ^ mask) for i in range(size)])


def fast_body(
    samples, analysis_taps, synthesis_taps, antenna_station, station_group, beam_group, beam_weights
):
    axes = ("row", "col", "sub")
    params = pltpu.CompilerParams(vmem_limit_bytes=VMEM_LIMIT)
    vmem = pl.BlockSpec(memory_space=pltpu.VMEM)
    smem = pl.BlockSpec(memory_space=pltpu.SMEM)
    hbm = pl.BlockSpec(memory_space=pltpu.HBM)
    local, _, chan, frames = samples.shape
    stations = station_group.shape[0]
    antennas = antenna_station.shape[0]

    held_chan = beam_weights.shape[0]
    beams = beam_weights.shape[2] // 4
    block = jax.ShapeDtypeStruct((4, 2 * local, frames), jnp.bfloat16)
    half = jax.ShapeDtypeStruct((2, 2 * local, frames), jnp.bfloat16)
    kept, crossing_a, crossing_b, paired, far_a, far_b = pl.pallas_call(
        functools.partial(spread_kernel, axes),
        out_shape=[block, half, half, block, half, half],
        in_specs=[vmem],
        out_specs=[vmem] * 6,
        compiler_params=params,
        name="lane_spread",
    )(samples)
    members, taps = pl.pallas_call(
        functools.partial(table_kernel, axes),
        out_shape=[
            jax.ShapeDtypeStruct((2 * stations, 8 * local), jnp.bfloat16),
            jax.ShapeDtypeStruct((analysis_taps.shape[0], frames), jnp.float32),
        ],
        in_specs=[vmem] * 2,
        out_specs=[vmem] * 2,
        compiler_params=params,
        cost_estimate=pl.CostEstimate(flops=0, bytes_accessed=16 << 20, transcendentals=0),
        name="station_tables",
    )(antenna_station.reshape(1, antennas), analysis_taps)
    far_a = swap(far_a, "sub", 1)
    crossing_a = swap(crossing_a, "col", 1)
    far_a = swap(far_a, "col", 1)
    far_b = swap(far_b, "sub", 1)
    paired = swap(paired, "sub", 1)
    crossing_b = swap(crossing_b, "col", 1)
    far_b = swap(far_b, "col", 1)

    lane = jax.ShapeDtypeStruct((2 * stations, frames), jnp.bfloat16)
    sums2, sums3 = pl.pallas_call(
        functools.partial(sum_kernel, 0),
        out_shape=[lane] * 2,
        in_specs=[vmem] * 5,
        out_specs=[vmem] * 2,
        compiler_params=params,
        name="plane_sums_far",
    )(members, kept, paired, crossing_a, far_a)
    sums3, sums2 = swap(sums3, "row", 3), swap(sums2, "row", 2)
    sums0, sums1 = pl.pallas_call(
        functools.partial(sum_kernel, 2),
        out_shape=[jax.ShapeDtypeStruct(lane.shape, jnp.float32), lane],
        in_specs=[vmem] * 5,
        out_specs=[vmem] * 2,
        compiler_params=params,
        name="plane_sums_near",
    )(members, kept, paired, crossing_b, far_b)

    share = jax.ShapeDtypeStruct((stations, 2 * held_chan * beams), jnp.bfloat16)
    shares = pl.pallas_call(
        functools.partial(pack_kernel, axes),
        out_shape=[share] * 4,
        in_specs=[vmem],
        out_specs=[vmem] * 4,
        compiler_params=params,
        cost_estimate=pl.CostEstimate(flops=0, bytes_accessed=8 << 20, transcendentals=0),
        name="weight_shares",
    )(beam_weights.transpose(0, 1, 3, 2))

    lane_share = jax.ShapeDtypeStruct((3 * stations, frames), jnp.bfloat16)
    filtered, *sent = pl.pallas_call(
        filter_kernel,
        out_shape=[lane] + [lane_share] * 3,
        in_specs=[vmem] * 8,
        out_specs=[vmem] * 4,
        compiler_params=params,
        name="station_filter",
    )(taps, sums0, swap(sums1, "row", 1), sums2, sums3, *shares[1:])
    moved = [swap(x, "row", m) for x, m in zip(sent, (1, 2, 3))]

    tile = 256
    table = jax.ShapeDtypeStruct((stations, beams), jnp.float32)
    other = [swap(filtered, "col", 1)]
    moved[0], *small = lax.optimization_barrier(
        (moved[0], station_group, beam_group, synthesis_taps)
    )
    other.append(swap(moved[0][: 2 * stations], "col", 1))
    bands, chosen, scale = pl.pallas_call(
        functools.partial(band_kernel, axes),
        out_shape=[
            jax.ShapeDtypeStruct((chan, 2 * (tile + HALO), tile), jnp.bfloat16),
            table,
            table,
        ],
        in_specs=[vmem, vmem, smem],
        out_specs=[vmem] * 3,
        compiler_params=params,
        cost_estimate=pl.CostEstimate(flops=0, bytes_accessed=16 << 20, transcendentals=0),
        name="synthesis_bands",
    )(
        small[0].reshape(1, stations),
        small[1].reshape(1, beam_group.shape[0]),
        small[2],
    )
    moved[1], moved[2], other[1], bands, chosen, scale = lax.optimization_barrier(
        (moved[1], moved[2], other[1], bands, chosen, scale)
    )
    matrix = pl.pallas_call(
        functools.partial(weight_kernel, axes),
        out_shape=jax.ShapeDtypeStruct((chan, 2 * beams, 2 * chan * stations), jnp.bfloat16),
        in_specs=[vmem] * 6,
        out_specs=vmem,
        scratch_shapes=[pltpu.VMEM((4,) + share.shape, jnp.bfloat16)],
        compiler_params=params,
        cost_estimate=pl.CostEstimate(flops=0, bytes_accessed=8 << 20, transcendentals=0),
        name="weight_matrix",
    )(chosen, scale, shares[0], *moved)

    def add_part(places, xs, before, name):
        return pl.pallas_call(
            functools.partial(part_kernel, axes, places),
            out_shape=jax.ShapeDtypeStruct((chan, 2 * beams, frames), jnp.float32),
            in_specs=[vmem] * (1 + len(xs) + len(before)),
            out_specs=vmem,
            scratch_shapes=[pltpu.VMEM((chan * 2 * stations, frames), jnp.bfloat16)],
            compiler_params=params,
            cost_estimate=pl.CostEstimate(flops=0, bytes_accessed=8 << 20, transcendentals=0),
            name=name,
        )(matrix, *xs, *before)

    distant = [x[: 2 * stations] for x in moved[1:]]
    held = jnp.stack([filtered, moved[0][: 2 * stations], *distant])
    near = jnp.stack(other)
    far = swap(jnp.stack(distant), "col", 1)
    paired, last_near = swap(held, "sub", 1), swap(near, "sub", 1)
    sums = add_part(PLACES[:1], [held], [], "own_beams")
    far, sums = lax.optimization_barrier((far, sums))
    last_far = swap(far, "sub", 1)
    sums = add_part(PLACES[1:4], [paired, near, far], [sums], "near_beams")
    pieces = [held, paired, near, far, last_near, last_far]

    visibilities, series = call_beams(axes, pieces, matrix, bands, sums)
    return visibilities, series.reshape(beams, 2, chan, frames)


def polyphase(signal, coefficients):
    length = signal.shape[-1]
    output = coefficients[0][:, None] * signal
    for tap_index in range(1, coefficients.shape[0]):
        shifted = jnp.pad(
            signal[..., : length - tap_index], [(0, 0)] * (signal.ndim - 1) + [(tap_index, 0)]
        )
        output = output + coefficients[tap_index][:, None] * shifted
    return output


def fourier_table(length, direction):
    indices = jnp.arange(length)
    angles = (
        2.0 * math.pi / length * (indices[:, None] * indices[None, :] % length).astype(jnp.float32)
    )
    cosine_part = jnp.cos(angles)
    sine_part = jnp.sin(angles)
    table = jnp.stack(
        [
            jnp.stack([cosine_part, direction * sine_part]),
            jnp.stack([-direction * sine_part, cosine_part]),
        ]
    )
    return table.transpose(0, 2, 1, 3) * (1.0 / math.sqrt(length))


def general_body(
    samples, analysis_taps, synthesis_taps, antenna_station, station_group, beam_group, beam_weights
):
    high = lax.Precision.HIGHEST
    block_count = lax.axis_size(("col", "sub"))
    block_index = lax.axis_index(("col", "sub"))
    filtered = polyphase(samples.astype(jnp.float32), analysis_taps)
    spectra = jnp.einsum(
        "aqcf,qcpk->apkf", filtered, fourier_table(samples.shape[2], -1.0), precision=high
    ).astype(jnp.bfloat16)
    turned = lax.all_to_all(spectra, "row", split_axis=2, concat_axis=0, tiled=True)
    local_count = spectra.shape[0]
    held_rows = turned.shape[0]
    chan_rows = turned.shape[2]
    spec_len = turned.shape[3]
    station_count = station_group.shape[0]
    flat_width = 2 * chan_rows * spec_len
    tile_rows = station_count // block_count
    shard_rows = lax.all_gather(turned, ("col", "sub"), axis=0, tiled=True)
    row_total = shard_rows.shape[0]
    positions = jnp.arange(row_total, dtype=jnp.int32)
    source_block = positions // held_rows
    offset_rows = positions % held_rows
    source_row = offset_rows // local_count
    antenna = offset_rows % local_count
    global_index = (source_row * block_count + source_block) * local_count + antenna
    targets = antenna_station[global_index]
    wanted = jnp.arange(station_count, dtype=jnp.int32)
    one_hot = (targets[None, :] == wanted[:, None]).astype(jnp.bfloat16)
    summed_values = jnp.dot(
        one_hot, shard_rows.reshape(row_total, flat_width), preferred_element_type=jnp.float32
    )
    flat_stations = (summed_values * (1.0 / math.sqrt(ANTENNAS_PER_STN))).astype(jnp.bfloat16)
    station_list = flat_stations.reshape(station_count, 2, chan_rows, spec_len)
    real_part = station_list[:, 0]
    imag_part = station_list[:, 1]
    own_rows = lax.dynamic_slice_in_dim(station_list, block_index * tile_rows, tile_rows, 0)
    own_real = own_rows[:, 0]
    own_imag = own_rows[:, 1]
    vis_real = (
        jnp.einsum("icf,jcf->cij", own_real, real_part, preferred_element_type=jnp.float32)
        + jnp.einsum("icf,jcf->cij", own_imag, imag_part, preferred_element_type=jnp.float32)
    ) * (1.0 / SPEC)
    vis_imag = (
        jnp.einsum("icf,jcf->cij", own_imag, real_part, preferred_element_type=jnp.float32)
        - jnp.einsum("icf,jcf->cij", own_real, imag_part, preferred_element_type=jnp.float32)
    ) * (1.0 / SPEC)
    visibilities = jnp.stack([vis_real, vis_imag], axis=1)
    beam_block = beam_weights.shape[2]
    own_groups = lax.dynamic_slice_in_dim(beam_group, block_index * beam_block, beam_block, 0)
    members = station_group[:, 0][None, :] == own_groups[:, None]
    scaling = 1.0 / jnp.sqrt(jnp.sum(members.astype(jnp.float32), axis=1))
    weights = jnp.where(members[None, None], beam_weights, jnp.zeros((), jnp.bfloat16))
    weight_real = weights[:, 0]
    imaginary_weight = weights[:, 1]
    beam_real = jnp.einsum(
        "cbs,scf->bcf", weight_real, real_part, preferred_element_type=jnp.float32
    ) - jnp.einsum("cbs,scf->bcf", imaginary_weight, imag_part, preferred_element_type=jnp.float32)
    beam_imag = jnp.einsum(
        "cbs,scf->bcf", weight_real, imag_part, preferred_element_type=jnp.float32
    ) + jnp.einsum("cbs,scf->bcf", imaginary_weight, real_part, preferred_element_type=jnp.float32)
    beams = (jnp.stack([beam_real, beam_imag], axis=1) * scaling[:, None, None, None]).astype(
        jnp.bfloat16
    )
    returned = lax.all_to_all(beams, "row", split_axis=0, concat_axis=2, tiled=True)
    inverse = jnp.einsum(
        "bqkf,qkpc->bpcf",
        returned.astype(jnp.float32),
        fourier_table(returned.shape[2], 1.0),
        precision=high,
    )
    beam_series = polyphase(inverse, synthesis_taps)
    return (visibilities, beam_series)


def solution(mesh):
    sizes = dict(mesh.shape)

    def body(samples, *others):
        chan = samples.shape[2]
        fits = (sizes["row"], sizes["col"], sizes["sub"], chan) == (4, 2, 2, 16)
        return (fast_body if fits else general_body)(samples, *others)

    return jax.shard_map(
        body,
        mesh=mesh,
        in_specs=(
            P(("grp", "row", "col", "sub"), None, None, None),
            P(),
            P(),
            P("grp"),
            P("grp", None),
            P("grp"),
            P(("grp", "row"), None, ("col", "sub"), None),
        ),
        out_specs=(
            P("row", None, ("grp", "col", "sub"), None),
            P(("grp", "col", "sub", "row"), None, None, None),
        ),
        check_vma=False,
    )
```

```python
import functools
import math

import jax
import jax.numpy as jnp
from jax import lax
from jax.experimental import pallas as pl
from jax.experimental.pallas import tpu as pltpu
from jax.sharding import PartitionSpec as P

ANTENNAS_PER_STN = 8
SPEC = 512
VMEM_LIMIT = 24 * 1024 * 1024
HALO = 128
FLIPS = ((0, 0), (0, 1), (1, 0), (1, 1))
NEAR, FAR = (0, 1), (2, 3)
PLACES = (
    (FLIPS[0], NEAR + FAR),
    (FLIPS[1], NEAR + FAR),
    (FLIPS[2], NEAR),
    (FLIPS[2], FAR),
    (FLIPS[3], NEAR),
    (FLIPS[3], FAR),
)


def fourier(parts, sign):
    count = len(parts)
    if count == 1:
        return parts
    even, odd = fourier(parts[0::2], sign), fourier(parts[1::2], sign)
    low, top = [], []
    for k in range(count // 2):
        er, ei = even[k]
        re, im = odd[k]
        if k == 0:
            tr, ti = re, im
        elif 4 * k == count:
            tr, ti = (-sign * im, sign * re)
        else:
            c, s = math.cos(2 * math.pi * k / count), sign * math.sin(2 * math.pi * k / count)
            tr, ti = re * c - im * s, re * s + im * c
        low.append((er + tr, ei + ti))
        top.append((er - tr, ei - ti))
    return low + top


def lane_of(row, col, sub):
    return sub * 8 + col * 4 + row


def spread_kernel(axes, x_ref, *out_refs):
    row, col, sub = (lax.axis_index(a) for a in axes)
    antennas, parts, chan, frames = x_ref.shape
    count = antennas * parts * chan
    shape = (count, count)
    place = lax.broadcasted_iota(jnp.int32, (count, 1), 0)
    antenna = place % antennas
    part = place // antennas % parts
    piece = place // (antennas * parts)
    lane = lane_of(row ^ (piece % 4) ^ 2, col ^ (piece // 4 % 2), sub ^ (piece // 8))
    source = (antenna * parts + part) * chan + lane
    order = jnp.where(lax.broadcasted_iota(jnp.int32, shape, 1) == source, 1.0, 0.0)
    moved = jnp.dot(
        order.astype(jnp.bfloat16),
        x_ref[...].reshape(count, frames),
        preferred_element_type=jnp.float32,
    ).astype(jnp.bfloat16)
    start = 0
    for ref in out_refs:
        size = ref.shape[0] * ref.shape[1]
        ref[...] = moved[start : start + size].reshape(ref.shape)
        start += size


def member_matrix(axes, names_ref, stations, local):
    row, col, sub = (lax.axis_index(a) for a in axes)
    antennas = names_ref.shape[1]
    every = jnp.broadcast_to(names_ref[...], (8, antennas))
    names = []
    for k in range(4):
        owner = (row * 2 + (col ^ (k // 2))) * 2 + (sub ^ (k % 2))
        names += [pltpu.roll(every, lax.rem(antennas - owner * local, antennas), 1)[:1, :local]] * 2
    names = jnp.concatenate(names, axis=1)
    shape = (2 * stations, 8 * local)
    place = lax.broadcasted_iota(jnp.int32, shape, 0)
    column = lax.broadcasted_iota(jnp.int32, shape, 1)
    same = (place % stations == names) & (place // stations == column // local % 2)
    return jnp.where(same, 1.0, 0.0).astype(jnp.bfloat16)


def table_kernel(axes, names_ref, taps_ref, members_ref, own_taps_ref):
    stations, local = members_ref.shape[0] // 2, members_ref.shape[1] // 8
    members_ref[...] = member_matrix(axes, names_ref, stations, local)
    taps = taps_ref[...]
    lane = lane_of(*(lax.axis_index(a) for a in axes))
    mine = lax.broadcasted_iota(jnp.int32, taps.shape, 1) == lane
    own = jnp.sum(jnp.where(mine, taps, 0.0), axis=1, keepdims=True)
    own_taps_ref[...] = jnp.broadcast_to(own, own_taps_ref.shape)


def sum_kernel(first, members_ref, *refs):
    x_refs, out_refs = refs[:4], refs[4:]
    for k, ref in enumerate(out_refs):
        rows = jnp.concatenate([x[first + k if x.shape[0] == 4 else k] for x in x_refs], axis=0)
        ref[...] = jnp.dot(
            members_ref[...], rows, preferred_element_type=jnp.float32
        ).astype(ref.dtype)


def filter_kernel(taps_ref, *refs):
    x_refs, share_refs, out_refs = refs[:4], refs[4:7], refs[7:]
    rows = out_refs[0].shape[0]
    total = x_refs[0][...]
    for ref in x_refs[1:]:
        total = total + ref[...].astype(jnp.float32)
    place = lax.broadcasted_iota(jnp.int32, total.shape, 1)
    result = total * taps_ref[0:1]
    for tap in range(1, taps_ref.shape[0]):
        moved = jnp.where(place >= tap, pltpu.roll(total, tap, 1), 0.0)
        result = result + moved * taps_ref[tap : tap + 1]
    result = result.astype(out_refs[0].dtype)
    out_refs[0][...] = result
    for ref, share in zip(out_refs[1:], share_refs):
        ref[:rows] = result
        ref[rows:] = share[...]


def pack_kernel(axes, w_ref, groups_ref, beam_ref, chosen_ref, scale_ref, *out_refs):
    row, col, sub = (lax.axis_index(a) for a in axes)
    chan, _, stations, width = w_ref.shape
    beams = width // 4
    for k in range(chan):
        for q in range(2):
            place = (2 * k + q) * beams
            parts = [w_ref[k, q, :, j * beams : (j + 1) * beams] for j in range(4)]
            for mask, ref in enumerate(out_refs):
                taken = parts[0]
                for j in range(1, 4):
                    taken = jnp.where((row ^ mask) == j, parts[j], taken)
                ref[:, place : place + beams] = taken
    square = (stations, stations)
    diagonal = lax.broadcasted_iota(jnp.int32, square, 0) == lax.broadcasted_iota(
        jnp.int32, square, 1
    )
    groups = jnp.broadcast_to(groups_ref[...], square).astype(jnp.float32)
    groups = jnp.sum(jnp.where(diagonal, groups, 0.0), axis=1, keepdims=True)
    total = beam_ref.shape[1]
    first = ((col * 2 + sub) * 4 + row) * beams
    every = jnp.broadcast_to(beam_ref[...], (8, total))
    wanted = pltpu.roll(every, lax.rem(total - first, total), 1)[:1, :beams]
    chosen = (groups == wanted.astype(jnp.float32)).astype(jnp.float32)
    chosen_ref[...] = chosen
    scale = (1.0 / (4 * chan * math.sqrt(ANTENNAS_PER_STN))) / jnp.sqrt(
        jnp.sum(chosen, axis=0, keepdims=True)
    )
    scale_ref[...] = jnp.broadcast_to(scale, scale_ref.shape)


def bands(taps_ref, lane, rows, cols):
    wide = 2 * cols
    places = lax.broadcasted_iota(jnp.int32, (8, wide), 1)
    base = jnp.zeros((8, wide), jnp.float32)
    for tap in range(taps_ref.shape[0]):
        base = jnp.where(places == (tap - HALO) % wide, taps_ref[tap, lane], base)
    whole = jnp.broadcast_to(base[0:1], (rows, wide))
    whole = pltpu.roll(whole, 0, 1, stride=1, stride_axis=0)[:, :cols]
    high = whole.astype(jnp.bfloat16)
    low = (whole - high.astype(jnp.float32)).astype(jnp.bfloat16)
    return jnp.concatenate([high[:HALO], low[:HALO], high[HALO:], low[HALO:]], axis=0)


def band_kernel(taps_ref, t_ref):
    for c in range(t_ref.shape[0]):
        t_ref[c] = bands(taps_ref, c, t_ref.shape[1] // 2, t_ref.shape[2])


def weight_kernel(axes, chosen_ref, scale_ref, *refs):
    row = lax.axis_index(axes[0])
    w_refs, (m_ref, all_ref) = refs[:4], refs[4:]
    stations, beams = chosen_ref.shape
    held = all_ref.shape[2] // (2 * beams)
    chan = 4 * held
    for mask, ref in enumerate(w_refs):
        all_ref[row ^ mask] = ref[ref.shape[0] - stations :]
    members = chosen_ref[...] > 0
    scale = scale_ref[...]
    zero = jnp.zeros((), jnp.float32)
    parts = []
    for k in range(chan):
        whole = all_ref[k // held].astype(jnp.float32)
        places = [(2 * (k % held) + q) * beams for q in range(2)]
        parts.append(tuple(jnp.where(members, whole[:, p : p + beams], zero) for p in places))
    parts = fourier(parts, -1.0)
    real = [p[0] * scale for p in parts]
    imag = [p[1] * scale for p in parts]
    upper = jnp.concatenate([v for k in range(chan) for v in (real[k], -imag[k])], axis=0)
    lower = jnp.concatenate([v for k in range(chan) for v in (imag[k], real[k])], axis=0)
    whole = jnp.concatenate([upper, lower], axis=1).T.astype(m_ref.dtype)
    count = 2 * beams
    place = lax.broadcasted_iota(jnp.int32, (count, 1), 0)
    source = place % 2 * beams + place // 2
    order = jnp.where(lax.broadcasted_iota(jnp.int32, (count, count), 1) == source, 1.0, 0.0)
    whole = jnp.dot(order.astype(m_ref.dtype), whole, preferred_element_type=jnp.float32)
    whole = whole.astype(m_ref.dtype)
    width = whole.shape[1]
    step = 2 * stations
    odd = jnp.concatenate([whole[:, width - step :], whole[:, : width - step]], axis=1)
    for c in range(chan):
        base = odd if c % 2 else whole
        start = c // 2 * 2 * step
        m_ref[c, :, start:] = base[:, : width - start]
        if start:
            m_ref[c, :, :start] = base[:, width - start :]


def gather_lanes(axes, x_refs, places, lanes_ref):
    row, col, sub = (lax.axis_index(a) for a in axes)
    rows = x_refs[0].shape[1]
    for ((dc, ds), masks), ref in zip(places, x_refs):
        for k, m in enumerate(masks):
            lane = lane_of(row ^ m, col ^ dc, sub ^ ds)
            lanes_ref[pl.ds(pl.multiple_of(lane * rows, rows), rows)] = ref[k]


def lane_products(axes, flips, m_ref, lanes_ref, first, count):
    col, sub = (lax.axis_index(a) for a in axes[1:])
    width = 4 * lanes_ref.shape[0] // 16
    total = None
    for dc, ds in flips:
        start = pl.multiple_of((2 * (sub ^ ds) + (col ^ dc)) * width, width)
        some = m_ref[first : first + count, :, pl.ds(start, width)]
        some = some.reshape(count * m_ref.shape[1], width)
        found = jnp.dot(some, lanes_ref[pl.ds(start, width)], preferred_element_type=jnp.float32)
        total = found if total is None else total + found
    return total


def part_kernel(axes, places, m_ref, *refs):
    x_refs, (sum_ref, lanes_ref) = refs[: len(places)], refs[-2:]
    before = refs[len(places) : -2]
    gather_lanes(axes, x_refs, places, lanes_ref)
    flips = sorted({flip for flip, _ in places})
    for first in range(0, m_ref.shape[0], 4):
        found = lane_products(axes, flips, m_ref, lanes_ref, first, 4)
        found = found.reshape((4,) + sum_ref.shape[1:])
        for ref in before:
            found = found + ref[first : first + 4]
        sum_ref[first : first + 4] = found


def beam_kernel(
    axes,
    x_refs,
    m_ref,
    t_ref,
    sum_ref,
    series_ref,
    vis_ref,
    lanes_ref,
    cross_ref,
    inverse_ref,
    out_ref,
    store_sems,
):
    row, col, sub = (lax.axis_index(a) for a in axes)
    rows = x_refs[0].shape[1]
    stations = rows // 2
    chan = 4 * 4
    frames = lanes_ref.shape[1]

    gather_lanes(axes, x_refs[4:], PLACES[4:], lanes_ref)
    beams = m_ref.shape[1] // 2
    tile = t_ref.shape[2]
    stores = []
    for first in range(0, 16, 4):
        found = lane_products(axes, FLIPS[3:], m_ref, lanes_ref, first, 4)
        found = found.reshape((4,) + sum_ref.shape[1:]) + sum_ref[first : first + 4]
        inverse_ref[first : first + 4] = found.astype(jnp.bfloat16)
    for lane in range(chan):
        for n in range(frames // tile):
            taken = [inverse_ref[lane, :, n * tile : (n + 1) * tile]] * 2
            first = 2 * HALO
            if n > 0:
                taken = [inverse_ref[lane, :, n * tile - HALO : n * tile]] * 2 + taken
                first = 0
            value = jnp.dot(
                jnp.concatenate(taken, axis=1), t_ref[lane, first:], preferred_element_type=jnp.float32
            )
            for part in range(tile // 128):
                slot = n * (tile // 128) + part
                out_ref[lane, slot] = value[:, part * 128 : (part + 1) * 128]
                stores.append(
                    pltpu.make_async_copy(
                        out_ref.at[lane, slot],
                        series_ref.at[:, lane // 8, lane % 8, pl.ds(slot * 128, 128)],
                        store_sems.at[lane, slot],
                    )
                )
                stores[-1].start()
    gather_lanes(axes, x_refs[:4], PLACES[:4], lanes_ref)
    inner = []
    for b in range(4):
        parts = []
        for a in range(4):
            start = (4 * a + b) * rows
            parts.append(
                tuple(
                    lanes_ref[start + q * stations : start + (q + 1) * stations].astype(
                        jnp.float32
                    )
                    for q in range(2)
                )
            )
        inner.append(fourier(parts, -1.0))
    scale = 1.0 / math.sqrt(chan * ANTENNAS_PER_STN)
    block = (col * 2 + sub) * vis_ref.shape[2]
    own = vis_ref.shape[2]
    for j in range(4):
        re, im = inner[0][j]
        for b in range(1, 4):
            cosine = jnp.float32(0.0)
            sine = jnp.float32(0.0)
            for r in range(4):
                angle = -2.0 * math.pi * b * (4 * r + j) / chan
                cosine = jnp.where(row == r, math.cos(angle), cosine)
                sine = jnp.where(row == r, math.sin(angle), sine)
            yr, yi = inner[b][j]
            re = re + (yr * cosine - yi * sine)
            im = im + (yr * sine + yi * cosine)
        both = (jnp.concatenate([re, im], axis=0) * scale).astype(jnp.bfloat16)
        cross_ref[...] = lax.dot_general(
            both, both, (((1,), (1,)), ((), ())), preferred_element_type=jnp.float32
        )
        own_real = cross_ref[pl.ds(pl.multiple_of(block, own), own)]
        own_imag = cross_ref[pl.ds(pl.multiple_of(stations + block, own), own)]
        vis_ref[j, 0] = (own_real[:, :stations] + own_imag[:, stations:]) * (1.0 / SPEC)
        vis_ref[j, 1] = (own_imag[:, :stations] - own_real[:, stations:]) * (1.0 / SPEC)
    for copy in stores:
        copy.wait()


def call_beams(axes, pieces, matrix, bands, sums):
    params = pltpu.CompilerParams(vmem_limit_bytes=VMEM_LIMIT)
    vmem = pl.BlockSpec(memory_space=pltpu.VMEM)
    chan, frames = bands.shape[0], pieces[0].shape[2]
    stations, beams = pieces[0].shape[1] // 2, matrix.shape[1] // 2
    anywhere = pl.BlockSpec(memory_space=pl.ANY)
    series, visibilities = pl.pallas_call(
        lambda *refs: beam_kernel(axes, refs[: len(pieces)], *refs[len(pieces) :]),
        out_shape=(
            jax.ShapeDtypeStruct((2 * beams, 2, 8, frames), jnp.float32),
            jax.ShapeDtypeStruct((4, 2, stations // 4, stations), jnp.float32),
        ),
        in_specs=[vmem] * (len(pieces) + 3),
        out_specs=(anywhere, vmem),
        scratch_shapes=[
            pltpu.VMEM((chan * 2 * stations, frames), jnp.bfloat16),
            pltpu.VMEM((2 * stations, 2 * stations), jnp.float32),
            pltpu.VMEM((chan, 2 * beams, frames), jnp.bfloat16),
            pltpu.VMEM((chan, frames // 128, 2 * beams, 128), jnp.float32),
            pltpu.SemaphoreType.DMA((chan, frames // 128)),
        ],
        compiler_params=params,
        name="beams_and_series",
    )(*pieces, matrix, bands, sums)
    return visibilities, series


def swap(x, axis, mask):
    size = lax.axis_size(axis)
    return lax.ppermute(x, axis, [(i, i ^ mask) for i in range(size)])


def fast_body(
    samples, analysis_taps, synthesis_taps, antenna_station, station_group, beam_group, beam_weights
):
    axes = ("row", "col", "sub")
    params = pltpu.CompilerParams(vmem_limit_bytes=VMEM_LIMIT)
    vmem = pl.BlockSpec(memory_space=pltpu.VMEM)
    smem = pl.BlockSpec(memory_space=pltpu.SMEM)
    hbm = pl.BlockSpec(memory_space=pltpu.HBM)
    local, _, chan, frames = samples.shape
    stations = station_group.shape[0]
    antennas = antenna_station.shape[0]

    held_chan = beam_weights.shape[0]
    beams = beam_weights.shape[2] // 4
    block = jax.ShapeDtypeStruct((4, 2 * local, frames), jnp.bfloat16)
    half = jax.ShapeDtypeStruct((2, 2 * local, frames), jnp.bfloat16)
    kept, crossing_a, crossing_b, paired, far_a, far_b = pl.pallas_call(
        functools.partial(spread_kernel, axes),
        out_shape=[block, half, half, block, half, half],
        in_specs=[vmem],
        out_specs=[vmem] * 6,
        compiler_params=params,
        name="lane_spread",
    )(samples)
    members, taps = pl.pallas_call(
        functools.partial(table_kernel, axes),
        out_shape=[
            jax.ShapeDtypeStruct((2 * stations, 8 * local), jnp.bfloat16),
            jax.ShapeDtypeStruct((analysis_taps.shape[0], frames), jnp.float32),
        ],
        in_specs=[vmem] * 2,
        out_specs=[vmem] * 2,
        compiler_params=params,
        cost_estimate=pl.CostEstimate(flops=0, bytes_accessed=16 << 20, transcendentals=0),
        name="station_tables",
    )(antenna_station.reshape(1, antennas), analysis_taps)
    far_a = swap(far_a, "sub", 1)
    crossing_a = swap(crossing_a, "col", 1)
    far_a = swap(far_a, "col", 1)
    far_b = swap(far_b, "sub", 1)
    paired = swap(paired, "sub", 1)
    crossing_b = swap(crossing_b, "col", 1)
    far_b = swap(far_b, "col", 1)

    lane = jax.ShapeDtypeStruct((2 * stations, frames), jnp.bfloat16)
    sums2, sums3 = pl.pallas_call(
        functools.partial(sum_kernel, 0),
        out_shape=[lane] * 2,
        in_specs=[vmem] * 5,
        out_specs=[vmem] * 2,
        compiler_params=params,
        name="plane_sums_far",
    )(members, kept, paired, crossing_a, far_a)
    sums3, sums2 = swap(sums3, "row", 3), swap(sums2, "row", 2)
    sums0, sums1 = pl.pallas_call(
        functools.partial(sum_kernel, 2),
        out_shape=[jax.ShapeDtypeStruct(lane.shape, jnp.float32), lane],
        in_specs=[vmem] * 5,
        out_specs=[vmem] * 2,
        compiler_params=params,
        name="plane_sums_near",
    )(members, kept, paired, crossing_b, far_b)

    share = jax.ShapeDtypeStruct((stations, 2 * held_chan * beams), jnp.bfloat16)
    table = jax.ShapeDtypeStruct((stations, beams), jnp.float32)
    chosen, scale, *shares = pl.pallas_call(
        functools.partial(pack_kernel, axes),
        out_shape=[table] * 2 + [share] * 4,
        in_specs=[vmem] * 3,
        out_specs=[vmem] * 6,
        compiler_params=params,
        cost_estimate=pl.CostEstimate(flops=0, bytes_accessed=8 << 20, transcendentals=0),
        name="weight_shares",
    )(
        beam_weights.transpose(0, 1, 3, 2),
        station_group.reshape(1, stations),
        beam_group.reshape(1, beam_group.shape[0]),
    )

    lane_share = jax.ShapeDtypeStruct((3 * stations, frames), jnp.bfloat16)
    filtered, *sent = pl.pallas_call(
        filter_kernel,
        out_shape=[lane] + [lane_share] * 3,
        in_specs=[vmem] * 8,
        out_specs=[vmem] * 4,
        compiler_params=params,
        name="station_filter",
    )(taps, sums0, swap(sums1, "row", 1), sums2, sums3, *shares[1:])
    moved = [swap(x, "row", m) for x, m in zip(sent, (1, 2, 3))]

    tile = 256
    late_taps = synthesis_taps
    other = [swap(filtered, "col", 1), swap(moved[0][: 2 * stations], "col", 1)]
    bands = pl.pallas_call(
        band_kernel,
        out_shape=jax.ShapeDtypeStruct((chan, 2 * (tile + HALO), tile), jnp.bfloat16),
        in_specs=[smem],
        out_specs=vmem,
        compiler_params=params,
        cost_estimate=pl.CostEstimate(flops=0, bytes_accessed=16 << 20, transcendentals=0),
        name="synthesis_bands",
    )(late_taps)
    moved[1], moved[2], other[1], bands = lax.optimization_barrier(
        (moved[1], moved[2], other[1], bands)
    )
    matrix = pl.pallas_call(
        functools.partial(weight_kernel, axes),
        out_shape=jax.ShapeDtypeStruct((chan, 2 * beams, 2 * chan * stations), jnp.bfloat16),
        in_specs=[vmem] * 6,
        out_specs=vmem,
        scratch_shapes=[pltpu.VMEM((4,) + share.shape, jnp.bfloat16)],
        compiler_params=params,
        cost_estimate=pl.CostEstimate(flops=0, bytes_accessed=8 << 20, transcendentals=0),
        name="weight_matrix",
    )(chosen, scale, shares[0], *moved)

    def add_part(places, xs, before, name):
        return pl.pallas_call(
            functools.partial(part_kernel, axes, places),
            out_shape=jax.ShapeDtypeStruct((chan, 2 * beams, frames), jnp.float32),
            in_specs=[vmem] * (1 + len(xs) + len(before)),
            out_specs=vmem,
            scratch_shapes=[pltpu.VMEM((chan * 2 * stations, frames), jnp.bfloat16)],
            compiler_params=params,
            cost_estimate=pl.CostEstimate(flops=0, bytes_accessed=8 << 20, transcendentals=0),
            name=name,
        )(matrix, *xs, *before)

    distant = [x[: 2 * stations] for x in moved[1:]]
    held = jnp.stack([filtered, moved[0][: 2 * stations], *distant])
    near = jnp.stack(other)
    far = swap(jnp.stack(distant), "col", 1)
    paired, last_near = swap(held, "sub", 1), swap(near, "sub", 1)
    sums = add_part(PLACES[:1], [held], [], "own_beams")
    far, sums = lax.optimization_barrier((far, sums))
    last_far = swap(far, "sub", 1)
    sums = add_part(PLACES[1:4], [paired, near, far], [sums], "near_beams")
    pieces = [held, paired, near, far, last_near, last_far]

    visibilities, series = call_beams(axes, pieces, matrix, bands, sums)
    return visibilities, series.reshape(beams, 2, chan, frames)


def polyphase(signal, coefficients):
    length = signal.shape[-1]
    output = coefficients[0][:, None] * signal
    for tap_index in range(1, coefficients.shape[0]):
        shifted = jnp.pad(
            signal[..., : length - tap_index], [(0, 0)] * (signal.ndim - 1) + [(tap_index, 0)]
        )
        output = output + coefficients[tap_index][:, None] * shifted
    return output


def fourier_table(length, direction):
    indices = jnp.arange(length)
    angles = (
        2.0 * math.pi / length * (indices[:, None] * indices[None, :] % length).astype(jnp.float32)
    )
    cosine_part = jnp.cos(angles)
    sine_part = jnp.sin(angles)
    table = jnp.stack(
        [
            jnp.stack([cosine_part, direction * sine_part]),
            jnp.stack([-direction * sine_part, cosine_part]),
        ]
    )
    return table.transpose(0, 2, 1, 3) * (1.0 / math.sqrt(length))


def general_body(
    samples, analysis_taps, synthesis_taps, antenna_station, station_group, beam_group, beam_weights
):
    high = lax.Precision.HIGHEST
    block_count = lax.axis_size(("col", "sub"))
    block_index = lax.axis_index(("col", "sub"))
    filtered = polyphase(samples.astype(jnp.float32), analysis_taps)
    spectra = jnp.einsum(
        "aqcf,qcpk->apkf", filtered, fourier_table(samples.shape[2], -1.0), precision=high
    ).astype(jnp.bfloat16)
    turned = lax.all_to_all(spectra, "row", split_axis=2, concat_axis=0, tiled=True)
    local_count = spectra.shape[0]
    held_rows = turned.shape[0]
    chan_rows = turned.shape[2]
    spec_len = turned.shape[3]
    station_count = station_group.shape[0]
    flat_width = 2 * chan_rows * spec_len
    tile_rows = station_count // block_count
    shard_rows = lax.all_gather(turned, ("col", "sub"), axis=0, tiled=True)
    row_total = shard_rows.shape[0]
    positions = jnp.arange(row_total, dtype=jnp.int32)
    source_block = positions // held_rows
    offset_rows = positions % held_rows
    source_row = offset_rows // local_count
    antenna = offset_rows % local_count
    global_index = (source_row * block_count + source_block) * local_count + antenna
    targets = antenna_station[global_index]
    wanted = jnp.arange(station_count, dtype=jnp.int32)
    one_hot = (targets[None, :] == wanted[:, None]).astype(jnp.bfloat16)
    summed_values = jnp.dot(
        one_hot, shard_rows.reshape(row_total, flat_width), preferred_element_type=jnp.float32
    )
    flat_stations = (summed_values * (1.0 / math.sqrt(ANTENNAS_PER_STN))).astype(jnp.bfloat16)
    station_list = flat_stations.reshape(station_count, 2, chan_rows, spec_len)
    real_part = station_list[:, 0]
    imag_part = station_list[:, 1]
    own_rows = lax.dynamic_slice_in_dim(station_list, block_index * tile_rows, tile_rows, 0)
    own_real = own_rows[:, 0]
    own_imag = own_rows[:, 1]
    vis_real = (
        jnp.einsum("icf,jcf->cij", own_real, real_part, preferred_element_type=jnp.float32)
        + jnp.einsum("icf,jcf->cij", own_imag, imag_part, preferred_element_type=jnp.float32)
    ) * (1.0 / SPEC)
    vis_imag = (
        jnp.einsum("icf,jcf->cij", own_imag, real_part, preferred_element_type=jnp.float32)
        - jnp.einsum("icf,jcf->cij", own_real, imag_part, preferred_element_type=jnp.float32)
    ) * (1.0 / SPEC)
    visibilities = jnp.stack([vis_real, vis_imag], axis=1)
    beam_block = beam_weights.shape[2]
    own_groups = lax.dynamic_slice_in_dim(beam_group, block_index * beam_block, beam_block, 0)
    members = station_group[:, 0][None, :] == own_groups[:, None]
    scaling = 1.0 / jnp.sqrt(jnp.sum(members.astype(jnp.float32), axis=1))
    weights = jnp.where(members[None, None], beam_weights, jnp.zeros((), jnp.bfloat16))
    weight_real = weights[:, 0]
    imaginary_weight = weights[:, 1]
    beam_real = jnp.einsum(
        "cbs,scf->bcf", weight_real, real_part, preferred_element_type=jnp.float32
    ) - jnp.einsum("cbs,scf->bcf", imaginary_weight, imag_part, preferred_element_type=jnp.float32)
    beam_imag = jnp.einsum(
        "cbs,scf->bcf", weight_real, imag_part, preferred_element_type=jnp.float32
    ) + jnp.einsum("cbs,scf->bcf", imaginary_weight, real_part, preferred_element_type=jnp.float32)
    beams = (jnp.stack([beam_real, beam_imag], axis=1) * scaling[:, None, None, None]).astype(
        jnp.bfloat16
    )
    returned = lax.all_to_all(beams, "row", split_axis=0, concat_axis=2, tiled=True)
    inverse = jnp.einsum(
        "bqkf,qkpc->bpcf",
        returned.astype(jnp.float32),
        fourier_table(returned.shape[2], 1.0),
        precision=high,
    )
    beam_series = polyphase(inverse, synthesis_taps)
    return (visibilities, beam_series)


def solution(mesh):
    sizes = dict(mesh.shape)

    def body(samples, *others):
        chan = samples.shape[2]
        fits = (sizes["row"], sizes["col"], sizes["sub"], chan) == (4, 2, 2, 16)
        return (fast_body if fits else general_body)(samples, *others)

    return jax.shard_map(
        body,
        mesh=mesh,
        in_specs=(
            P(("grp", "row", "col", "sub"), None, None, None),
            P(),
            P(),
            P("grp"),
            P("grp", None),
            P("grp"),
            P(("grp", "row"), None, ("col", "sub"), None),
        ),
        out_specs=(
            P("row", None, ("grp", "col", "sub"), None),
            P(("grp", "col", "sub", "row"), None, None, None),
        ),
        check_vma=False,
    )
```

```python
import functools
import math

import jax
import jax.numpy as jnp
from jax import lax
from jax.experimental import pallas as pl
from jax.experimental.pallas import tpu as pltpu
from jax.sharding import PartitionSpec as P

ANTENNAS_PER_STN = 8
SPEC = 512
VMEM_LIMIT = 24 * 1024 * 1024
HALO = 128
FLIPS = ((0, 0), (0, 1), (1, 0), (1, 1))
NEAR, FAR = (0, 1), (2, 3)
PLACES = (
    (FLIPS[0], NEAR + FAR),
    (FLIPS[1], NEAR + FAR),
    (FLIPS[2], NEAR),
    (FLIPS[2], FAR),
    (FLIPS[3], NEAR),
    (FLIPS[3], FAR),
)


def fourier(parts, sign):
    count = len(parts)
    if count == 1:
        return parts
    even, odd = fourier(parts[0::2], sign), fourier(parts[1::2], sign)
    low, top = [], []
    for k in range(count // 2):
        er, ei = even[k]
        re, im = odd[k]
        if k == 0:
            tr, ti = re, im
        elif 4 * k == count:
            tr, ti = (-sign * im, sign * re)
        else:
            c, s = math.cos(2 * math.pi * k / count), sign * math.sin(2 * math.pi * k / count)
            tr, ti = re * c - im * s, re * s + im * c
        low.append((er + tr, ei + ti))
        top.append((er - tr, ei - ti))
    return low + top


def lane_of(row, col, sub):
    return sub * 8 + col * 4 + row


def spread_kernel(axes, x_ref, *out_refs):
    row, col, sub = (lax.axis_index(a) for a in axes)
    antennas, parts, chan, frames = x_ref.shape
    count = antennas * parts * chan
    shape = (count, count)
    place = lax.broadcasted_iota(jnp.int32, (count, 1), 0)
    antenna = place % antennas
    part = place // antennas % parts
    piece = place // (antennas * parts)
    lane = lane_of(row ^ (piece % 4) ^ 2, col ^ (piece // 4 % 2), sub ^ (piece // 8))
    source = (antenna * parts + part) * chan + lane
    order = jnp.where(lax.broadcasted_iota(jnp.int32, shape, 1) == source, 1.0, 0.0)
    moved = jnp.dot(
        order.astype(jnp.bfloat16),
        x_ref[...].reshape(count, frames),
        preferred_element_type=jnp.float32,
    ).astype(jnp.bfloat16)
    start = 0
    for ref in out_refs:
        size = ref.shape[0] * ref.shape[1]
        ref[...] = moved[start : start + size].reshape(ref.shape)
        start += size


def member_matrix(axes, names_ref, stations, local):
    row, col, sub = (lax.axis_index(a) for a in axes)
    antennas = names_ref.shape[1]
    every = jnp.broadcast_to(names_ref[...], (8, antennas))
    names = []
    for k in range(4):
        owner = (row * 2 + (col ^ (k // 2))) * 2 + (sub ^ (k % 2))
        names += [pltpu.roll(every, lax.rem(antennas - owner * local, antennas), 1)[:1, :local]] * 2
    names = jnp.concatenate(names, axis=1)
    shape = (2 * stations, 8 * local)
    place = lax.broadcasted_iota(jnp.int32, shape, 0)
    column = lax.broadcasted_iota(jnp.int32, shape, 1)
    same = (place % stations == names) & (place // stations == column // local % 2)
    return jnp.where(same, 1.0, 0.0).astype(jnp.bfloat16)


def table_kernel(axes, names_ref, taps_ref, members_ref, own_taps_ref):
    stations, local = members_ref.shape[0] // 2, members_ref.shape[1] // 8
    members_ref[...] = member_matrix(axes, names_ref, stations, local)
    taps = taps_ref[...]
    lane = lane_of(*(lax.axis_index(a) for a in axes))
    mine = lax.broadcasted_iota(jnp.int32, taps.shape, 1) == lane
    own = jnp.sum(jnp.where(mine, taps, 0.0), axis=1, keepdims=True)
    own_taps_ref[...] = jnp.broadcast_to(own, own_taps_ref.shape)


def sum_kernel(first, members_ref, *refs):
    x_refs, out_refs = refs[:4], refs[4:]
    for k, ref in enumerate(out_refs):
        rows = jnp.concatenate([x[first + k if x.shape[0] == 4 else k] for x in x_refs], axis=0)
        ref[...] = jnp.dot(
            members_ref[...], rows, preferred_element_type=jnp.float32
        ).astype(ref.dtype)


def filter_kernel(taps_ref, *refs):
    x_refs, share_refs, out_refs = refs[:4], refs[4:7], refs[7:]
    rows = out_refs[0].shape[0]
    total = x_refs[0][...]
    for ref in x_refs[1:]:
        total = total + ref[...].astype(jnp.float32)
    place = lax.broadcasted_iota(jnp.int32, total.shape, 1)
    result = total * taps_ref[0:1]
    for tap in range(1, taps_ref.shape[0]):
        moved = jnp.where(place >= tap, pltpu.roll(total, tap, 1), 0.0)
        result = result + moved * taps_ref[tap : tap + 1]
    result = result.astype(out_refs[0].dtype)
    out_refs[0][...] = result
    for ref, share in zip(out_refs[1:], share_refs):
        ref[:rows] = result
        ref[rows:] = share[...]


def pack_kernel(axes, w_ref, groups_ref, beam_ref, chosen_ref, scale_ref, *out_refs):
    row, col, sub = (lax.axis_index(a) for a in axes)
    chan, _, stations, width = w_ref.shape
    beams = width // 4
    for k in range(chan):
        for q in range(2):
            place = (2 * k + q) * beams
            parts = [w_ref[k, q, :, j * beams : (j + 1) * beams] for j in range(4)]
            for mask, ref in enumerate(out_refs):
                taken = parts[0]
                for j in range(1, 4):
                    taken = jnp.where((row ^ mask) == j, parts[j], taken)
                ref[:, place : place + beams] = taken
    square = (stations, stations)
    diagonal = lax.broadcasted_iota(jnp.int32, square, 0) == lax.broadcasted_iota(
        jnp.int32, square, 1
    )
    groups = jnp.broadcast_to(groups_ref[...], square).astype(jnp.float32)
    groups = jnp.sum(jnp.where(diagonal, groups, 0.0), axis=1, keepdims=True)
    total = beam_ref.shape[1]
    first = ((col * 2 + sub) * 4 + row) * beams
    every = jnp.broadcast_to(beam_ref[...], (8, total))
    wanted = pltpu.roll(every, lax.rem(total - first, total), 1)[:1, :beams]
    chosen = (groups == wanted.astype(jnp.float32)).astype(jnp.float32)
    chosen_ref[...] = chosen
    scale = (1.0 / (4 * chan * math.sqrt(ANTENNAS_PER_STN))) / jnp.sqrt(
        jnp.sum(chosen, axis=0, keepdims=True)
    )
    scale_ref[...] = jnp.broadcast_to(scale, scale_ref.shape)


def bands(taps_ref, lane, rows, cols):
    wide = 2 * cols
    places = lax.broadcasted_iota(jnp.int32, (8, wide), 1)
    base = jnp.zeros((8, wide), jnp.float32)
    for tap in range(taps_ref.shape[0]):
        base = jnp.where(places == (tap - HALO) % wide, taps_ref[tap, lane], base)
    whole = jnp.broadcast_to(base[0:1], (rows, wide))
    whole = pltpu.roll(whole, 0, 1, stride=1, stride_axis=0)[:, :cols]
    high = whole.astype(jnp.bfloat16)
    low = (whole - high.astype(jnp.float32)).astype(jnp.bfloat16)
    return jnp.concatenate([high[:HALO], low[:HALO], high[HALO:], low[HALO:]], axis=0)


def band_kernel(taps_ref, t_ref):
    for c in range(t_ref.shape[0]):
        t_ref[c] = bands(taps_ref, c, t_ref.shape[1] // 2, t_ref.shape[2])


def weight_kernel(axes, chosen_ref, scale_ref, *refs):
    row = lax.axis_index(axes[0])
    w_refs, (m_ref, all_ref) = refs[:4], refs[4:]
    stations, beams = chosen_ref.shape
    held = all_ref.shape[2] // (2 * beams)
    chan = 4 * held
    for mask, ref in enumerate(w_refs):
        all_ref[row ^ mask] = ref[ref.shape[0] - stations :]
    members = chosen_ref[...] > 0
    scale = scale_ref[...]
    zero = jnp.zeros((), jnp.float32)
    parts = []
    for k in range(chan):
        whole = all_ref[k // held].astype(jnp.float32)
        places = [(2 * (k % held) + q) * beams for q in range(2)]
        parts.append(tuple(jnp.where(members, whole[:, p : p + beams], zero) for p in places))
    parts = fourier(parts, -1.0)
    real = [p[0] * scale for p in parts]
    imag = [p[1] * scale for p in parts]
    upper = jnp.concatenate([v for k in range(chan) for v in (real[k], -imag[k])], axis=0)
    lower = jnp.concatenate([v for k in range(chan) for v in (imag[k], real[k])], axis=0)
    whole = jnp.concatenate([upper, lower], axis=1).T.astype(m_ref.dtype)
    count = 2 * beams
    place = lax.broadcasted_iota(jnp.int32, (count, 1), 0)
    source = place % 2 * beams + place // 2
    order = jnp.where(lax.broadcasted_iota(jnp.int32, (count, count), 1) == source, 1.0, 0.0)
    whole = jnp.dot(order.astype(m_ref.dtype), whole, preferred_element_type=jnp.float32)
    whole = whole.astype(m_ref.dtype)
    width = whole.shape[1]
    step = 2 * stations
    odd = jnp.concatenate([whole[:, width - step :], whole[:, : width - step]], axis=1)
    for c in range(chan):
        base = odd if c % 2 else whole
        start = c // 2 * 2 * step
        m_ref[c, :, start:] = base[:, : width - start]
        if start:
            m_ref[c, :, :start] = base[:, width - start :]


def gather_lanes(axes, x_refs, places, lanes_ref):
    row, col, sub = (lax.axis_index(a) for a in axes)
    rows = x_refs[0].shape[1]
    for ((dc, ds), masks), ref in zip(places, x_refs):
        for k, m in enumerate(masks):
            lane = lane_of(row ^ m, col ^ dc, sub ^ ds)
            lanes_ref[pl.ds(pl.multiple_of(lane * rows, rows), rows)] = ref[k]


def lane_products(axes, flips, m_ref, lanes_ref, first, count):
    col, sub = (lax.axis_index(a) for a in axes[1:])
    width = 4 * lanes_ref.shape[0] // 16
    total = None
    for dc, ds in flips:
        start = pl.multiple_of((2 * (sub ^ ds) + (col ^ dc)) * width, width)
        some = m_ref[first : first + count, :, pl.ds(start, width)]
        some = some.reshape(count * m_ref.shape[1], width)
        found = jnp.dot(some, lanes_ref[pl.ds(start, width)], preferred_element_type=jnp.float32)
        total = found if total is None else total + found
    return total


def part_kernel(axes, places, m_ref, *refs):
    x_refs, (sum_ref, lanes_ref) = refs[: len(places)], refs[-2:]
    before = refs[len(places) : -2]
    gather_lanes(axes, x_refs, places, lanes_ref)
    flips = sorted({flip for flip, _ in places})
    for first in range(0, m_ref.shape[0], 4):
        found = lane_products(axes, flips, m_ref, lanes_ref, first, 4)
        found = found.reshape((4,) + sum_ref.shape[1:])
        for ref in before:
            found = found + ref[first : first + 4]
        sum_ref[first : first + 4] = found


def beam_kernel(
    axes,
    x_refs,
    m_ref,
    t_ref,
    sum_ref,
    series_ref,
    vis_ref,
    lanes_ref,
    cross_ref,
    inverse_ref,
    out_ref,
    store_sem,
):
    row, col, sub = (lax.axis_index(a) for a in axes)
    rows = x_refs[0].shape[1]
    stations = rows // 2
    chan = 4 * 4
    frames = lanes_ref.shape[1]

    gather_lanes(axes, x_refs[4:], PLACES[4:], lanes_ref)
    beams = m_ref.shape[1] // 2
    tile = t_ref.shape[2]
    for first in range(0, 16, 4):
        found = lane_products(axes, FLIPS[3:], m_ref, lanes_ref, first, 4)
        found = found.reshape((4,) + sum_ref.shape[1:]) + sum_ref[first : first + 4]
        inverse_ref[first : first + 4] = found.astype(jnp.bfloat16)
    for lane in range(chan):
        for n in range(frames // tile):
            taken = [inverse_ref[lane, :, n * tile : (n + 1) * tile]] * 2
            first = 2 * HALO
            if n > 0:
                taken = [inverse_ref[lane, :, n * tile - HALO : n * tile]] * 2 + taken
                first = 0
            value = jnp.dot(
                jnp.concatenate(taken, axis=1), t_ref[lane, first:], preferred_element_type=jnp.float32
            )
            for part in range(tile // 128):
                slot = n * (tile // 128) + part
                out_ref[lane, slot] = value[:, part * 128 : (part + 1) * 128]
                pltpu.make_async_copy(
                    out_ref.at[lane, slot],
                    series_ref.at[:, lane // 8, lane % 8, pl.ds(slot * 128, 128)],
                    store_sem,
                ).start()
    gather_lanes(axes, x_refs[:4], PLACES[:4], lanes_ref)
    inner = []
    for b in range(4):
        parts = []
        for a in range(4):
            start = (4 * a + b) * rows
            parts.append(
                tuple(
                    lanes_ref[start + q * stations : start + (q + 1) * stations].astype(
                        jnp.float32
                    )
                    for q in range(2)
                )
            )
        inner.append(fourier(parts, -1.0))
    scale = 1.0 / math.sqrt(chan * ANTENNAS_PER_STN)
    block = (col * 2 + sub) * vis_ref.shape[2]
    own = vis_ref.shape[2]
    for j in range(4):
        re, im = inner[0][j]
        for b in range(1, 4):
            cosine = jnp.float32(0.0)
            sine = jnp.float32(0.0)
            for r in range(4):
                angle = -2.0 * math.pi * b * (4 * r + j) / chan
                cosine = jnp.where(row == r, math.cos(angle), cosine)
                sine = jnp.where(row == r, math.sin(angle), sine)
            yr, yi = inner[b][j]
            re = re + (yr * cosine - yi * sine)
            im = im + (yr * sine + yi * cosine)
        both = (jnp.concatenate([re, im], axis=0) * scale).astype(jnp.bfloat16)
        cross_ref[...] = lax.dot_general(
            both, both, (((1,), (1,)), ((), ())), preferred_element_type=jnp.float32
        )
        own_real = cross_ref[pl.ds(pl.multiple_of(block, own), own)]
        own_imag = cross_ref[pl.ds(pl.multiple_of(stations + block, own), own)]
        vis_ref[j, 0] = (own_real[:, :stations] + own_imag[:, stations:]) * (1.0 / SPEC)
        vis_ref[j, 1] = (own_imag[:, :stations] - own_real[:, stations:]) * (1.0 / SPEC)
    pltpu.make_async_copy(out_ref, out_ref, store_sem).wait()


def call_beams(axes, pieces, matrix, bands, sums):
    params = pltpu.CompilerParams(vmem_limit_bytes=VMEM_LIMIT)
    vmem = pl.BlockSpec(memory_space=pltpu.VMEM)
    chan, frames = bands.shape[0], pieces[0].shape[2]
    stations, beams = pieces[0].shape[1] // 2, matrix.shape[1] // 2
    anywhere = pl.BlockSpec(memory_space=pl.ANY)
    series, visibilities = pl.pallas_call(
        lambda *refs: beam_kernel(axes, refs[: len(pieces)], *refs[len(pieces) :]),
        out_shape=(
            jax.ShapeDtypeStruct((2 * beams, 2, 8, frames), jnp.float32),
            jax.ShapeDtypeStruct((4, 2, stations // 4, stations), jnp.float32),
        ),
        in_specs=[vmem] * (len(pieces) + 3),
        out_specs=(anywhere, vmem),
        scratch_shapes=[
            pltpu.VMEM((chan * 2 * stations, frames), jnp.bfloat16),
            pltpu.VMEM((2 * stations, 2 * stations), jnp.float32),
            pltpu.VMEM((chan, 2 * beams, frames), jnp.bfloat16),
            pltpu.VMEM((chan, frames // 128, 2 * beams, 128), jnp.float32),
            pltpu.SemaphoreType.DMA,
        ],
        compiler_params=params,
        name="beams_and_series",
    )(*pieces, matrix, bands, sums)
    return visibilities, series


def swap(x, axis, mask):
    size = lax.axis_size(axis)
    return lax.ppermute(x, axis, [(i, i ^ mask) for i in range(size)])


def fast_body(
    samples, analysis_taps, synthesis_taps, antenna_station, station_group, beam_group, beam_weights
):
    axes = ("row", "col", "sub")
    params = pltpu.CompilerParams(vmem_limit_bytes=VMEM_LIMIT)
    vmem = pl.BlockSpec(memory_space=pltpu.VMEM)
    smem = pl.BlockSpec(memory_space=pltpu.SMEM)
    hbm = pl.BlockSpec(memory_space=pltpu.HBM)
    local, _, chan, frames = samples.shape
    stations = station_group.shape[0]
    antennas = antenna_station.shape[0]

    held_chan = beam_weights.shape[0]
    beams = beam_weights.shape[2] // 4
    block = jax.ShapeDtypeStruct((4, 2 * local, frames), jnp.bfloat16)
    half = jax.ShapeDtypeStruct((2, 2 * local, frames), jnp.bfloat16)
    kept, crossing_a, crossing_b, paired, far_a, far_b = pl.pallas_call(
        functools.partial(spread_kernel, axes),
        out_shape=[block, half, half, block, half, half],
        in_specs=[vmem],
        out_specs=[vmem] * 6,
        compiler_params=params,
        name="lane_spread",
    )(samples)
    members, taps = pl.pallas_call(
        functools.partial(table_kernel, axes),
        out_shape=[
            jax.ShapeDtypeStruct((2 * stations, 8 * local), jnp.bfloat16),
            jax.ShapeDtypeStruct((analysis_taps.shape[0], frames), jnp.float32),
        ],
        in_specs=[vmem] * 2,
        out_specs=[vmem] * 2,
        compiler_params=params,
        cost_estimate=pl.CostEstimate(flops=0, bytes_accessed=16 << 20, transcendentals=0),
        name="station_tables",
    )(antenna_station.reshape(1, antennas), analysis_taps)
    far_a = swap(far_a, "sub", 1)
    crossing_a = swap(crossing_a, "col", 1)
    far_a = swap(far_a, "col", 1)
    far_b = swap(far_b, "sub", 1)
    paired = swap(paired, "sub", 1)
    crossing_b = swap(crossing_b, "col", 1)
    far_b = swap(far_b, "col", 1)

    lane = jax.ShapeDtypeStruct((2 * stations, frames), jnp.bfloat16)
    sums2, sums3 = pl.pallas_call(
        functools.partial(sum_kernel, 0),
        out_shape=[lane] * 2,
        in_specs=[vmem] * 5,
        out_specs=[vmem] * 2,
        compiler_params=params,
        name="plane_sums_far",
    )(members, kept, paired, crossing_a, far_a)
    sums3, sums2 = swap(sums3, "row", 3), swap(sums2, "row", 2)
    sums0, sums1 = pl.pallas_call(
        functools.partial(sum_kernel, 2),
        out_shape=[jax.ShapeDtypeStruct(lane.shape, jnp.float32), lane],
        in_specs=[vmem] * 5,
        out_specs=[vmem] * 2,
        compiler_params=params,
        name="plane_sums_near",
    )(members, kept, paired, crossing_b, far_b)

    share = jax.ShapeDtypeStruct((stations, 2 * held_chan * beams), jnp.bfloat16)
    table = jax.ShapeDtypeStruct((stations, beams), jnp.float32)
    chosen, scale, *shares = pl.pallas_call(
        functools.partial(pack_kernel, axes),
        out_shape=[table] * 2 + [share] * 4,
        in_specs=[vmem] * 3,
        out_specs=[vmem] * 6,
        compiler_params=params,
        cost_estimate=pl.CostEstimate(flops=0, bytes_accessed=8 << 20, transcendentals=0),
        name="weight_shares",
    )(
        beam_weights.transpose(0, 1, 3, 2),
        station_group.reshape(1, stations),
        beam_group.reshape(1, beam_group.shape[0]),
    )

    lane_share = jax.ShapeDtypeStruct((3 * stations, frames), jnp.bfloat16)
    filtered, *sent = pl.pallas_call(
        filter_kernel,
        out_shape=[lane] + [lane_share] * 3,
        in_specs=[vmem] * 8,
        out_specs=[vmem] * 4,
        compiler_params=params,
        name="station_filter",
    )(taps, sums0, swap(sums1, "row", 1), sums2, sums3, *shares[1:])
    moved = [swap(x, "row", m) for x, m in zip(sent, (1, 2, 3))]

    tile = 256
    late_taps = synthesis_taps
    other = [swap(filtered, "col", 1), swap(moved[0][: 2 * stations], "col", 1)]
    bands = pl.pallas_call(
        band_kernel,
        out_shape=jax.ShapeDtypeStruct((chan, 2 * (tile + HALO), tile), jnp.bfloat16),
        in_specs=[smem],
        out_specs=vmem,
        compiler_params=params,
        cost_estimate=pl.CostEstimate(flops=0, bytes_accessed=16 << 20, transcendentals=0),
        name="synthesis_bands",
    )(late_taps)
    moved[1], moved[2], other[1], bands = lax.optimization_barrier(
        (moved[1], moved[2], other[1], bands)
    )
    matrix = pl.pallas_call(
        functools.partial(weight_kernel, axes),
        out_shape=jax.ShapeDtypeStruct((chan, 2 * beams, 2 * chan * stations), jnp.bfloat16),
        in_specs=[vmem] * 6,
        out_specs=vmem,
        scratch_shapes=[pltpu.VMEM((4,) + share.shape, jnp.bfloat16)],
        compiler_params=params,
        cost_estimate=pl.CostEstimate(flops=0, bytes_accessed=8 << 20, transcendentals=0),
        name="weight_matrix",
    )(chosen, scale, shares[0], *moved)

    def add_part(places, xs, before, name):
        return pl.pallas_call(
            functools.partial(part_kernel, axes, places),
            out_shape=jax.ShapeDtypeStruct((chan, 2 * beams, frames), jnp.float32),
            in_specs=[vmem] * (1 + len(xs) + len(before)),
            out_specs=vmem,
            scratch_shapes=[pltpu.VMEM((chan * 2 * stations, frames), jnp.bfloat16)],
            compiler_params=params,
            cost_estimate=pl.CostEstimate(flops=0, bytes_accessed=8 << 20, transcendentals=0),
            name=name,
        )(matrix, *xs, *before)

    distant = [x[: 2 * stations] for x in moved[1:]]
    held = jnp.stack([filtered, moved[0][: 2 * stations], *distant])
    near = jnp.stack(other)
    far = swap(jnp.stack(distant), "col", 1)
    paired, last_near = swap(held, "sub", 1), swap(near, "sub", 1)
    sums = add_part(PLACES[:1], [held], [], "own_beams")
    far, sums = lax.optimization_barrier((far, sums))
    last_far = swap(far, "sub", 1)
    sums = add_part(PLACES[1:4], [paired, near, far], [sums], "near_beams")
    pieces = [held, paired, near, far, last_near, last_far]

    visibilities, series = call_beams(axes, pieces, matrix, bands, sums)
    return visibilities, series.reshape(beams, 2, chan, frames)


def polyphase(signal, coefficients):
    length = signal.shape[-1]
    output = coefficients[0][:, None] * signal
    for tap_index in range(1, coefficients.shape[0]):
        shifted = jnp.pad(
            signal[..., : length - tap_index], [(0, 0)] * (signal.ndim - 1) + [(tap_index, 0)]
        )
        output = output + coefficients[tap_index][:, None] * shifted
    return output


def fourier_table(length, direction):
    indices = jnp.arange(length)
    angles = (
        2.0 * math.pi / length * (indices[:, None] * indices[None, :] % length).astype(jnp.float32)
    )
    cosine_part = jnp.cos(angles)
    sine_part = jnp.sin(angles)
    table = jnp.stack(
        [
            jnp.stack([cosine_part, direction * sine_part]),
            jnp.stack([-direction * sine_part, cosine_part]),
        ]
    )
    return table.transpose(0, 2, 1, 3) * (1.0 / math.sqrt(length))


def general_body(
    samples, analysis_taps, synthesis_taps, antenna_station, station_group, beam_group, beam_weights
):
    high = lax.Precision.HIGHEST
    block_count = lax.axis_size(("col", "sub"))
    block_index = lax.axis_index(("col", "sub"))
    filtered = polyphase(samples.astype(jnp.float32), analysis_taps)
    spectra = jnp.einsum(
        "aqcf,qcpk->apkf", filtered, fourier_table(samples.shape[2], -1.0), precision=high
    ).astype(jnp.bfloat16)
    turned = lax.all_to_all(spectra, "row", split_axis=2, concat_axis=0, tiled=True)
    local_count = spectra.shape[0]
    held_rows = turned.shape[0]
    chan_rows = turned.shape[2]
    spec_len = turned.shape[3]
    station_count = station_group.shape[0]
    flat_width = 2 * chan_rows * spec_len
    tile_rows = station_count // block_count
    shard_rows = lax.all_gather(turned, ("col", "sub"), axis=0, tiled=True)
    row_total = shard_rows.shape[0]
    positions = jnp.arange(row_total, dtype=jnp.int32)
    source_block = positions // held_rows
    offset_rows = positions % held_rows
    source_row = offset_rows // local_count
    antenna = offset_rows % local_count
    global_index = (source_row * block_count + source_block) * local_count + antenna
    targets = antenna_station[global_index]
    wanted = jnp.arange(station_count, dtype=jnp.int32)
    one_hot = (targets[None, :] == wanted[:, None]).astype(jnp.bfloat16)
    summed_values = jnp.dot(
        one_hot, shard_rows.reshape(row_total, flat_width), preferred_element_type=jnp.float32
    )
    flat_stations = (summed_values * (1.0 / math.sqrt(ANTENNAS_PER_STN))).astype(jnp.bfloat16)
    station_list = flat_stations.reshape(station_count, 2, chan_rows, spec_len)
    real_part = station_list[:, 0]
    imag_part = station_list[:, 1]
    own_rows = lax.dynamic_slice_in_dim(station_list, block_index * tile_rows, tile_rows, 0)
    own_real = own_rows[:, 0]
    own_imag = own_rows[:, 1]
    vis_real = (
        jnp.einsum("icf,jcf->cij", own_real, real_part, preferred_element_type=jnp.float32)
        + jnp.einsum("icf,jcf->cij", own_imag, imag_part, preferred_element_type=jnp.float32)
    ) * (1.0 / SPEC)
    vis_imag = (
        jnp.einsum("icf,jcf->cij", own_imag, real_part, preferred_element_type=jnp.float32)
        - jnp.einsum("icf,jcf->cij", own_real, imag_part, preferred_element_type=jnp.float32)
    ) * (1.0 / SPEC)
    visibilities = jnp.stack([vis_real, vis_imag], axis=1)
    beam_block = beam_weights.shape[2]
    own_groups = lax.dynamic_slice_in_dim(beam_group, block_index * beam_block, beam_block, 0)
    members = station_group[:, 0][None, :] == own_groups[:, None]
    scaling = 1.0 / jnp.sqrt(jnp.sum(members.astype(jnp.float32), axis=1))
    weights = jnp.where(members[None, None], beam_weights, jnp.zeros((), jnp.bfloat16))
    weight_real = weights[:, 0]
    imaginary_weight = weights[:, 1]
    beam_real = jnp.einsum(
        "cbs,scf->bcf", weight_real, real_part, preferred_element_type=jnp.float32
    ) - jnp.einsum("cbs,scf->bcf", imaginary_weight, imag_part, preferred_element_type=jnp.float32)
    beam_imag = jnp.einsum(
        "cbs,scf->bcf", weight_real, imag_part, preferred_element_type=jnp.float32
    ) + jnp.einsum("cbs,scf->bcf", imaginary_weight, real_part, preferred_element_type=jnp.float32)
    beams = (jnp.stack([beam_real, beam_imag], axis=1) * scaling[:, None, None, None]).astype(
        jnp.bfloat16
    )
    returned = lax.all_to_all(beams, "row", split_axis=0, concat_axis=2, tiled=True)
    inverse = jnp.einsum(
        "bqkf,qkpc->bpcf",
        returned.astype(jnp.float32),
        fourier_table(returned.shape[2], 1.0),
        precision=high,
    )
    beam_series = polyphase(inverse, synthesis_taps)
    return (visibilities, beam_series)


def solution(mesh):
    sizes = dict(mesh.shape)

    def body(samples, *others):
        chan = samples.shape[2]
        fits = (sizes["row"], sizes["col"], sizes["sub"], chan) == (4, 2, 2, 16)
        return (fast_body if fits else general_body)(samples, *others)

    return jax.shard_map(
        body,
        mesh=mesh,
        in_specs=(
            P(("grp", "row", "col", "sub"), None, None, None),
            P(),
            P(),
            P("grp"),
            P("grp", None),
            P("grp"),
            P(("grp", "row"), None, ("col", "sub"), None),
        ),
        out_specs=(
            P("row", None, ("grp", "col", "sub"), None),
            P(("grp", "col", "sub", "row"), None, None, None),
        ),
        check_vma=False,
    )
```

```python
import functools
import math

import jax
import jax.numpy as jnp
from jax import lax
from jax.experimental import pallas as pl
from jax.experimental.pallas import tpu as pltpu
from jax.sharding import PartitionSpec as P

ANTENNAS_PER_STN = 8
SPEC = 512
VMEM_LIMIT = 24 * 1024 * 1024
HALO = 128
FLIPS = ((0, 0), (0, 1), (1, 0), (1, 1))
NEAR, FAR = (0, 1), (2, 3)
PLACES = (
    (FLIPS[0], NEAR + FAR),
    (FLIPS[1], NEAR + FAR),
    (FLIPS[2], NEAR),
    (FLIPS[2], FAR),
    (FLIPS[3], NEAR),
    (FLIPS[3], FAR),
)


def fourier(parts, sign):
    count = len(parts)
    if count == 1:
        return parts
    even, odd = fourier(parts[0::2], sign), fourier(parts[1::2], sign)
    low, top = [], []
    for k in range(count // 2):
        er, ei = even[k]
        re, im = odd[k]
        if k == 0:
            tr, ti = re, im
        elif 4 * k == count:
            tr, ti = (-sign * im, sign * re)
        else:
            c, s = math.cos(2 * math.pi * k / count), sign * math.sin(2 * math.pi * k / count)
            tr, ti = re * c - im * s, re * s + im * c
        low.append((er + tr, ei + ti))
        top.append((er - tr, ei - ti))
    return low + top


def lane_of(row, col, sub):
    return sub * 8 + col * 4 + row


def spread_kernel(axes, x_ref, *out_refs):
    row, col, sub = (lax.axis_index(a) for a in axes)
    antennas, parts, chan, frames = x_ref.shape
    count = antennas * parts * chan
    shape = (count, count)
    place = lax.broadcasted_iota(jnp.int32, (count, 1), 0)
    antenna = place % antennas
    part = place // antennas % parts
    piece = place // (antennas * parts)
    lane = lane_of(row ^ (piece % 4) ^ 2, col ^ (piece // 4 % 2), sub ^ (piece // 8))
    source = (antenna * parts + part) * chan + lane
    order = jnp.where(lax.broadcasted_iota(jnp.int32, shape, 1) == source, 1.0, 0.0)
    moved = jnp.dot(
        order.astype(jnp.bfloat16),
        x_ref[...].reshape(count, frames),
        preferred_element_type=jnp.float32,
    ).astype(jnp.bfloat16)
    start = 0
    for ref in out_refs:
        size = ref.shape[0] * ref.shape[1]
        ref[...] = moved[start : start + size].reshape(ref.shape)
        start += size


def member_matrix(axes, names_ref, stations, local):
    row, col, sub = (lax.axis_index(a) for a in axes)
    antennas = names_ref.shape[1]
    every = jnp.broadcast_to(names_ref[...], (8, antennas))
    names = []
    for k in range(4):
        owner = (row * 2 + (col ^ (k // 2))) * 2 + (sub ^ (k % 2))
        names += [pltpu.roll(every, lax.rem(antennas - owner * local, antennas), 1)[:1, :local]] * 2
    names = jnp.concatenate(names, axis=1)
    shape = (2 * stations, 8 * local)
    place = lax.broadcasted_iota(jnp.int32, shape, 0)
    column = lax.broadcasted_iota(jnp.int32, shape, 1)
    same = (place % stations == names) & (place // stations == column // local % 2)
    return jnp.where(same, 1.0, 0.0).astype(jnp.bfloat16)


def table_kernel(axes, names_ref, taps_ref, members_ref, own_taps_ref):
    stations, local = members_ref.shape[0] // 2, members_ref.shape[1] // 8
    members_ref[...] = member_matrix(axes, names_ref, stations, local)
    taps = taps_ref[...]
    lane = lane_of(*(lax.axis_index(a) for a in axes))
    mine = lax.broadcasted_iota(jnp.int32, taps.shape, 1) == lane
    own = jnp.sum(jnp.where(mine, taps, 0.0), axis=1, keepdims=True)
    own_taps_ref[...] = jnp.broadcast_to(own, own_taps_ref.shape)


def sum_kernel(first, members_ref, *refs):
    x_refs, out_refs = refs[:4], refs[4:]
    for k, ref in enumerate(out_refs):
        rows = jnp.concatenate([x[first + k if x.shape[0] == 4 else k] for x in x_refs], axis=0)
        ref[...] = jnp.dot(
            members_ref[...], rows, preferred_element_type=jnp.float32
        ).astype(ref.dtype)


def filter_kernel(taps_ref, *refs):
    x_refs, share_refs, out_refs = refs[:4], refs[4:7], refs[7:]
    rows = out_refs[0].shape[0]
    total = x_refs[0][...]
    for ref in x_refs[1:]:
        total = total + ref[...].astype(jnp.float32)
    place = lax.broadcasted_iota(jnp.int32, total.shape, 1)
    result = total * taps_ref[0:1]
    for tap in range(1, taps_ref.shape[0]):
        moved = jnp.where(place >= tap, pltpu.roll(total, tap, 1), 0.0)
        result = result + moved * taps_ref[tap : tap + 1]
    result = result.astype(out_refs[0].dtype)
    out_refs[0][...] = result
    for ref, share in zip(out_refs[1:], share_refs):
        ref[:rows] = result
        ref[rows:] = share[...]


def pack_kernel(axes, w_ref, groups_ref, beam_ref, chosen_ref, scale_ref, *out_refs):
    row, col, sub = (lax.axis_index(a) for a in axes)
    chan, _, stations, width = w_ref.shape
    beams = width // 4
    for k in range(chan):
        for q in range(2):
            place = (2 * k + q) * beams
            parts = [w_ref[k, q, :, j * beams : (j + 1) * beams] for j in range(4)]
            for mask, ref in enumerate(out_refs):
                taken = parts[0]
                for j in range(1, 4):
                    taken = jnp.where((row ^ mask) == j, parts[j], taken)
                ref[:, place : place + beams] = taken
    square = (stations, stations)
    diagonal = lax.broadcasted_iota(jnp.int32, square, 0) == lax.broadcasted_iota(
        jnp.int32, square, 1
    )
    groups = jnp.broadcast_to(groups_ref[...], square).astype(jnp.float32)
    groups = jnp.sum(jnp.where(diagonal, groups, 0.0), axis=1, keepdims=True)
    total = beam_ref.shape[1]
    first = ((col * 2 + sub) * 4 + row) * beams
    every = jnp.broadcast_to(beam_ref[...], (8, total))
    wanted = pltpu.roll(every, lax.rem(total - first, total), 1)[:1, :beams]
    chosen = (groups == wanted.astype(jnp.float32)).astype(jnp.float32)
    chosen_ref[...] = chosen
    scale = (1.0 / (4 * chan * math.sqrt(ANTENNAS_PER_STN))) / jnp.sqrt(
        jnp.sum(chosen, axis=0, keepdims=True)
    )
    scale_ref[...] = jnp.broadcast_to(scale, scale_ref.shape)


def bands(taps_ref, lane, rows, cols):
    wide = 2 * cols
    places = lax.broadcasted_iota(jnp.int32, (8, wide), 1)
    base = jnp.zeros((8, wide), jnp.float32)
    for tap in range(taps_ref.shape[0]):
        base = jnp.where(places == (tap - HALO) % wide, taps_ref[tap, lane], base)
    whole = jnp.broadcast_to(base[0:1], (rows, wide))
    whole = pltpu.roll(whole, 0, 1, stride=1, stride_axis=0)[:, :cols]
    high = whole.astype(jnp.bfloat16)
    low = (whole - high.astype(jnp.float32)).astype(jnp.bfloat16)
    return jnp.concatenate([high[:HALO], low[:HALO], high[HALO:], low[HALO:]], axis=0)


def band_kernel(taps_ref, t_ref):
    for c in range(t_ref.shape[0]):
        t_ref[c] = bands(taps_ref, c, t_ref.shape[1] // 2, t_ref.shape[2])


def weight_kernel(axes, chosen_ref, scale_ref, *refs):
    row = lax.axis_index(axes[0])
    w_refs, (m_ref, all_ref) = refs[:4], refs[4:]
    stations, beams = chosen_ref.shape
    held = all_ref.shape[2] // (2 * beams)
    chan = 4 * held
    for mask, ref in enumerate(w_refs):
        all_ref[row ^ mask] = ref[ref.shape[0] - stations :]
    members = chosen_ref[...] > 0
    scale = scale_ref[...]
    zero = jnp.zeros((), jnp.float32)
    parts = []
    for k in range(chan):
        whole = all_ref[k // held].astype(jnp.float32)
        places = [(2 * (k % held) + q) * beams for q in range(2)]
        parts.append(tuple(jnp.where(members, whole[:, p : p + beams], zero) for p in places))
    parts = fourier(parts, -1.0)
    real = [p[0] * scale for p in parts]
    imag = [p[1] * scale for p in parts]
    upper = jnp.concatenate([v for k in range(chan) for v in (real[k], -imag[k])], axis=0)
    lower = jnp.concatenate([v for k in range(chan) for v in (imag[k], real[k])], axis=0)
    whole = jnp.concatenate([upper, lower], axis=1).T.astype(m_ref.dtype)
    count = 2 * beams
    place = lax.broadcasted_iota(jnp.int32, (count, 1), 0)
    source = place % 2 * beams + place // 2
    order = jnp.where(lax.broadcasted_iota(jnp.int32, (count, count), 1) == source, 1.0, 0.0)
    whole = jnp.dot(order.astype(m_ref.dtype), whole, preferred_element_type=jnp.float32)
    whole = whole.astype(m_ref.dtype)
    width = whole.shape[1]
    step = 2 * stations
    odd = jnp.concatenate([whole[:, width - step :], whole[:, : width - step]], axis=1)
    for c in range(chan):
        base = odd if c % 2 else whole
        start = c // 2 * 2 * step
        m_ref[c, :, start:] = base[:, : width - start]
        if start:
            m_ref[c, :, :start] = base[:, width - start :]


def gather_lanes(axes, x_refs, places, lanes_ref):
    row, col, sub = (lax.axis_index(a) for a in axes)
    rows = x_refs[0].shape[1]
    for ((dc, ds), masks), ref in zip(places, x_refs):
        for k, m in enumerate(masks):
            lane = lane_of(row ^ m, col ^ dc, sub ^ ds)
            lanes_ref[pl.ds(pl.multiple_of(lane * rows, rows), rows)] = ref[k]


def lane_products(axes, flips, m_ref, lanes_ref, first, count):
    col, sub = (lax.axis_index(a) for a in axes[1:])
    width = 4 * lanes_ref.shape[0] // 16
    total = None
    for dc, ds in flips:
        start = pl.multiple_of((2 * (sub ^ ds) + (col ^ dc)) * width, width)
        some = m_ref[first : first + count, :, pl.ds(start, width)]
        some = some.reshape(count * m_ref.shape[1], width)
        found = jnp.dot(some, lanes_ref[pl.ds(start, width)], preferred_element_type=jnp.float32)
        total = found if total is None else total + found
    return total


def part_kernel(axes, places, m_ref, *refs):
    x_refs, (sum_ref, lanes_ref) = refs[: len(places)], refs[-2:]
    before = refs[len(places) : -2]
    gather_lanes(axes, x_refs, places, lanes_ref)
    flips = sorted({flip for flip, _ in places})
    for first in range(0, m_ref.shape[0], 4):
        found = lane_products(axes, flips, m_ref, lanes_ref, first, 4)
        found = found.reshape((4,) + sum_ref.shape[1:])
        for ref in before:
            found = found + ref[first : first + 4]
        sum_ref[first : first + 4] = found


def beam_kernel(
    axes,
    x_refs,
    m_ref,
    t_ref,
    sum_ref,
    series_ref,
    vis_ref,
    lanes_ref,
    cross_ref,
    inverse_ref,
    out_ref,
    store_sem,
):
    row, col, sub = (lax.axis_index(a) for a in axes)
    rows = x_refs[0].shape[1]
    stations = rows // 2
    chan = 4 * 4
    frames = lanes_ref.shape[1]

    gather_lanes(axes, x_refs[4:], PLACES[4:], lanes_ref)
    beams = m_ref.shape[1] // 2
    tile = t_ref.shape[2]
    for first in range(0, 16, 4):
        found = lane_products(axes, FLIPS[3:], m_ref, lanes_ref, first, 4)
        found = found.reshape((4,) + sum_ref.shape[1:]) + sum_ref[first : first + 4]
        inverse_ref[first : first + 4] = found.astype(jnp.bfloat16)
        for lane in range(first, first + 4):
            for n in range(frames // tile):
                taken = [inverse_ref[lane, :, n * tile : (n + 1) * tile]] * 2
                start = 2 * HALO
                if n > 0:
                    taken = [inverse_ref[lane, :, n * tile - HALO : n * tile]] * 2 + taken
                    start = 0
                value = jnp.dot(
                    jnp.concatenate(taken, axis=1), t_ref[lane, start:], preferred_element_type=jnp.float32
                )
                for part in range(tile // 128):
                    slot = n * (tile // 128) + part
                    out_ref[lane, slot] = value[:, part * 128 : (part + 1) * 128]
                    pltpu.make_async_copy(
                        out_ref.at[lane, slot],
                        series_ref.at[:, lane // 8, lane % 8, pl.ds(slot * 128, 128)],
                        store_sem,
                    ).start()
    gather_lanes(axes, x_refs[:4], PLACES[:4], lanes_ref)
    inner = []
    for b in range(4):
        parts = []
        for a in range(4):
            start = (4 * a + b) * rows
            parts.append(
                tuple(
                    lanes_ref[start + q * stations : start + (q + 1) * stations].astype(
                        jnp.float32
                    )
                    for q in range(2)
                )
            )
        inner.append(fourier(parts, -1.0))
    scale = 1.0 / math.sqrt(chan * ANTENNAS_PER_STN)
    block = (col * 2 + sub) * vis_ref.shape[2]
    own = vis_ref.shape[2]
    for j in range(4):
        re, im = inner[0][j]
        for b in range(1, 4):
            cosine = jnp.float32(0.0)
            sine = jnp.float32(0.0)
            for r in range(4):
                angle = -2.0 * math.pi * b * (4 * r + j) / chan
                cosine = jnp.where(row == r, math.cos(angle), cosine)
                sine = jnp.where(row == r, math.sin(angle), sine)
            yr, yi = inner[b][j]
            re = re + (yr * cosine - yi * sine)
            im = im + (yr * sine + yi * cosine)
        both = (jnp.concatenate([re, im], axis=0) * scale).astype(jnp.bfloat16)
        cross_ref[...] = lax.dot_general(
            both, both, (((1,), (1,)), ((), ())), preferred_element_type=jnp.float32
        )
        own_real = cross_ref[pl.ds(pl.multiple_of(block, own), own)]
        own_imag = cross_ref[pl.ds(pl.multiple_of(stations + block, own), own)]
        vis_ref[j, 0] = (own_real[:, :stations] + own_imag[:, stations:]) * (1.0 / SPEC)
        vis_ref[j, 1] = (own_imag[:, :stations] - own_real[:, stations:]) * (1.0 / SPEC)
    pltpu.make_async_copy(out_ref, out_ref, store_sem).wait()


def call_beams(axes, pieces, matrix, bands, sums):
    params = pltpu.CompilerParams(vmem_limit_bytes=VMEM_LIMIT)
    vmem = pl.BlockSpec(memory_space=pltpu.VMEM)
    chan, frames = bands.shape[0], pieces[0].shape[2]
    stations, beams = pieces[0].shape[1] // 2, matrix.shape[1] // 2
    anywhere = pl.BlockSpec(memory_space=pl.ANY)
    series, visibilities = pl.pallas_call(
        lambda *refs: beam_kernel(axes, refs[: len(pieces)], *refs[len(pieces) :]),
        out_shape=(
            jax.ShapeDtypeStruct((2 * beams, 2, 8, frames), jnp.float32),
            jax.ShapeDtypeStruct((4, 2, stations // 4, stations), jnp.float32),
        ),
        in_specs=[vmem] * (len(pieces) + 3),
        out_specs=(anywhere, vmem),
        scratch_shapes=[
            pltpu.VMEM((chan * 2 * stations, frames), jnp.bfloat16),
            pltpu.VMEM((2 * stations, 2 * stations), jnp.float32),
            pltpu.VMEM((chan, 2 * beams, frames), jnp.bfloat16),
            pltpu.VMEM((chan, frames // 128, 2 * beams, 128), jnp.float32),
            pltpu.SemaphoreType.DMA,
        ],
        compiler_params=params,
        name="beams_and_series",
    )(*pieces, matrix, bands, sums)
    return visibilities, series


def swap(x, axis, mask):
    size = lax.axis_size(axis)
    return lax.ppermute(x, axis, [(i, i ^ mask) for i in range(size)])


def fast_body(
    samples, analysis_taps, synthesis_taps, antenna_station, station_group, beam_group, beam_weights
):
    axes = ("row", "col", "sub")
    params = pltpu.CompilerParams(vmem_limit_bytes=VMEM_LIMIT)
    vmem = pl.BlockSpec(memory_space=pltpu.VMEM)
    smem = pl.BlockSpec(memory_space=pltpu.SMEM)
    hbm = pl.BlockSpec(memory_space=pltpu.HBM)
    local, _, chan, frames = samples.shape
    stations = station_group.shape[0]
    antennas = antenna_station.shape[0]

    held_chan = beam_weights.shape[0]
    beams = beam_weights.shape[2] // 4
    block = jax.ShapeDtypeStruct((4, 2 * local, frames), jnp.bfloat16)
    half = jax.ShapeDtypeStruct((2, 2 * local, frames), jnp.bfloat16)
    kept, crossing_a, crossing_b, paired, far_a, far_b = pl.pallas_call(
        functools.partial(spread_kernel, axes),
        out_shape=[block, half, half, block, half, half],
        in_specs=[vmem],
        out_specs=[vmem] * 6,
        compiler_params=params,
        name="lane_spread",
    )(samples)
    members, taps = pl.pallas_call(
        functools.partial(table_kernel, axes),
        out_shape=[
            jax.ShapeDtypeStruct((2 * stations, 8 * local), jnp.bfloat16),
            jax.ShapeDtypeStruct((analysis_taps.shape[0], frames), jnp.float32),
        ],
        in_specs=[vmem] * 2,
        out_specs=[vmem] * 2,
        compiler_params=params,
        cost_estimate=pl.CostEstimate(flops=0, bytes_accessed=16 << 20, transcendentals=0),
        name="station_tables",
    )(antenna_station.reshape(1, antennas), analysis_taps)
    far_a = swap(far_a, "sub", 1)
    crossing_a = swap(crossing_a, "col", 1)
    far_a = swap(far_a, "col", 1)
    far_b = swap(far_b, "sub", 1)
    paired = swap(paired, "sub", 1)
    crossing_b = swap(crossing_b, "col", 1)
    far_b = swap(far_b, "col", 1)

    lane = jax.ShapeDtypeStruct((2 * stations, frames), jnp.bfloat16)
    sums2, sums3 = pl.pallas_call(
        functools.partial(sum_kernel, 0),
        out_shape=[lane] * 2,
        in_specs=[vmem] * 5,
        out_specs=[vmem] * 2,
        compiler_params=params,
        name="plane_sums_far",
    )(members, kept, paired, crossing_a, far_a)
    sums3, sums2 = swap(sums3, "row", 3), swap(sums2, "row", 2)
    sums0, sums1 = pl.pallas_call(
        functools.partial(sum_kernel, 2),
        out_shape=[jax.ShapeDtypeStruct(lane.shape, jnp.float32), lane],
        in_specs=[vmem] * 5,
        out_specs=[vmem] * 2,
        compiler_params=params,
        name="plane_sums_near",
    )(members, kept, paired, crossing_b, far_b)

    share = jax.ShapeDtypeStruct((stations, 2 * held_chan * beams), jnp.bfloat16)
    table = jax.ShapeDtypeStruct((stations, beams), jnp.float32)
    chosen, scale, *shares = pl.pallas_call(
        functools.partial(pack_kernel, axes),
        out_shape=[table] * 2 + [share] * 4,
        in_specs=[vmem] * 3,
        out_specs=[vmem] * 6,
        compiler_params=params,
        cost_estimate=pl.CostEstimate(flops=0, bytes_accessed=8 << 20, transcendentals=0),
        name="weight_shares",
    )(
        beam_weights.transpose(0, 1, 3, 2),
        station_group.reshape(1, stations),
        beam_group.reshape(1, beam_group.shape[0]),
    )

    lane_share = jax.ShapeDtypeStruct((3 * stations, frames), jnp.bfloat16)
    filtered, *sent = pl.pallas_call(
        filter_kernel,
        out_shape=[lane] + [lane_share] * 3,
        in_specs=[vmem] * 8,
        out_specs=[vmem] * 4,
        compiler_params=params,
        name="station_filter",
    )(taps, sums0, swap(sums1, "row", 1), sums2, sums3, *shares[1:])
    moved = [swap(x, "row", m) for x, m in zip(sent, (1, 2, 3))]

    tile = 256
    late_taps = synthesis_taps
    other = [swap(filtered, "col", 1), swap(moved[0][: 2 * stations], "col", 1)]
    bands = pl.pallas_call(
        band_kernel,
        out_shape=jax.ShapeDtypeStruct((chan, 2 * (tile + HALO), tile), jnp.bfloat16),
        in_specs=[smem],
        out_specs=vmem,
        compiler_params=params,
        cost_estimate=pl.CostEstimate(flops=0, bytes_accessed=16 << 20, transcendentals=0),
        name="synthesis_bands",
    )(late_taps)
    moved[1], moved[2], other[1], bands = lax.optimization_barrier(
        (moved[1], moved[2], other[1], bands)
    )
    matrix = pl.pallas_call(
        functools.partial(weight_kernel, axes),
        out_shape=jax.ShapeDtypeStruct((chan, 2 * beams, 2 * chan * stations), jnp.bfloat16),
        in_specs=[vmem] * 6,
        out_specs=vmem,
        scratch_shapes=[pltpu.VMEM((4,) + share.shape, jnp.bfloat16)],
        compiler_params=params,
        cost_estimate=pl.CostEstimate(flops=0, bytes_accessed=8 << 20, transcendentals=0),
        name="weight_matrix",
    )(chosen, scale, shares[0], *moved)

    def add_part(places, xs, before, name):
        return pl.pallas_call(
            functools.partial(part_kernel, axes, places),
            out_shape=jax.ShapeDtypeStruct((chan, 2 * beams, frames), jnp.float32),
            in_specs=[vmem] * (1 + len(xs) + len(before)),
            out_specs=vmem,
            scratch_shapes=[pltpu.VMEM((chan * 2 * stations, frames), jnp.bfloat16)],
            compiler_params=params,
            cost_estimate=pl.CostEstimate(flops=0, bytes_accessed=8 << 20, transcendentals=0),
            name=name,
        )(matrix, *xs, *before)

    distant = [x[: 2 * stations] for x in moved[1:]]
    held = jnp.stack([filtered, moved[0][: 2 * stations], *distant])
    near = jnp.stack(other)
    far = swap(jnp.stack(distant), "col", 1)
    paired, last_near = swap(held, "sub", 1), swap(near, "sub", 1)
    sums = add_part(PLACES[:1], [held], [], "own_beams")
    far, sums = lax.optimization_barrier((far, sums))
    last_far = swap(far, "sub", 1)
    sums = add_part(PLACES[1:4], [paired, near, far], [sums], "near_beams")
    pieces = [held, paired, near, far, last_near, last_far]

    visibilities, series = call_beams(axes, pieces, matrix, bands, sums)
    return visibilities, series.reshape(beams, 2, chan, frames)


def polyphase(signal, coefficients):
    length = signal.shape[-1]
    output = coefficients[0][:, None] * signal
    for tap_index in range(1, coefficients.shape[0]):
        shifted = jnp.pad(
            signal[..., : length - tap_index], [(0, 0)] * (signal.ndim - 1) + [(tap_index, 0)]
        )
        output = output + coefficients[tap_index][:, None] * shifted
    return output


def fourier_table(length, direction):
    indices = jnp.arange(length)
    angles = (
        2.0 * math.pi / length * (indices[:, None] * indices[None, :] % length).astype(jnp.float32)
    )
    cosine_part = jnp.cos(angles)
    sine_part = jnp.sin(angles)
    table = jnp.stack(
        [
            jnp.stack([cosine_part, direction * sine_part]),
            jnp.stack([-direction * sine_part, cosine_part]),
        ]
    )
    return table.transpose(0, 2, 1, 3) * (1.0 / math.sqrt(length))


def general_body(
    samples, analysis_taps, synthesis_taps, antenna_station, station_group, beam_group, beam_weights
):
    high = lax.Precision.HIGHEST
    block_count = lax.axis_size(("col", "sub"))
    block_index = lax.axis_index(("col", "sub"))
    filtered = polyphase(samples.astype(jnp.float32), analysis_taps)
    spectra = jnp.einsum(
        "aqcf,qcpk->apkf", filtered, fourier_table(samples.shape[2], -1.0), precision=high
    ).astype(jnp.bfloat16)
    turned = lax.all_to_all(spectra, "row", split_axis=2, concat_axis=0, tiled=True)
    local_count = spectra.shape[0]
    held_rows = turned.shape[0]
    chan_rows = turned.shape[2]
    spec_len = turned.shape[3]
    station_count = station_group.shape[0]
    flat_width = 2 * chan_rows * spec_len
    tile_rows = station_count // block_count
    shard_rows = lax.all_gather(turned, ("col", "sub"), axis=0, tiled=True)
    row_total = shard_rows.shape[0]
    positions = jnp.arange(row_total, dtype=jnp.int32)
    source_block = positions // held_rows
    offset_rows = positions % held_rows
    source_row = offset_rows // local_count
    antenna = offset_rows % local_count
    global_index = (source_row * block_count + source_block) * local_count + antenna
    targets = antenna_station[global_index]
    wanted = jnp.arange(station_count, dtype=jnp.int32)
    one_hot = (targets[None, :] == wanted[:, None]).astype(jnp.bfloat16)
    summed_values = jnp.dot(
        one_hot, shard_rows.reshape(row_total, flat_width), preferred_element_type=jnp.float32
    )
    flat_stations = (summed_values * (1.0 / math.sqrt(ANTENNAS_PER_STN))).astype(jnp.bfloat16)
    station_list = flat_stations.reshape(station_count, 2, chan_rows, spec_len)
    real_part = station_list[:, 0]
    imag_part = station_list[:, 1]
    own_rows = lax.dynamic_slice_in_dim(station_list, block_index * tile_rows, tile_rows, 0)
    own_real = own_rows[:, 0]
    own_imag = own_rows[:, 1]
    vis_real = (
        jnp.einsum("icf,jcf->cij", own_real, real_part, preferred_element_type=jnp.float32)
        + jnp.einsum("icf,jcf->cij", own_imag, imag_part, preferred_element_type=jnp.float32)
    ) * (1.0 / SPEC)
    vis_imag = (
        jnp.einsum("icf,jcf->cij", own_imag, real_part, preferred_element_type=jnp.float32)
        - jnp.einsum("icf,jcf->cij", own_real, imag_part, preferred_element_type=jnp.float32)
    ) * (1.0 / SPEC)
    visibilities = jnp.stack([vis_real, vis_imag], axis=1)
    beam_block = beam_weights.shape[2]
    own_groups = lax.dynamic_slice_in_dim(beam_group, block_index * beam_block, beam_block, 0)
    members = station_group[:, 0][None, :] == own_groups[:, None]
    scaling = 1.0 / jnp.sqrt(jnp.sum(members.astype(jnp.float32), axis=1))
    weights = jnp.where(members[None, None], beam_weights, jnp.zeros((), jnp.bfloat16))
    weight_real = weights[:, 0]
    imaginary_weight = weights[:, 1]
    beam_real = jnp.einsum(
        "cbs,scf->bcf", weight_real, real_part, preferred_element_type=jnp.float32
    ) - jnp.einsum("cbs,scf->bcf", imaginary_weight, imag_part, preferred_element_type=jnp.float32)
    beam_imag = jnp.einsum(
        "cbs,scf->bcf", weight_real, imag_part, preferred_element_type=jnp.float32
    ) + jnp.einsum("cbs,scf->bcf", imaginary_weight, real_part, preferred_element_type=jnp.float32)
    beams = (jnp.stack([beam_real, beam_imag], axis=1) * scaling[:, None, None, None]).astype(
        jnp.bfloat16
    )
    returned = lax.all_to_all(beams, "row", split_axis=0, concat_axis=2, tiled=True)
    inverse = jnp.einsum(
        "bqkf,qkpc->bpcf",
        returned.astype(jnp.float32),
        fourier_table(returned.shape[2], 1.0),
        precision=high,
    )
    beam_series = polyphase(inverse, synthesis_taps)
    return (visibilities, beam_series)


def solution(mesh):
    sizes = dict(mesh.shape)

    def body(samples, *others):
        chan = samples.shape[2]
        fits = (sizes["row"], sizes["col"], sizes["sub"], chan) == (4, 2, 2, 16)
        return (fast_body if fits else general_body)(samples, *others)

    return jax.shard_map(
        body,
        mesh=mesh,
        in_specs=(
            P(("grp", "row", "col", "sub"), None, None, None),
            P(),
            P(),
            P("grp"),
            P("grp", None),
            P("grp"),
            P(("grp", "row"), None, ("col", "sub"), None),
        ),
        out_specs=(
            P("row", None, ("grp", "col", "sub"), None),
            P(("grp", "col", "sub", "row"), None, None, None),
        ),
        check_vma=False,
    )
```
